32 devices in a mesh: seq: 8 (over z, y), wshard: 4 (over x, core).
Axes of the slice: x: 2, y: 2, z: 4, core: 2. Of those that a mesh axis runs over, the one named last changes fastest.
Arguments:
- hidden_in: bfloat16 [4, 8192, 768], P('wshard', 'seq'), may hold values from -6 to 6
- cotangent: bfloat16 [4, 8192, 768], P('wshard', 'seq'), may hold values from -6 to 6
- block_seq: int32 [4, 8], P('wshard'), may hold values from 0 to 31, as said below
- block_place: int32 [4, 8], P('wshard'), may hold values from 0 to 3, as said below
- attn_in: bfloat16 [768, 2304], P('wshard'), may hold values from -0.21875 to 0.21875
- attn_out: bfloat16 [768, 768], P('wshard'), may hold values from -1.25 to 1.25
- ffn_in: bfloat16 [768, 2304], P('wshard'), may hold values from -0.21875 to 0.21875
- ffn_out: bfloat16 [1152, 768], P('wshard'), may hold values from -0.1875 to 0.1875
- norm_attn: bfloat16 [768], P('wshard'), may hold values from 0.5 to 1.5
- norm_ffn: bfloat16 [768], P('wshard'), may hold values from 0.5 to 1.5
- first_attn_in: float32 [768, 2304], P('wshard'), may hold values from -128 to 128
- first_attn_out: float32 [768, 768], P('wshard'), may hold values from -24 to 24
- first_ffn_in: float32 [768, 2304], P('wshard'), may hold values from -64 to 64
- first_ffn_out: float32 [1152, 768], P('wshard'), may hold values from -80 to 80
- first_norm_attn: float32 [768], P('wshard'), may hold values from -160 to 160
- first_norm_ffn: float32 [768], P('wshard'), may hold values from -112 to 112
- second_attn_in: float32 [768, 2304], P('wshard'), may hold values from 163.84 to 1310.72
- second_attn_out: float32 [768, 768], P('wshard'), may hold values from 13.1072 to 98.304
- second_ffn_in: float32 [768, 2304], P('wshard'), may hold values from 65.536 to 327.68
- second_ffn_out: float32 [1152, 768], P('wshard'), may hold values from 98.304 to 557.056
- second_norm_attn: float32 [768], P('wshard'), may hold values from 327.68 to 1966.08
- second_norm_ffn: float32 [768], P('wshard'), may hold values from 163.84 to 983.04
Outputs:
- block_out: bfloat16 [4, 8192, 768], P('wshard', 'seq')
- grad_in: bfloat16 [4, 8192, 768], P('wshard', 'seq')
- grad_attn_in: float32 [768, 2304], P('wshard')
- grad_attn_out: float32 [768, 768], P('wshard')
- grad_ffn_in: float32 [768, 2304], P('wshard')
- grad_ffn_out: float32 [1152, 768], P('wshard')
- grad_norm_attn: float32 [768], P('wshard')
- grad_norm_ffn: float32 [768], P('wshard')
- new_first_attn_in: float32 [768, 2304], P('wshard')
- new_first_attn_out: float32 [768, 768], P('wshard')
- new_first_ffn_in: float32 [768, 2304], P('wshard')
- new_first_ffn_out: float32 [1152, 768], P('wshard')
- new_first_norm_attn: float32 [768], P('wshard')
- new_first_norm_ffn: float32 [768], P('wshard')
- new_second_attn_in: float32 [768, 2304], P('wshard')
- new_second_attn_out: float32 [768, 768], P('wshard')
- new_second_ffn_in: float32 [768, 2304], P('wshard')
- new_second_ffn_out: float32 [1152, 768], P('wshard')
- new_second_norm_attn: float32 [768], P('wshard')
- new_second_norm_ffn: float32 [768], P('wshard')
- step_attn_in: float32 [768, 2304], P('wshard')
- step_attn_out: float32 [768, 768], P('wshard')
- step_ffn_in: float32 [768, 2304], P('wshard')
- step_ffn_out: float32 [1152, 768], P('wshard')
- step_norm_attn: float32 [768], P('wshard')
- step_norm_ffn: float32 [768], P('wshard')
The draws below stay inside these ranges and needn't reach their ends.
Inputs may be any that keep to these rules, and one draw needn't show every extreme that they name: `block_seq`: blocks of one sequence are consecutive within a stream and share one id; ids of different sequences differ, also across streams; a sequence has 4, 2 or 1 blocks, fewer only where a stream begins or ends; in every stream block 4 is the third block of a sequence of 4 blocks. `block_place`: counts 0, 1, 2 upward along the blocks of each sequence.
All inputs are finite; a program needn't handle non-finite values.
Results may differ from the reference program's by a relative error of at most 0.025.
Values may be sent and summed in bfloat16 or wider, within the bound.
No kernel may reach another device: no remote copies, remote signals or barrier semaphores. Data moves between devices by JAX's collectives and lax.ppermute only.
A program may use at most 256 MiB of HBM per device.

```python
import math
import jax
import jax.numpy as jnp
from jax import lax

D = 768
FF = 1152
HEADS = 12
HD = 64
HALF = 64
RUN_MOST = 4
STEP = 10
BLK = 1024
STREAMS = 4
NBLK = 8
STREAM_TOK = 8192
TOKENS = 32768
QBLK = 512


def block_table(key):
    shift_by = RUN_MOST // 2
    pieces = NBLK // RUN_MOST + 1
    run_kinds = jax.random.randint(jax.random.fold_in(key, 7), (STREAMS, pieces), 0, 3)
    full_piece = (NBLK // 2 + shift_by) // RUN_MOST
    run_kinds = jnp.where(jnp.arange(pieces)[None, :] == full_piece, 0, run_kinds).astype(jnp.int32)
    run_length = jnp.right_shift(jnp.full(run_kinds.shape, RUN_MOST, jnp.int32), run_kinds)
    blocks = jnp.arange(NBLK, dtype=jnp.int32)[None, :]
    shifted = blocks + shift_by
    piece_index = jnp.broadcast_to(shifted // RUN_MOST, (STREAMS, NBLK)).astype(jnp.int32)
    block_len = jnp.take_along_axis(run_length, piece_index, axis=1)
    shifted_start = shifted - shifted % RUN_MOST % block_len
    starts = jnp.maximum(shifted_start - shift_by, 0)
    places = blocks - starts
    seq_ids = jnp.arange(STREAMS, dtype=jnp.int32)[:, None] * NBLK + starts
    return (seq_ids.astype(jnp.int32), places.astype(jnp.int32))


def draw_block_seq(key, part):
    return block_table(key)[0]


def draw_block_place(key, part):
    return block_table(key)[1]


def shard_levels(rng, extent, cuts, smallest, largest):
    factor_of = 1.0
    for axis_at, parts in cuts:
        draws = jax.random.uniform(jax.random.fold_in(jax.random.fold_in(rng, 6), axis_at), (parts,), jnp.float32, smallest / len(cuts), largest / len(cuts))
        factor_of = factor_of * jnp.repeat(jnp.exp(draws), extent[axis_at] // parts).reshape((-1,) + (1,) * (len(extent) - 1 - axis_at))
    return factor_of


def scatter_about(own_key, extent, scale, bound, shards=(), kind=jnp.bfloat16):
    result = jax.random.normal(own_key, extent, jnp.float32) * scale
    if len(shards) > 0:
        result = shard_levels(own_key, extent, shards, -0.22, 0.18) * result
    return jnp.clip(result, min=-bound, max=bound).astype(kind)


def setup_inputs(seed: int = 0) -> dict:
    key_list = jax.random.split(jax.random.key(seed), 23)
    hidden_in = scatter_about(key_list[0], (STREAMS, STREAM_TOK, D), 1.0, 6.0, ((0, 4), (1, 8)))
    cotangent = scatter_about(key_list[1], (STREAMS, STREAM_TOK, D), 1.0, 6.0, ((0, 4), (1, 8)))
    block_seq = draw_block_seq(jax.random.fold_in(key_list[22], 71), 0)
    block_place = draw_block_place(jax.random.fold_in(key_list[22], 71), 0)
    attn_in = scatter_about(key_list[4], (D, 3 * D), D ** -0.5, 0.21875, ((0, 4),))
    attn_out = scatter_about(key_list[5], (D, D), (max(D // 32, 4)) ** -0.5, 1.25, ((0, 4),))
    ffn_in = scatter_about(key_list[6], (D, 2 * FF), D ** -0.5, 0.21875, ((0, 4),))
    ffn_out = scatter_about(key_list[7], (FF, D), FF ** -0.5, 0.1875, ((0, 4),))
    norm_attn = jnp.clip(1.0 + 0.1 * jax.random.normal(key_list[8], (D,), jnp.float32), 0.5, 1.5).astype(jnp.bfloat16)
    norm_ffn = jnp.clip(1.0 + 0.1 * jax.random.normal(key_list[9], (D,), jnp.float32), 0.5, 1.5).astype(jnp.bfloat16)
    first_attn_in = scatter_about(key_list[10], (D, 3 * D), (0.11 * TOKENS ** 0.5), 128.0, ((0, 4),), jnp.float32)
    first_attn_out = scatter_about(key_list[11], (D, D), (0.022 * TOKENS ** 0.5), 24.0, ((0, 4),), jnp.float32)
    first_ffn_in = scatter_about(key_list[12], (D, 2 * FF), (0.055 * TOKENS ** 0.5), 64.0, ((0, 4),), jnp.float32)
    first_ffn_out = scatter_about(key_list[13], (FF, D), (0.07 * TOKENS ** 0.5), 80.0, ((0, 4),), jnp.float32)
    first_norm_attn = scatter_about(key_list[14], (D,), (0.15 * TOKENS ** 0.5), 160.0, ((0, 4),), jnp.float32)
    first_norm_ffn = scatter_about(key_list[15], (D,), (0.1 * TOKENS ** 0.5), 112.0, ((0, 4),), jnp.float32)
    second_attn_in = jnp.clip(jnp.exp(math.log(1310.72) - 2.0794415 * jax.random.uniform(key_list[16], (D, 3 * D), jnp.float32) ** shard_levels(key_list[16], (D, 3 * D), ((0, 4),), -0.2, 0.2)), 163.84, 1310.72)
    second_attn_out = jnp.clip(jnp.exp(math.log(98.304) - 2.014903 * jax.random.uniform(key_list[17], (D, D), jnp.float32) ** shard_levels(key_list[17], (D, D), ((0, 4),), -0.2, 0.2)), 13.1072, 98.304)
    second_ffn_in = jnp.clip(jnp.exp(math.log(327.68) - 1.6094378 * jax.random.uniform(key_list[18], (D, 2 * FF), jnp.float32) ** shard_levels(key_list[18], (D, 2 * FF), ((0, 4),), -0.2, 0.2)), 65.536, 327.68)
    second_ffn_out = jnp.clip(jnp.exp(math.log(557.056) - 1.7346011 * jax.random.uniform(key_list[19], (FF, D), jnp.float32) ** shard_levels(key_list[19], (FF, D), ((0, 4),), -0.2, 0.2)), 98.304, 557.056)
    second_norm_attn = jnp.clip(jnp.exp(math.log(1966.08) - 1.7917595 * jax.random.uniform(key_list[20], (D,), jnp.float32) ** shard_levels(key_list[20], (D,), ((0, 4),), -0.2, 0.2)), 327.68, 1966.08)
    second_norm_ffn = jnp.clip(jnp.exp(math.log(983.04) - 1.7917595 * jax.random.uniform(key_list[21], (D,), jnp.float32) ** shard_levels(key_list[21], (D,), ((0, 4),), -0.2, 0.2)), 163.84, 983.04)
    return {"hidden_in": hidden_in, "cotangent": cotangent, "block_seq": block_seq, "block_place": block_place, "attn_in": attn_in, "attn_out": attn_out, "ffn_in": ffn_in, "ffn_out": ffn_out, "norm_attn": norm_attn, "norm_ffn": norm_ffn, "first_attn_in": first_attn_in, "first_attn_out": first_attn_out, "first_ffn_in": first_ffn_in, "first_ffn_out": first_ffn_out, "first_norm_attn": first_norm_attn, "first_norm_ffn": first_norm_ffn, "second_attn_in": second_attn_in, "second_attn_out": second_attn_out, "second_ffn_in": second_ffn_in, "second_ffn_out": second_ffn_out, "second_norm_attn": second_norm_attn, "second_norm_ffn": second_norm_ffn}


@jax.custom_vjp
def low(v):
    return lax.optimization_barrier(v.astype(jnp.bfloat16)).astype(jnp.float32)

@jax.custom_vjp
def low_back(v):
    return v

def low_keep(v):
    return (low(v), None)

def low_pass(kept, grad):
    return (grad,)

def back_keep(v):
    return (v, None)

def back_low(kept, grad):
    return (low(grad),)
low.defvjp(low_keep, low_pass)
low_back.defvjp(back_keep, back_low)
NORM_EPS = 1e-05
BETA_ONE = 0.9
BETA_TWO = 0.98
LEARN_RATE = 0.05
WEIGHT_DECAY = 0.01
ADAM_EPS = 1e-06
NEG_FILL = -1e+30
THETA = 10000.0
HIGHEST = lax.Precision.HIGHEST

def matmul(left, right):
    return jnp.dot(left, right, precision=HIGHEST, preferred_element_type=jnp.float32)

def layer_norm(inputs, scales):
    row_mean = lax.optimization_barrier(jnp.mean(inputs, axis=-1, keepdims=True))
    centered = inputs - row_mean
    variance = lax.optimization_barrier(jnp.mean(centered * centered, axis=-1, keepdims=True))
    return centered * lax.rsqrt(variance + NORM_EPS) * scales

def rotary(inputs, positions):
    half_dim = HD // 2
    frequency = THETA ** (-2.0 * jnp.arange(half_dim).astype(jnp.float32) / HD)
    angles = positions.astype(jnp.float32)[:, None] * frequency[None, :]
    cosine = jnp.cos(angles)[:, None, :]
    sine_part = jnp.sin(angles)[:, None, :]
    first_half = inputs[..., :half_dim]
    second_half = inputs[..., half_dim:]
    return jnp.concatenate([first_half * cosine - second_half * sine_part, second_half * cosine + first_half * sine_part], axis=-1)

def gated_unit(gate_up):
    return jax.nn.gelu(gate_up[:, :FF], approximate=False) * gate_up[:, FF:]

def attention(queries, key_rows, value_rows, seq_tok):
    stream_len = queries.shape[0]
    pad_width = ((HALF, HALF), (0, 0), (0, 0))
    key_pad = jnp.pad(key_rows, pad_width)
    value_pad = jnp.pad(value_rows, pad_width)
    seq_pad = jnp.pad(seq_tok, (HALF, HALF), constant_values=-1)
    offsets = jnp.arange(QBLK + 2 * HALF)[None, :] - jnp.arange(QBLK)[:, None]
    in_band = (offsets >= 0) & (offsets <= 2 * HALF)

    def block_fn(block_index):
        row_start = (block_index * QBLK).astype(jnp.int32)
        query_blk = lax.dynamic_slice_in_dim(queries, row_start, QBLK, 0)
        key_win = lax.dynamic_slice_in_dim(key_pad, row_start, QBLK + 2 * HALF, 0)
        value_win = lax.dynamic_slice_in_dim(value_pad, row_start, QBLK + 2 * HALF, 0)
        seq_query = lax.dynamic_slice_in_dim(seq_tok, row_start, QBLK, 0)
        seq_key = lax.dynamic_slice_in_dim(seq_pad, row_start, QBLK + 2 * HALF, 0)
        allowed = in_band & (seq_query[:, None] == seq_key[None, :])
        scores = low_back(jnp.einsum('qhd,khd->hqk', query_blk, key_win, precision=HIGHEST) * HD ** (-0.5))
        scores = jnp.where(allowed[None], scores, NEG_FILL)
        row_max = lax.optimization_barrier(jnp.max(scores, axis=-1, keepdims=True))
        exp_scores = jnp.exp(scores - row_max)
        soft_probs = low(exp_scores / lax.optimization_barrier(jnp.sum(exp_scores, axis=-1, keepdims=True)))
        return jnp.einsum('hqk,khd->qhd', soft_probs, value_win, precision=HIGHEST)
    blocks = lax.map(jax.checkpoint(block_fn), jnp.arange(stream_len // QBLK).astype(jnp.int32))
    return blocks.reshape(stream_len, HEADS * HD)

def forward(inputs, attn_w, out_w, ffn_w, down_w, norm_one, norm_two, seq_tok, pos_tok):
    stream_len = inputs.shape[0]
    normed = low(layer_norm(inputs, norm_one))
    qkv_rows = low_back(matmul(normed, attn_w))
    queries = low(rotary(qkv_rows[:, :D].reshape(stream_len, HEADS, HD), pos_tok))
    key_rows = low(rotary(qkv_rows[:, D:2 * D].reshape(stream_len, HEADS, HD), pos_tok))
    value_rows = low(qkv_rows[:, 2 * D:].reshape(stream_len, HEADS, HD))
    mixed_rows = low_back(low(attention(queries, key_rows, value_rows, seq_tok)))
    branch = low_back(matmul(mixed_rows, out_w))
    middle = inputs + branch
    normed_two = low(layer_norm(middle, norm_two))
    gate_up = low_back(matmul(normed_two, ffn_w))
    activated = low(gated_unit(gate_up))
    return middle + matmul(activated, down_w)

def adam_update(weight, grad, first_old, second, decay_rate):
    new_first = BETA_ONE * first_old + (1.0 - BETA_ONE) * grad
    new_second = BETA_TWO * second + (1.0 - BETA_TWO) * grad * grad
    first_hat = new_first / (1.0 - BETA_ONE ** STEP)
    second_hat = new_second / (1.0 - BETA_TWO ** STEP)
    change = -LEARN_RATE * (first_hat / (jnp.sqrt(second_hat) + ADAM_EPS) + decay_rate * weight)
    return (new_first, new_second, change)

def reference(hidden_in, cotangent, block_seq, block_place, attn_in, attn_out, ffn_in, ffn_out, norm_attn, norm_ffn, first_attn_in, first_attn_out, first_ffn_in, first_ffn_out, first_norm_attn, first_norm_ffn, second_attn_in, second_attn_out, second_ffn_in, second_ffn_out, second_norm_attn, second_norm_ffn):
    params = tuple((weight.astype(jnp.float32) for weight in (attn_in, attn_out, ffn_in, ffn_out, norm_attn, norm_ffn)))
    zero_grads = tuple((jnp.zeros(param.shape, jnp.float32) for param in params))

    def stream_step(totals_in, stream_data):
        inputs, cot_rows, seq_blocks, place_blocks = stream_data
        seq_tok = jnp.repeat(seq_blocks, BLK).astype(jnp.int32)
        pos_tok = jnp.repeat(place_blocks, BLK).astype(jnp.int32) * BLK + jnp.tile(jnp.arange(BLK), NBLK).astype(jnp.int32)

        def run_layer(inputs_f, attn_f, out_f, ffn_f, down_f, norm_one_f, norm_two_f):
            return forward(inputs_f, attn_f, out_f, ffn_f, down_f, norm_one_f, norm_two_f, seq_tok, pos_tok)
        outputs, pull_back = jax.vjp(run_layer, inputs.astype(jnp.float32), params[0], params[1], params[2], params[3], params[4], params[5])
        grad_list = pull_back(cot_rows.astype(jnp.float32))
        totals_out = tuple((total + grad for total, grad in zip(totals_in, grad_list[1:])))
        return (totals_out, (outputs.astype(jnp.bfloat16), grad_list[0].astype(jnp.bfloat16)))
    totals, (block_out, grad_in) = lax.scan(stream_step, zero_grads, (hidden_in, cotangent, block_seq, block_place))
    firsts = (first_attn_in, first_attn_out, first_ffn_in, first_ffn_out, first_norm_attn, first_norm_ffn)
    seconds = (second_attn_in, second_attn_out, second_ffn_in, second_ffn_out, second_norm_attn, second_norm_ffn)
    decays = (WEIGHT_DECAY, WEIGHT_DECAY, WEIGHT_DECAY, WEIGHT_DECAY, 0.0, 0.0)
    updates = [adam_update(param, grad, first_old, second, decay_rate) for param, grad, first_old, second, decay_rate in zip(params, totals, firsts, seconds, decays)]
    new_firsts = tuple((update_set[0] for update_set in updates))
    new_seconds = tuple((update_set[1] for update_set in updates))
    changes = tuple((update_set[2] for update_set in updates))
    return (block_out, grad_in, totals[0], totals[1], totals[2], totals[3], totals[4], totals[5], new_firsts[0], new_firsts[1], new_firsts[2], new_firsts[3], new_firsts[4], new_firsts[5], new_seconds[0], new_seconds[1], new_seconds[2], new_seconds[3], new_seconds[4], new_seconds[5], changes[0], changes[1], changes[2], changes[3], changes[4], changes[5])
```

```python
import jax
import jax.numpy as jnp
from jax import lax
from jax.experimental import pallas as pl
from jax.experimental.pallas import tpu as pltpu
from jax.sharding import PartitionSpec as P

D = 768
FF = 1152
HEADS = 12
HD = 64
HALF = 64
STEP = 10
PAIR = 2 * HD
QB = 128
TILE = 256
CHUNK = 384

NORM_EPS = 1e-05
BETA_ONE = 0.9
BETA_TWO = 0.98
LEARN_RATE = 0.05
WEIGHT_DECAY = 0.01
ADAM_EPS = 1e-06
NEG_FILL = -1e30
THETA = 10000.0
BF = jnp.bfloat16
F32 = jnp.float32
VMEM_BYTES = 56 * 1024 * 1024


def dot(left, right):
    return lax.dot_general(left, right, (((1,), (0,)), ((), ())), preferred_element_type=F32)


def dot_bt(left, right):
    return lax.dot_general(left, right, (((1,), (1,)), ((), ())), preferred_element_type=F32)


def dot_at(left, right):
    return lax.dot_general(left, right, (((0,), (0,)), ((), ())), preferred_element_type=F32)


def full(shape):
    return pl.BlockSpec(shape, lambda i: (0,) * len(shape))


def rows(tile, width):
    return pl.BlockSpec((tile, width), lambda i: (i, 0))


def params():
    return pltpu.CompilerParams(
        dimension_semantics=("arbitrary",), vmem_limit_bytes=VMEM_BYTES
    )


def cost(flops, nbytes, trans=0):
    return pl.CostEstimate(flops=int(flops), bytes_accessed=int(nbytes), transcendentals=int(trans))


def normalize(x):
    mean = jnp.mean(x, axis=-1, keepdims=True)
    centered = x - mean
    var = jnp.mean(centered * centered, axis=-1, keepdims=True)
    r = lax.rsqrt(var + NORM_EPS)
    return centered * r, r


def turn(u, cos, sin_left, sin_right):
    return u * cos + pltpu.roll(u, PAIR - HD // 2, 1) * sin_left + pltpu.roll(u, HD // 2, 1) * sin_right


def qkv_body(x_ref, gain_ref, w_ref, cos_ref, sl_ref, sr_ref, normed_ref, q_ref, k_ref, v_ref):
    n, _ = normalize(x_ref[...].astype(F32))
    normed = (n * gain_ref[...]).astype(BF)
    normed_ref[...] = normed
    cos, sl, sr = cos_ref[...], sl_ref[...], sr_ref[...]
    for part, ref, scale in ((0, q_ref, HD**-0.5), (1, k_ref, 1.0)):
        u = dot(normed, w_ref[:, part * D : (part + 1) * D])
        for p in range(D // PAIR):
            t = turn(u[:, p * PAIR : (p + 1) * PAIR], cos, sl, sr)
            ref[:, p * PAIR : (p + 1) * PAIR] = (t * scale).astype(BF)
    v_ref[...] = dot(normed, w_ref[:, 2 * D :]).astype(BF)


def qkv_call(x_ext, gain, w, cos, sl, sr):
    ext = x_ext.shape[0]
    t = ext // 3
    out = jax.ShapeDtypeStruct((ext, D), BF)
    return pl.pallas_call(
        qkv_body,
        grid=(3,),
        in_specs=[rows(t, D), full((1, D)), full((D, 3 * D)), rows(t, PAIR), rows(t, PAIR), rows(t, PAIR)],
        out_specs=[rows(t, D)] * 4,
        out_shape=[out] * 4,
        compiler_params=params(),
        cost_estimate=cost(2 * ext * D * 3 * D, ext * D * 10 + D * D * 6),
        name="qkv",
    )(x_ext, gain, w, cos, sl, sr)


def two_heads(u):
    lane = lax.broadcasted_iota(jnp.int32, u.shape, 1)
    zero = jnp.zeros_like(u)
    return jnp.concatenate([jnp.where(lane < HD, u, zero), jnp.where(lane >= HD, u, zero)], axis=0)


def one_row(u):
    n = u.shape[0] // 2
    lane = lax.broadcasted_iota(jnp.int32, (n, PAIR), 1)
    return jnp.where(lane < HD, u[:n], u[n:])


def band(key_axis, b, last, side_ref):
    shape = (2 * QB, QB + 2 * HALF) if key_axis == 1 else (QB + 2 * HALF, 2 * QB)
    key = lax.broadcasted_iota(jnp.int32, shape, key_axis)
    query = lax.broadcasted_iota(jnp.int32, shape, 1 - key_axis) & (QB - 1)
    off = key - query
    low = jnp.where((b > 0) | (side_ref[0] > 0), 0, HALF)
    high = jnp.where((b < last) | (side_ref[1] > 0), QB + 2 * HALF, QB + HALF)
    return (off >= 0) & (off <= 2 * HALF) & (key >= low) & (key < high)


def attend_body(side_ref, q_ref, k_ref, v_ref, x_ref, w_ref, gain_ref, mixed_ref, middle_ref, n2_ref):
    i = pl.program_id(0)
    last = pl.num_programs(0) * (TILE // QB) - 1
    for s in range(TILE // QB):
        b = i * (TILE // QB) + s
        start = pl.multiple_of(b * QB, QB)
        ok = band(1, b, last, side_ref)
        for p in range(D // PAIR):
            cols = slice(p * PAIR, (p + 1) * PAIR)
            q2 = two_heads(q_ref[pl.ds(start + HALF, QB), cols])
            scores = dot_bt(q2, k_ref[pl.ds(start, QB + 2 * HALF), cols])
            scores = jnp.where(ok, scores, NEG_FILL)
            e = jnp.exp(scores - jnp.max(scores, axis=1, keepdims=True))
            probs = (e * (1.0 / jnp.sum(e, axis=1, keepdims=True))).astype(BF)
            o = dot(probs, v_ref[pl.ds(start, QB + 2 * HALF), cols])
            mixed_ref[s * QB : (s + 1) * QB, cols] = one_row(o).astype(BF)
    middle = x_ref[...].astype(F32) + dot(mixed_ref[...], w_ref[...])
    middle_ref[...] = middle
    n, _ = normalize(middle)
    n2_ref[...] = (n * gain_ref[...]).astype(BF)


def attend_call(side, q, k, v, x, w, gain):
    n = x.shape[0]
    ext = q.shape[0]
    return pl.pallas_call(
        attend_body,
        grid=(n // TILE,),
        in_specs=[
            pl.BlockSpec(memory_space=pltpu.SMEM),
            full((ext, D)), full((ext, D)), full((ext, D)), rows(TILE, D), full((D, D)), full((1, D)),
        ],
        out_specs=[rows(TILE, D)] * 3,
        out_shape=[
            jax.ShapeDtypeStruct((n, D), BF), jax.ShapeDtypeStruct((n, D), F32), jax.ShapeDtypeStruct((n, D), BF),
        ],
        compiler_params=params(),
        cost_estimate=cost(2 * n * D * (D + 16 * QB), n * D * 16),
        name="attend",
    )(side, q, k, v, x, w, gain)


def ffn_body(first, *refs):
    if first:
        n2_ref, cot_ref, wg_ref, wu_ref, wd_ref, out_ref, gn_ref, gg_ref, gu_ref, gd_ref, ag, au, ad = refs
    else:
        n2_ref, cot_ref, wg_ref, wu_ref, wd_ref, pout_ref, pgn_ref, out_ref, gn_ref, gg_ref, gu_ref, gd_ref, ag, au, ad = refs
    i = pl.program_id(0)
    n2 = n2_ref[...]
    cot = cot_ref[...]
    gate = dot(n2, wg_ref[...])
    up = dot(n2, wu_ref[...])
    ga = dot_bt(cot, wd_ref[...])
    phi = 0.5 + 0.5 * lax.erf(gate * (2.0**-0.5))
    gelu = gate * phi
    act = (gelu * up).astype(BF)
    slope = phi + gate * (jnp.exp(-0.5 * gate * gate) * 0.3989422804014327)
    dgate = (ga * up * slope).astype(BF)
    dup = (ga * gelu).astype(BF)
    out = dot(act, wd_ref[...])
    gn = dot_bt(dgate, wg_ref[...]) + dot_bt(dup, wu_ref[...])
    if first:
        out_ref[...] = out
        gn_ref[...] = gn
    else:
        out_ref[...] = pout_ref[...] + out
        gn_ref[...] = pgn_ref[...] + gn

    @pl.when(i == 0)
    def _():
        ag[...] = jnp.zeros_like(ag)
        au[...] = jnp.zeros_like(au)
        ad[...] = jnp.zeros_like(ad)

    ag[...] += dot_at(n2, dgate)
    au[...] += dot_at(n2, dup)
    ad[...] += dot_at(act, cot)

    @pl.when(i == pl.num_programs(0) - 1)
    def _():
        gg_ref[...] = ag[...].astype(BF)
        gu_ref[...] = au[...].astype(BF)
        gd_ref[...] = ad[...].astype(BF)


def ffn_call(c, n2, cot, w_in, w_down, before):
    import functools

    n = n2.shape[0]
    up_at = FF // CHUNK
    first = before is None
    in_specs = [
        rows(TILE, D), rows(TILE, D),
        pl.BlockSpec((D, CHUNK), lambda i: (0, c)),
        pl.BlockSpec((D, CHUNK), lambda i: (0, up_at + c)),
        pl.BlockSpec((CHUNK, D), lambda i: (c, 0)),
    ]
    args = [n2, cot, w_in, w_in, w_down]
    if not first:
        in_specs += [rows(TILE, D)] * 2
        args += list(before)
    part = jax.ShapeDtypeStruct((n, D), F32)
    return pl.pallas_call(
        functools.partial(ffn_body, first),
        grid=(n // TILE,),
        in_specs=in_specs,
        out_specs=[rows(TILE, D), rows(TILE, D), full((D, CHUNK)), full((D, CHUNK)), full((CHUNK, D))],
        out_shape=[
            part, part,
            jax.ShapeDtypeStruct((D, CHUNK), BF), jax.ShapeDtypeStruct((D, CHUNK), BF), jax.ShapeDtypeStruct((CHUNK, D), BF),
        ],
        scratch_shapes=[pltpu.VMEM((D, CHUNK), F32), pltpu.VMEM((D, CHUNK), F32), pltpu.VMEM((CHUNK, D), F32)],
        compiler_params=params(),
        cost_estimate=cost(2 * n * D * CHUNK * 9, n * D * 20),
        name="ffn",
    )(*args)


def norm_back(grad, n, r, gain):
    e = grad * gain
    return r * (e - jnp.mean(e, axis=-1, keepdims=True) - n * jnp.mean(e * n, axis=-1, keepdims=True))


def middle_body(mid_ref, gn_ref, ffn_ref, cot_ref, mixed_ref, w_ref, gain_ref,
                out_ref, gmid_ref, gmix_ref, gw_ref, gg_ref, acc):
    i = pl.program_id(0)
    middle = mid_ref[...]
    gn = gn_ref[...]
    out_ref[...] = (middle + ffn_ref[...]).astype(BF)
    n, r = normalize(middle)

    @pl.when(i == 0)
    def _():
        gg_ref[...] = jnp.zeros_like(gg_ref)
        acc[...] = jnp.zeros_like(acc)

    gg_ref[...] += jnp.sum(gn * n, axis=0, keepdims=True)
    gmid = cot_ref[...].astype(F32) + norm_back(gn, n, r, gain_ref[...])
    gmid_ref[...] = gmid
    branch = gmid.astype(BF)
    gmix_ref[...] = dot_bt(branch, w_ref[...]).astype(BF)
    acc[...] += dot_at(mixed_ref[...], branch)

    @pl.when(i == pl.num_programs(0) - 1)
    def _():
        gw_ref[...] = acc[...].astype(BF)


def middle_call(middle, gn, ffn, cot, mixed, w, gain):
    n = middle.shape[0]
    return pl.pallas_call(
        middle_body,
        grid=(n // TILE,),
        in_specs=[rows(TILE, D)] * 5 + [full((D, D)), full((1, D))],
        out_specs=[rows(TILE, D)] * 3 + [full((D, D)), full((1, D))],
        out_shape=[
            jax.ShapeDtypeStruct((n, D), BF), jax.ShapeDtypeStruct((n, D), F32), jax.ShapeDtypeStruct((n, D), BF),
            jax.ShapeDtypeStruct((D, D), BF), jax.ShapeDtypeStruct((1, D), F32),
        ],
        scratch_shapes=[pltpu.VMEM((D, D), F32)],
        compiler_params=params(),
        cost_estimate=cost(4 * n * D * D, n * D * 24),
        name="middle",
    )(middle, gn, ffn, cot, mixed, w, gain)


def attend_back_body(side_ref, q_ref, k_ref, v_ref, g_ref, cos_ref, sl_ref, sr_ref,
                     dq_ref, dk_ref, dv_ref, ak, av):
    b = pl.program_id(0)
    last = pl.num_programs(0) - 1
    start = pl.multiple_of(b * QB, QB)
    win = pl.ds(start, QB + 2 * HALF)
    here = pl.ds(start + HALF, QB)

    @pl.when(b == 0)
    def _():
        ak[...] = jnp.zeros_like(ak)
        av[...] = jnp.zeros_like(av)

    ok = band(0, b, last, side_ref)
    cos, sl, sr = cos_ref[here, :], sl_ref[here, :], sr_ref[here, :]
    for p in range(D // PAIR):
        cols = slice(p * PAIR, (p + 1) * PAIR)
        q2 = two_heads(q_ref[here, cols])
        g2 = two_heads(g_ref[:, cols])
        kw = k_ref[win, cols]
        scores = jnp.where(ok, dot_bt(kw, q2), NEG_FILL)
        e = jnp.exp(scores - jnp.max(scores, axis=0, keepdims=True))
        probs = e * (1.0 / jnp.sum(e, axis=0, keepdims=True))
        dp = dot_bt(v_ref[win, cols], g2)
        ds = (probs * (dp - jnp.sum(probs * dp, axis=0, keepdims=True))).astype(BF)
        ak[win, cols] += dot(ds, q2)
        av[win, cols] += dot(probs.astype(BF), g2)
        dq = one_row(dot_at(ds, kw)) * HD**-0.5
        dq_ref[:, cols] = turn(dq, cos, -sl, -sr).astype(BF)

    @pl.when(b == last)
    def _():
        cos, sl, sr = cos_ref[...], -sl_ref[...], -sr_ref[...]
        for p in range(D // PAIR):
            cols = slice(p * PAIR, (p + 1) * PAIR)
            dk_ref[:, cols] = turn(ak[:, cols], cos, sl, sr).astype(BF)
        dv_ref[...] = av[...].astype(BF)


def attend_back_call(side, q, k, v, g, cos, sl, sr):
    n = g.shape[0]
    ext = q.shape[0]
    return pl.pallas_call(
        attend_back_body,
        grid=(n // QB,),
        in_specs=[
            pl.BlockSpec(memory_space=pltpu.SMEM),
            full((ext, D)), full((ext, D)), full((ext, D)), rows(QB, D),
            full((ext, PAIR)), full((ext, PAIR)), full((ext, PAIR)),
        ],
        out_specs=[rows(QB, D), full((ext, D)), full((ext, D))],
        out_shape=[
            jax.ShapeDtypeStruct((n, D), BF), jax.ShapeDtypeStruct((ext, D), BF), jax.ShapeDtypeStruct((ext, D), BF),
        ],
        scratch_shapes=[pltpu.VMEM((ext, D), F32), pltpu.VMEM((ext, D), F32)],
        compiler_params=params(),
        cost_estimate=cost(2 * n * D * 40 * QB, n * D * 16),
        name="attend_back",
    )(side, q, k, v, g, cos, sl, sr)


def qkv_back_body(x_ref, normed_ref, dq_ref, dk_ref, dv_ref, rim_ref, gmid_ref, w_ref, gain_ref,
                  gin_ref, gw_ref, gg_ref, acc):
    i = pl.program_id(0)
    last = pl.num_programs(0) - 1
    start = pl.multiple_of(i * TILE, TILE)
    here = pl.ds(start + HALF, TILE)

    @pl.when(i == 0)
    def _():
        gg_ref[...] = jnp.zeros_like(gg_ref)
        acc[...] = jnp.zeros_like(acc)
        for at, ref in ((0, dk_ref), (D, dv_ref)):
            ref[HALF : 2 * HALF, :] += rim_ref[:HALF, at : at + D]

    @pl.when(i == last)
    def _():
        end = dk_ref.shape[0] - HALF
        for at, ref in ((0, dk_ref), (D, dv_ref)):
            ref[end - HALF : end, :] += rim_ref[HALF:, at : at + D]

    normed = normed_ref[here, :]
    total = jnp.zeros((TILE, D), F32)
    for part, d in enumerate((dq_ref[...], dk_ref[here, :], dv_ref[here, :])):
        cols = slice(part * D, (part + 1) * D)
        total += dot_bt(d, w_ref[:, cols])
        acc[:, cols] += dot_at(normed, d)
    n, r = normalize(x_ref[here, :].astype(F32))
    gg_ref[...] += jnp.sum(total * n, axis=0, keepdims=True)
    gin_ref[...] = (gmid_ref[...] + norm_back(total, n, r, gain_ref[...])).astype(BF)

    @pl.when(i == last)
    def _():
        gw_ref[...] = acc[...].astype(BF)


def qkv_back_call(x_ext, normed, dq, dk, dv, rim, gmid, w, gain):
    n = gmid.shape[0]
    ext = x_ext.shape[0]
    return pl.pallas_call(
        qkv_back_body,
        grid=(n // TILE,),
        in_specs=[
            full((ext, D)), full((ext, D)), rows(TILE, D), full((ext, D)), full((ext, D)), full((2 * HALF, 2 * D)),
            rows(TILE, D), full((D, 3 * D)), full((1, D)),
        ],
        out_specs=[rows(TILE, D), full((D, 3 * D)), full((1, D))],
        out_shape=[
            jax.ShapeDtypeStruct((n, D), BF), jax.ShapeDtypeStruct((D, 3 * D), BF), jax.ShapeDtypeStruct((1, D), F32),
        ],
        scratch_shapes=[pltpu.VMEM((D, 3 * D), F32)],
        compiler_params=params(),
        cost_estimate=cost(4 * n * D * 3 * D, n * D * 24),
        name="qkv_back",
    )(x_ext, normed, dq, dk, dv, rim, gmid, w, gain)


def adam_update(weight, grad, first_old, second, decay_rate):
    new_first = BETA_ONE * first_old + (1.0 - BETA_ONE) * grad
    new_second = BETA_TWO * second + (1.0 - BETA_TWO) * grad * grad
    first_hat = new_first / (1.0 - BETA_ONE**STEP)
    second_hat = new_second / (1.0 - BETA_TWO**STEP)
    change = -LEARN_RATE * (first_hat / (jnp.sqrt(second_hat) + ADAM_EPS) + decay_rate * weight)
    return (new_first, new_second, change)


def neighbours(count):
    up = [(i, i + 1) for i in range(count - 1)]
    return up, [(j, i) for i, j in up]


def local_part(x_ext, cot, side, place, weights, swap_rims):
    attn_w, out_w, ffn_w, down_w, gain_one, gain_two = weights
    ext = x_ext.shape[0]
    n = ext - 2 * HALF
    pos = place * n - HALF + jnp.arange(ext, dtype=jnp.int32)
    lane = jnp.arange(PAIR)
    freq = THETA ** (-2.0 * (lane % (HD // 2)).astype(F32) / HD)
    angle = pos.astype(F32)[:, None] * freq[None, :]
    cos = jnp.cos(angle)
    sin = jnp.sin(angle)
    low = (lane % HD < HD // 2)[None, :]
    sl = jnp.where(low, -sin, 0.0)
    sr = jnp.where(low, 0.0, sin)
    g1 = gain_one.astype(F32).reshape(1, D)
    g2 = gain_two.astype(F32).reshape(1, D)
    x = x_ext[HALF : HALF + n]
    normed, q, k, v = qkv_call(x_ext, g1, attn_w, cos, sl, sr)
    mixed, middle, n2 = attend_call(side, q, k, v, x, out_w, g2)
    acc = None
    gates, ups, downs = [], [], []
    for c in range(FF // CHUNK):
        ffn, gn, gg, gu, gd = ffn_call(c, n2, cot, ffn_w, down_w, acc)
        acc = (ffn, gn)
        gates.append(gg)
        ups.append(gu)
        downs.append(gd)
    block_out, gmid, gmix, g_out, gg_two = middle_call(middle, gn, ffn, cot, mixed, out_w, g2)
    dq, dk, dv = attend_back_call(side, q, k, v, gmix, cos, sl, sr)
    rim = swap_rims(dk, dv)
    grad_in, g_attn, gg_one = qkv_back_call(x_ext, normed, dq, dk, dv, rim, gmid, attn_w, g1)
    g_ffn = jnp.concatenate(gates + ups, axis=1)
    g_down = jnp.concatenate(downs, axis=0)
    return block_out, grad_in, (g_attn, g_out, g_ffn, g_down, gg_one.reshape(D), gg_two.reshape(D))


def shards(*args):
    hidden_in, cotangent, block_seq, block_place = args[:4]
    own_weights = args[4:10]
    firsts = args[10:16]
    seconds = args[16:22]
    weights = tuple(lax.all_gather(w, "wshard", axis=0, tiled=True) for w in own_weights)
    count = lax.axis_size("seq")
    at = lax.axis_index("seq")
    ids = block_seq[0]

    def pick(i):
        return lax.dynamic_index_in_dim(ids, i, keepdims=False)

    own = pick(at)
    left = (at > 0) & (pick(jnp.maximum(at - 1, 0)) == own)
    right = (at < count - 1) & (pick(jnp.minimum(at + 1, count - 1)) == own)
    side = jnp.stack([left, right]).astype(jnp.int32)
    place = lax.dynamic_index_in_dim(block_place[0], at, keepdims=False)
    x = hidden_in[0]
    n = x.shape[0]
    up, down = neighbours(count)
    x_ext = jnp.concatenate(
        [lax.ppermute(x[n - HALF :], "seq", up), x, lax.ppermute(x[:HALF], "seq", down)], axis=0
    )

    def swap_rims(dk, dv):
        first = jnp.concatenate([dk[:HALF], dv[:HALF]], axis=1)
        last = jnp.concatenate([dk[n + HALF :], dv[n + HALF :]], axis=1)
        return jnp.concatenate([lax.ppermute(last, "seq", up), lax.ppermute(first, "seq", down)], axis=0)

    block_out, grad_in, grads = local_part(x_ext, cotangent[0], side, place, weights, swap_rims)
    shard_grads = []
    for g in grads:
        s = lax.psum_scatter(g.astype(BF), "wshard", scatter_dimension=0, tiled=True)
        shard_grads.append(lax.psum(s, "seq").astype(F32))
    decays = (WEIGHT_DECAY, WEIGHT_DECAY, WEIGHT_DECAY, WEIGHT_DECAY, 0.0, 0.0)
    updates = [
        adam_update(w.astype(F32), g, m, v, c)
        for w, g, m, v, c in zip(own_weights, shard_grads, firsts, seconds, decays)
    ]
    return (
        (block_out[None], grad_in[None]) + tuple(shard_grads)
        + tuple(u[0] for u in updates) + tuple(u[1] for u in updates) + tuple(u[2] for u in updates)
    )


def solution(mesh):
    big = P("wshard", "seq", None)
    mat = P("wshard", None)
    vec = P("wshard")
    group = (mat, mat, mat, mat, vec, vec)
    in_specs = (big, big, mat, mat) + group * 3
    out_specs = (big, big) + group * 4
    return jax.shard_map(shards, mesh=mesh, in_specs=in_specs, out_specs=out_specs, check_vma=False)
```

```python
import functools

import jax
import jax.numpy as jnp
from jax import lax
from jax.experimental import pallas as pl
from jax.experimental.pallas import tpu as pltpu
from jax.sharding import PartitionSpec as P

D = 768
FF = 1152
HEADS = 12
HD = 64
HALF = 64
STEP = 10
PAIR = 2 * HD
QB = 128
TILE = 256
WIDE = 384
QUAD = 4 * HD

NORM_EPS = 1e-05
BETA_ONE = 0.9
BETA_TWO = 0.98
LEARN_RATE = 0.05
WEIGHT_DECAY = 0.01
ADAM_EPS = 1e-06
NEG_FILL = -1e30
THETA = 10000.0
BF = jnp.bfloat16
F32 = jnp.float32


def dot(left, right):
    return lax.dot_general(left, right, (((1,), (0,)), ((), ())), preferred_element_type=F32)


def dot_bt(left, right):
    return lax.dot_general(left, right, (((1,), (1,)), ((), ())), preferred_element_type=F32)


def dot_at(left, right):
    return lax.dot_general(left, right, (((0,), (0,)), ((), ())), preferred_element_type=F32)


def call(body, args, in_specs, out_specs, out_shape, megabytes, deps=(), aliases=None, **kw):
    first = len(args)
    n_out = len(out_shape)

    def wrapped(*refs):
        refs = refs[:first] + refs[first + len(deps) :]
        token = refs[first + n_out]
        token[...] = jnp.zeros_like(token)
        body(*refs[: first + n_out], *refs[first + n_out + 1 :])

    return pl.pallas_call(
        wrapped,
        in_specs=list(in_specs) + [pl.BlockSpec(memory_space=pl.ANY)] * len(deps),
        out_specs=list(out_specs) + [full((8, 128))],
        out_shape=list(out_shape) + [jax.ShapeDtypeStruct((8, 128), F32)],
        input_output_aliases=aliases or {},
        compiler_params=pltpu.CompilerParams(
            dimension_semantics=("arbitrary",), vmem_limit_bytes=megabytes * 1024 * 1024
        ),
        **kw,
    )(*args, *deps)


def full(shape):
    return pl.BlockSpec(shape, lambda i: (0,) * len(shape))


def rows(tile, width):
    return pl.BlockSpec((tile, width), lambda i: (i, 0))


def cost(microseconds):
    return pl.CostEstimate(flops=int(microseconds * 1.1e9), bytes_accessed=0, transcendentals=0)


def normalize(x):
    mean = jnp.mean(x, axis=-1, keepdims=True)
    centered = x - mean
    var = jnp.mean(centered * centered, axis=-1, keepdims=True)
    r = lax.rsqrt(var + NORM_EPS)
    return centered * r, r


def turn(u, cos, sin_left, sin_right):
    return u * cos + pltpu.roll(u, PAIR - HD // 2, 1) * sin_left + pltpu.roll(u, HD // 2, 1) * sin_right


def lay(w, parts, out_ref, first=0):
    r = out_ref.shape[0] // 4
    for i, ref in enumerate(parts):
        out_ref[pl.ds(pl.multiple_of((w ^ i) * r, 32), r), :] = ref[first : first + r, :]


def deal(w, acc, cols, keep_ref, send_ref, at):
    r = acc.shape[0] // 4
    c = w & 1
    for x in range(2):
        keep_ref[x, at : at + r, :] = acc[pl.ds(pl.multiple_of((2 * x + c) * r, 32), r), cols].astype(BF)
        send_ref[x, at : at + r, :] = acc[pl.ds(pl.multiple_of((2 * x + 1 - c) * r, 32), r), cols].astype(BF)


def smem():
    return pl.BlockSpec(memory_space=pltpu.SMEM)


def piece(n_rows):
    return jax.ShapeDtypeStruct((2, n_rows, WIDE), BF)


def qkv_body(info_ref, x_ref, gain_ref, wa, wb, wc, wd, cos_ref, sl_ref, sr_ref, nt_ref, q_ref, k_ref, v_ref, w_ref):
    @pl.when(pl.program_id(0) == 0)
    def _():
        lay(info_ref[2], (wa, wb, wc, wd), w_ref)

    n, _ = normalize(x_ref[...].astype(F32))
    normed = (n * gain_ref[...]).astype(BF)
    nt_ref[...] = normed.T
    cos, sl, sr = cos_ref[...], sl_ref[...], sr_ref[...]
    for part, ref, scale in ((0, q_ref, HD**-0.5), (1, k_ref, 1.0)):
        u = dot(normed, w_ref[:, part * D : (part + 1) * D])
        for p in range(D // PAIR):
            t = turn(u[:, p * PAIR : (p + 1) * PAIR], cos, sl, sr)
            ref[:, p * PAIR : (p + 1) * PAIR] = (t * scale).astype(BF)
    v_ref[...] = dot(normed, w_ref[:, 2 * D :]).astype(BF)


def qkv_call(info, x_ext, gain, w_parts, cos, sl, sr, deps=()):
    ext = x_ext.shape[0]
    t = ext // 3
    out = jax.ShapeDtypeStruct((ext, D), BF)
    return call(
        qkv_body,
        [info, x_ext, gain, *w_parts, cos, sl, sr],
        grid=(3,),
        in_specs=[smem(), rows(t, D), full((1, D))] + [full((D // 4, 3 * D))] * 4 + [rows(t, PAIR)] * 3,
        out_specs=[pl.BlockSpec((D, t), lambda i: (0, i))] + [rows(t, D)] * 3,
        out_shape=[jax.ShapeDtypeStruct((D, ext), BF)] + [out] * 3,
        scratch_shapes=[pltpu.VMEM((D, 3 * D), BF)],
        megabytes=18,
        deps=deps,
        cost_estimate=cost(9),
        name="qkv",
    )


def apart(u):
    head = lax.broadcasted_iota(jnp.int32, u.shape, 1) // HD
    zero = jnp.zeros_like(u)
    return jnp.concatenate([jnp.where(head == h, u, zero) for h in range(4)], axis=0)


def together(u):
    r = u.shape[0] // 4
    head = lax.broadcasted_iota(jnp.int32, (r, QUAD), 1) // HD
    out = u[:r]
    for h in range(1, 4):
        out = jnp.where(head == h, u[h * r : (h + 1) * r], out)
    return out


def repeat(u):
    return jnp.concatenate([u] * 4, axis=1)


def attend_body(info_ref, bias_ref, q_ref, k_ref, v_ref, x_ref, wa, wb, wc, wd, gain_ref,
                mixed_ref, middle_ref, n2_ref, w_ref, lse_ref):
    i = pl.program_id(0)
    last = pl.num_programs(0) * (TILE // QB) - 1

    @pl.when(i == 0)
    def _():
        lay(info_ref[2], (wa, wb, wc, wd), w_ref)

    for s in range(TILE // QB):
        b = i * (TILE // QB) + s
        start = pl.multiple_of(b * QB, QB)
        which = jnp.where(b == 0, 0, jnp.where(b == last, 2, 1))
        bias = repeat(bias_ref[which])
        for g in range(D // QUAD):
            cols = slice(g * QUAD, (g + 1) * QUAD)
            win = pl.ds(start, QB + 2 * HALF)
            q4 = apart(q_ref[pl.ds(start + HALF, QB), cols])
            scores = dot_bt(k_ref[win, cols], q4) + bias
            most = jnp.max(scores, axis=0, keepdims=True)
            e = jnp.exp(scores - most)
            total = jnp.sum(e, axis=0, keepdims=True)
            probs = (e * (1.0 / total)).astype(BF)
            o = together(dot_at(probs, v_ref[win, cols]))
            mixed_ref[s * QB : (s + 1) * QB, cols] = o.astype(BF)
            lse = most + jnp.log(total)
            for h in range(4):
                lse_ref[g, h : h + 1, s * QB : (s + 1) * QB] = lse[:, h * QB : (h + 1) * QB]
    middle = x_ref[...].astype(F32) + dot(mixed_ref[...], w_ref[...])
    middle_ref[...] = middle.astype(BF)
    n, _ = normalize(middle)
    n2_ref[...] = (n * gain_ref[...]).astype(BF)


def attend_call(info, bias, q, k, v, x, w_parts, gain, deps=()):
    n = x.shape[0]
    ext = q.shape[0]
    groups = D // QUAD
    return call(
        attend_body,
        [info, bias, q, k, v, x, *w_parts, gain],
        grid=(n // TILE,),
        in_specs=[smem(), full(bias.shape)] + [full((ext, D))] * 3 + [rows(TILE, D)] + [full((D // 4, D))] * 4 + [full((1, D))],
        out_specs=[rows(TILE, D)] * 3 + [full((D, D)), pl.BlockSpec((groups, 4, TILE), lambda i: (0, 0, i))],
        out_shape=[
            jax.ShapeDtypeStruct((n, D), BF), jax.ShapeDtypeStruct((n, D), BF), jax.ShapeDtypeStruct((n, D), BF),
            jax.ShapeDtypeStruct((D, D), BF), jax.ShapeDtypeStruct((groups, 4, n), F32),
        ],
        megabytes=12,
        deps=deps,
        cost_estimate=cost(11),
        name="attend",
    )


def hidden(n2, cot, wg, wu, wd):
    gate = dot(n2, wg)
    up = dot(n2, wu)
    ga = dot_bt(cot, wd)
    phi = 0.5 + 0.5 * lax.erf(gate * (2.0**-0.5))
    gelu = gate * phi
    act = (gelu * up).astype(BF)
    slope = phi + gate * (jnp.exp(-0.5 * gate * gate) * 0.3989422804014327)
    dgate = (ga * up * slope).astype(BF)
    dup = (ga * gelu).astype(BF)
    out = dot(act, wd)
    gn = dot_bt(dgate, wg) + dot_bt(dup, wu)
    return act, dgate, dup, out, gn


def ffn_a_body(info_ref, n2_ref, cot_ref, ga, gb, gc, gd, ua, ub, uc, ud, oa, ob, oc, od,
               out_ref, gn_ref, keep_ref, send_ref, wg_ref, wu_ref, wd_ref, acc, ad):
    i = pl.program_id(0)

    @pl.when(i == 0)
    def _():
        lay(info_ref[2], (ga, gb, gc, gd), wg_ref)
        lay(info_ref[2], (ua, ub, uc, ud), wu_ref)
        lay(info_ref[2], (oa, ob, oc, od), wd_ref)
        acc[...] = jnp.zeros_like(acc)
        ad[...] = jnp.zeros_like(ad)

    n2 = n2_ref[...]
    cot = cot_ref[...]
    nt = n2.T
    total_out = jnp.zeros((TILE, D), F32)
    total_gn = jnp.zeros((TILE, D), F32)
    for h in range(2):
        g, u = slice(h * WIDE, (h + 1) * WIDE), slice(D + h * WIDE, D + (h + 1) * WIDE)
        act, dgate, dup, out, gn = hidden(n2, cot, wg_ref[:, g], wu_ref[:, g], wd_ref[g, :])
        total_out += out
        total_gn += gn
        acc[:, g] += dot(nt, dgate)
        acc[:, u] += dot(nt, dup)
        ad[g, :] += dot_at(act, cot)
    out_ref[...] = total_out.astype(BF)
    gn_ref[...] = total_gn.astype(BF)

    @pl.when(i == pl.num_programs(0) - 1)
    def _():
        for b in range(4):
            deal(info_ref[2], acc, slice(b * WIDE, (b + 1) * WIDE), keep_ref, send_ref, b * D // 4)
        for b in range(2):
            deal(info_ref[2], ad, slice(b * WIDE, (b + 1) * WIDE), keep_ref, send_ref, (4 + b) * D // 4)


def ffn_a_call(info, n2, cot, gate_parts, up_parts, down_parts, deps=()):
    n = n2.shape[0]
    part = jax.ShapeDtypeStruct((n, D), BF)
    size = 6 * D // 4
    return call(
        ffn_a_body,
        [info, n2, cot, *gate_parts, *up_parts, *down_parts],
        grid=(n // TILE,),
        in_specs=[smem()] + [rows(TILE, D)] * 2 + [full((D // 4, D))] * 8 + [full((FF // 4, D))] * 4,
        out_specs=[rows(TILE, D)] * 2 + [full((2, size, WIDE))] * 2,
        out_shape=[part, part, piece(size), piece(size)],
        scratch_shapes=[pltpu.VMEM((D, D), BF)] * 3 + [pltpu.VMEM((D, 2 * D), F32), pltpu.VMEM((D, D), F32)],
        megabytes=24,
        deps=deps,
        cost_estimate=cost(18),
        name="ffn_a",
    )


def norm_back(grad, n, r, gain):
    e = grad * gain
    return r * (e - jnp.mean(e, axis=-1, keepdims=True) - n * jnp.mean(e * n, axis=-1, keepdims=True))


def ffn_b_body(info_ref, n2_ref, cot_ref, ia, ib, ic, id_, oa, ob, oc, od, pout_ref, pgn_ref, mid_ref, mixed_ref, wo_ref, gain_ref,
               out_ref, gmid_ref, gmix_ref, keep_ref, send_ref, w_ref, wd_ref, acc, ad, ao):
    i = pl.program_id(0)

    @pl.when(i == 0)
    def _():
        lay(info_ref[2], (ia, ib, ic, id_), w_ref)
        lay(info_ref[2], (oa, ob, oc, od), wd_ref, D // 4)
        acc[...] = jnp.zeros_like(acc)
        ao[...] = jnp.zeros_like(ao)
        ad[...] = jnp.zeros_like(ad)

    n2 = n2_ref[...]
    cot = cot_ref[...]
    act, dgate, dup, out, gn = hidden(n2, cot, w_ref[:, :WIDE], w_ref[:, WIDE:], wd_ref[...])
    nt = n2.T
    acc[:, :WIDE] += dot(nt, dgate)
    acc[:, WIDE:] += dot(nt, dup)
    ad[...] += dot_at(act, cot)
    middle = mid_ref[...].astype(F32)
    out_ref[...] = (middle + pout_ref[...].astype(F32) + out).astype(BF)
    n, r = normalize(middle)
    branch = (cot.astype(F32) + norm_back(pgn_ref[...].astype(F32) + gn, n, r, gain_ref[...])).astype(BF)
    gmid_ref[...] = branch
    gmix_ref[...] = dot_bt(branch, wo_ref[...]).astype(BF)
    ao[...] += dot_at(mixed_ref[...], branch)

    @pl.when(i == pl.num_programs(0) - 1)
    def _():
        w = info_ref[2]
        r = D // 4
        for b in range(2):
            cols = slice(b * WIDE, (b + 1) * WIDE)
            deal(w, acc, cols, keep_ref, send_ref, b * r)
            deal(w, ao, cols, keep_ref, send_ref, (2 + b) * r)
            deal(w, ad, cols, keep_ref, send_ref, 4 * r + b * r // 2)


def ffn_b_call(info, n2, cot, in_parts, down_parts, pout, pgn, middle, mixed, wo, gain, deps=()):
    n = n2.shape[0]
    size = 5 * D // 4
    return call(
        ffn_b_body,
        [info, n2, cot, *in_parts, *down_parts, pout, pgn, middle, mixed, wo, gain],
        grid=(n // TILE,),
        in_specs=[smem()] + [rows(TILE, D)] * 2 + [full((D // 4, D))] * 4 + [full((FF // 4, D))] * 4
        + [rows(TILE, D)] * 4 + [full((D, D)), full((1, D))],
        out_specs=[rows(TILE, D)] * 3 + [full((2, size, WIDE))] * 2,
        out_shape=[jax.ShapeDtypeStruct((n, D), BF)] * 3 + [piece(size), piece(size)],
        scratch_shapes=[pltpu.VMEM((D, D), BF), pltpu.VMEM((WIDE, D), BF),
                        pltpu.VMEM((D, D), F32), pltpu.VMEM((WIDE, D), F32), pltpu.VMEM((D, D), F32)],
        megabytes=24,
        deps=deps,
        cost_estimate=cost(14),
        name="ffn_b",
    )


def attend_back_body(info_ref, bias_ref, q_ref, k_ref, v_ref, g_ref, mixed_ref, lse_ref, cos_ref, sl_ref, sr_ref, nt_ref, *rest):
    dq_ref, dk_ref, dv_ref, keep_ref, send_ref, ak, av, aw = rest[-8:]
    ext = ak.shape[0]
    blocks = (ext - 2 * HALF) // QB
    ak[...] = jnp.zeros_like(ak)
    av[...] = jnp.zeros_like(av)
    zero = jnp.zeros((HALF, QUAD), BF)
    dq_ref[:HALF, :] = zero
    dq_ref[ext - HALF :, :] = zero
    prod = mixed_ref[...].astype(F32) * g_ref[...].astype(F32)
    head = lax.broadcasted_iota(jnp.int32, (8, QUAD), 1) // HD
    pick = jnp.where(head == lax.broadcasted_iota(jnp.int32, (8, QUAD), 0), 1.0, 0.0).astype(BF)
    high = prod.astype(BF)
    delta = dot_bt(pick, high) + dot_bt(pick, (prod - high.astype(F32)).astype(BF))

    def of_heads(a, start):
        return jnp.concatenate([a[h : h + 1, start : start + QB] for h in range(4)], axis=1)

    def unturn(u, at):
        cos, sl, sr = cos_ref[at, :], -sl_ref[at, :], -sr_ref[at, :]
        return jnp.concatenate([turn(u[:, c : c + PAIR], cos, sl, sr) for c in (0, PAIR)], axis=1).astype(BF)

    for b in range(blocks):
        start = b * QB
        win = slice(start, start + QB + 2 * HALF)
        here = slice(start + HALF, start + HALF + QB)
        bias = repeat(bias_ref[0 if b == 0 else 2 if b == blocks - 1 else 1])
        q4 = apart(q_ref[here, :])
        g4 = apart(g_ref[start : start + QB, :])
        kw = k_ref[win, :]
        probs = jnp.exp(dot_bt(kw, q4) + bias - of_heads(lse_ref[0], start))
        ds = (probs * (dot_bt(v_ref[win, :], g4) - of_heads(delta, start))).astype(BF)
        ak[win, :] += dot(ds, q4)
        av[win, :] += dot(probs.astype(BF), g4)
        dq_ref[here, :] = unturn(together(dot_at(ds, kw)) * HD**-0.5, here)
    dk_ref[...] = unturn(ak[...], slice(0, ext))
    dv_ref[...] = av[...].astype(BF)
    for part, ref in enumerate((dq_ref, dk_ref, dv_ref)):
        aw[...] = dot(nt_ref[...], ref[...])
        deal(info_ref[2], aw, slice(0, QUAD), keep_ref, send_ref, part * D // 4)


def attend_back_call(p, at, width, info, bias, q, k, v, g, mixed, lse, cos, sl, sr, nt, sofar, pieces, deps=()):
    n = g.shape[0]
    ext = q.shape[0]
    cols = pl.BlockSpec((ext, QUAD), lambda i: (0, p))
    inner = pl.BlockSpec((n, QUAD), lambda i: (0, p))
    own = jax.ShapeDtypeStruct((ext, D), BF)
    out = jax.ShapeDtypeStruct((2, 3 * D // 4, width), BF)
    args = [info, bias, q, k, v, g, mixed, lse, cos, sl, sr, nt]
    extra = list(sofar) + list(pieces)
    aliases = {}
    for i in range(len(sofar)):
        aliases[len(args) + i] = i
    for i in range(len(pieces)):
        aliases[len(args) + len(sofar) + i] = 3 + i
    mine = pl.BlockSpec((2, 3 * D // 4, QUAD), lambda i: (0, 0, at))
    return call(
        attend_back_body,
        args + extra,
        grid=(1,),
        in_specs=[smem(), full(bias.shape), cols, cols, cols, inner, inner, pl.BlockSpec((1, 4, n), lambda i: (p, 0, 0))]
        + [full((ext, PAIR))] * 3 + [full((D, ext))] + [pl.BlockSpec(memory_space=pl.ANY)] * len(extra),
        out_specs=[cols] * 3 + [mine] * 2,
        out_shape=[own, own, own, out, out],
        scratch_shapes=[pltpu.VMEM((ext, QUAD), F32), pltpu.VMEM((ext, QUAD), F32), pltpu.VMEM((D, QUAD), F32)],
        aliases=aliases,
        megabytes=12,
        deps=deps,
        cost_estimate=cost(4),
        name="attend_back",
    )


def last_body(info_ref, x_ref, dq_ref, dk_ref, dv_ref, rim_ref, gmid_ref, wa, wb, wc, wd, gain_ref, gin_ref, w_ref, *both):
    i = pl.program_id(0)
    start = pl.multiple_of(i * TILE, TILE)
    here = pl.ds(start + HALF, TILE)
    ext = x_ref.shape[0]

    @pl.when(i == 0)
    def _():
        lay(info_ref[2], (wa, wb, wc, wd), w_ref)
        for j, ref in enumerate((dk_ref, dv_ref)):
            cols = slice(j * D, (j + 1) * D)
            both[j][...] = ref[...]
            both[j][HALF : 2 * HALF, :] += rim_ref[:HALF, cols]
            both[j][ext - 2 * HALF : ext - HALF, :] += rim_ref[HALF:, cols]

    total = jnp.zeros((TILE, D), F32)
    for j, ref in enumerate((dq_ref, *both)):
        total += dot_bt(ref[here, :], w_ref[:, j * D : (j + 1) * D])
    n, r = normalize(x_ref[here, :].astype(F32))
    gin_ref[...] = (gmid_ref[...].astype(F32) + norm_back(total, n, r, gain_ref[...])).astype(BF)


def last_call(info, x_ext, grads, rim, gmid, w_parts, gain, deps=()):
    n = gmid.shape[0]
    ext = x_ext.shape[0]
    return call(
        last_body,
        [info, x_ext, *grads, rim, gmid, *w_parts, gain],
        grid=(n // TILE,),
        in_specs=[smem()] + [full((ext, D))] * 4 + [full((2 * HALF, 2 * D)), rows(TILE, D)] + [full((D // 4, 3 * D))] * 4 + [full((1, D))],
        out_specs=[rows(TILE, D)],
        out_shape=[jax.ShapeDtypeStruct((n, D), BF)],
        scratch_shapes=[pltpu.VMEM((D, 3 * D), BF)] + [pltpu.VMEM((ext, D), BF)] * 2,
        megabytes=16,
        deps=deps,
        cost_estimate=cost(7),
        name="last",
    )


def adam(weight, grad, first_old, second, decay_rate):
    new_first = BETA_ONE * first_old + (1.0 - BETA_ONE) * grad
    new_second = BETA_TWO * second + (1.0 - BETA_TWO) * grad * grad
    root = jnp.sqrt(new_second * (1.0 / (1.0 - BETA_TWO**STEP))) + ADAM_EPS
    change = (-LEARN_RATE / (1.0 - BETA_ONE**STEP)) * (new_first / root)
    if decay_rate:
        change = change - (LEARN_RATE * decay_rate) * weight
    return (new_first, new_second, change)


def adam_body(*refs):
    g_in, w_ref, m_ref, v_ref = refs[:4]
    g_ref, nm_ref, nv_ref, st_ref, dots_ref = refs[-5:]
    g = g_in[...].astype(F32)
    w = w_ref[...].astype(F32)
    g_ref[...] = g
    nm_ref[...], nv_ref[...], st_ref[...] = adam(w, g, m_ref[...], v_ref[...], WEIGHT_DECAY)

    @pl.when(pl.program_id(0) == 0)
    def _():
        dots_ref[...] = jnp.zeros_like(dots_ref)

    dots_ref[...] += jnp.sum(w * g, axis=1, keepdims=True)


def adam_call(grad, at, weight, first, second, wide, steps, cols, before=()):
    r, width = weight.shape
    own = pl.BlockSpec((r, wide), lambda j: (0, cols(j)))
    out = jax.ShapeDtypeStruct((r, width), F32)
    return pl.pallas_call(
        adam_body,
        grid=(steps,),
        in_specs=[pl.BlockSpec((r, wide), at)] + [own] * 3 + [pl.BlockSpec(memory_space=pl.ANY)] * len(before),
        out_specs=[own] * 4 + [full((r, 1))],
        out_shape=[out] * 4 + [jax.ShapeDtypeStruct((r, 1), F32)],
        input_output_aliases={4 + i: i for i in range(len(before))},
        compiler_params=pltpu.CompilerParams(dimension_semantics=("arbitrary",), vmem_limit_bytes=12 * 1024 * 1024),
        cost_estimate=cost(3),
        name="adam",
    )(grad, weight, first, second, *before)


def whole_adam(grad, weight, first, second):
    return adam_call(grad, lambda j: (0, j), weight, first, second, WIDE, weight.shape[1] // WIDE, lambda j: j)


CORES = [(0, 1), (1, 0), (2, 3), (3, 2)]
CHIPS = [(0, 2), (2, 0), (1, 3), (3, 1)]


def to_core(a):
    return lax.ppermute(a, "wshard", CORES)


def to_chip(a):
    return lax.ppermute(a, "wshard", CHIPS)


def after(a, first):
    return together_at([a, first])[0]


class Chain:
    def __init__(self, keep, send, halvings, seq_first=False):
        count = lax.axis_size("seq")
        self.kept = keep
        self.out = send
        plan = []
        shift = 0
        while 1 << shift < count:
            plan.append(("half" if shift < halvings else "whole", shift))
            shift += 1
        back = [("back", t) for kind, t in reversed(plan) if kind == "half"]
        plan.insert(1 if seq_first else 0, ("chip", 0))
        self.plan = [("core", 0)] + plan + back
        self.at = 0

    def done(self):
        return self.at == len(self.plan)

    def start(self):
        if self.done():
            return
        kind, shift = self.plan[self.at]
        sent = self.kept if self.out is None else self.out
        if kind == "core":
            self.flight = lax.ppermute(sent, "wshard", CORES)
        elif kind == "chip":
            self.flight = lax.ppermute(sent, "wshard", CHIPS)
        else:
            count = lax.axis_size("seq")
            self.flight = lax.ppermute(sent, "seq", [(i, i ^ (1 << shift)) for i in range(count)])

    def landing(self):
        kind, shift = self.plan[self.at]
        later = self.plan[self.at + 1] if self.at + 1 < len(self.plan) else ("end", 0)
        shape = self.kept.shape
        if kind == "back":
            shape = (2 * shape[0],) + shape[1:]
        if later[0] == "chip":
            shapes = [shape[1:]] * 2
        elif later[0] == "half":
            shapes = [shape[:-2] + (shape[-2] // 2, shape[-1])] * 2
        else:
            shapes = [shape]

        def bit(info_ref, kind, shift):
            return (info_ref[2] >> 1) & 1 if kind == "chip" else (info_ref[3] >> shift) & 1

        def body(info_ref, kept_ref, got_ref, outs):
            if kind == "back":
                r = kept_ref.shape[0]
                b = bit(info_ref, kind, shift)
                outs[0][pl.ds(pl.multiple_of(b * r, 16), r), :] = kept_ref[...]
                outs[0][pl.ds(pl.multiple_of((1 - b) * r, 16), r), :] = got_ref[...]
            elif later[0] == "chip":
                b = bit(info_ref, *later)
                outs[0][...] = sum_of(kept_ref[b], got_ref[b])
                outs[1][...] = sum_of(kept_ref[1 - b], got_ref[1 - b])
            elif later[0] == "half":
                b = bit(info_ref, *later)
                r = kept_ref.shape[-2] // 2
                for out, i in ((outs[0], b), (outs[1], 1 - b)):
                    here = pl.ds(pl.multiple_of(i * r, 16), r)
                    if len(shape) == 3:
                        out[...] = sum_of(kept_ref[:, here, :], got_ref[:, here, :])
                    else:
                        out[...] = sum_of(kept_ref[here, :], got_ref[here, :])
            else:
                outs[0][...] = sum_of(kept_ref[...], got_ref[...])

        return shapes, body

    def landed(self, outs):
        self.at += 1
        self.kept = outs[0]
        self.out = outs[1] if len(outs) > 1 else None


def sum_of(a, b):
    return (a.astype(F32) + b.astype(F32)).astype(BF)


def nothing(*refs):
    pass


def together_at(arrays):
    hbm = pl.BlockSpec(memory_space=pl.ANY)
    return pl.pallas_call(
        nothing,
        in_specs=[hbm] * len(arrays),
        out_specs=[hbm] * len(arrays),
        out_shape=[jax.ShapeDtypeStruct(a.shape, a.dtype) for a in arrays],
        input_output_aliases={i: i for i in range(len(arrays))},
        compiler_params=pltpu.CompilerParams(vmem_limit_bytes=1024 * 1024),
        name="boundary",
    )(*arrays)


def boundary(info, token, landing=(), starting=(), also=()):
    landing = [c for c in landing if not c.done()]
    plans = [c.landing() for c in landing]
    args = [info] + [a for c in landing for a in (c.kept, c.flight)]
    through = [c.out for c in starting] + list(also) + [token]
    shapes = [jax.ShapeDtypeStruct(t, BF) for p in plans for t in p[0]]
    count = len(args)

    def body(*refs):
        outs = list(refs[count + len(through) :])
        for i, (shapes_i, land) in enumerate(plans):
            land(refs[0], refs[1 + 2 * i], refs[2 + 2 * i], [outs.pop(0) for _ in shapes_i])

    hbm = pl.BlockSpec(memory_space=pl.ANY)
    outs = pl.pallas_call(
        body,
        grid=(1,),
        in_specs=[smem()] + [full(a.shape) for a in args[1:]] + [hbm] * len(through),
        out_specs=[full(t.shape) for t in shapes] + [hbm] * len(through),
        out_shape=shapes + [jax.ShapeDtypeStruct(a.shape, a.dtype) for a in through],
        input_output_aliases={count + i: len(shapes) + i for i in range(len(through))},
        compiler_params=pltpu.CompilerParams(vmem_limit_bytes=16 * 1024 * 1024),
        cost_estimate=cost(1),
        name="land",
    )(*args, *through)
    outs = list(outs)
    for c, (shapes_i, _) in zip(landing, plans):
        c.landed([outs.pop(0) for _ in shapes_i])
    for c in starting:
        c.out = outs.pop(0)
    waits = [outs[-1]]
    for c in landing + list(starting):
        waits.append(c.kept if c.out is None else c.out)
        c.start()
    return outs[:-1], tuple(waits)


def neighbours(count):
    up = [(i, i + 1) for i in range(count - 1)]
    return up, [(j, i) for i, j in up]


def shards(
    hidden_in, cotangent, block_seq, block_place, attn_in, attn_out, ffn_in, ffn_out, norm_attn, norm_ffn,
    m_attn_in, m_attn_out, m_ffn_in, m_ffn_out, m_norm_attn, m_norm_ffn,
    v_attn_in, v_attn_out, v_ffn_in, v_ffn_out, v_norm_attn, v_norm_ffn,
):
    x = hidden_in[0]
    cot = cotangent[0]
    n = x.shape[0]
    ext = n + 2 * HALF
    w = lax.axis_index("wshard")
    count = lax.axis_size("seq")
    at = lax.axis_index("seq")
    up, down = neighbours(count)

    far = to_chip(attn_in)
    mate = to_core(attn_in)
    mate, gain_own, x_low, x_high = together_at([mate, jnp.stack([norm_attn, norm_ffn]), x[:HALF], x[n - HALF :]])
    gain_far = to_chip(gain_own)
    gains = gain_own, to_core(gain_own), gain_far, to_core(gain_far)
    x_ext = jnp.concatenate([lax.ppermute(x_high, "seq", up), x, lax.ppermute(x_low, "seq", down)], axis=0)
    some, rest = D // 4, FF // 4 - D // 4

    def units(start, first, size):
        return [ffn_in[:, start + s * (FF // 4) + first :][:, :size] for s in range(4)]

    in_g = jnp.concatenate(units(0, 0, some), axis=1)
    in_u = jnp.concatenate(units(FF, 0, some), axis=1)
    in_b = jnp.concatenate(units(0, some, rest) + units(FF, some, rest), axis=1)
    out_mate, g_mate, u_mate, down_mate, b_mate = (to_core(a) for a in (attn_out, in_g, in_u, ffn_out, in_b))

    ids = block_seq[0]

    def pick(a, i):
        return lax.dynamic_index_in_dim(a, i, keepdims=False)

    own = pick(ids, at)
    left = (at > 0) & (pick(ids, jnp.maximum(at - 1, 0)) == own)
    right = (at < count - 1) & (pick(ids, jnp.minimum(at + 1, count - 1)) == own)
    info = jnp.stack([t.astype(jnp.int32) for t in (left, right, w, at)])
    key = jnp.arange(QB + 2 * HALF)[:, None]
    off = key - jnp.arange(QB)[None, :]
    band = (off >= 0) & (off <= 2 * HALF)
    bias = jnp.where(jnp.stack([band & (left | (key >= HALF)), band, band & (right | (key < QB + HALF))]), 0.0, NEG_FILL)
    pos = pick(block_place[0], at) * n - HALF + jnp.arange(ext, dtype=jnp.int32)
    lane = jnp.arange(PAIR)
    freq = THETA ** (-2.0 * (lane % (HD // 2)).astype(F32) / HD)
    angle = pos.astype(F32)[:, None] * freq[None, :]
    cos = jnp.cos(angle)
    sin = jnp.sin(angle)
    low = (lane % HD < HD // 2)[None, :]
    sl = jnp.where(low, -sin, 0.0)
    sr = jnp.where(low, 0.0, sin)
    by_owner = jnp.stack(gains)
    order = jnp.arange(4) ^ w
    gain = jnp.take(by_owner, order, axis=0).transpose(1, 0, 2).reshape(2, D).astype(F32)
    g1, g2 = gain[0:1], gain[1:2]

    far, in_g, x_ext, g1, g2, cos, sl, sr, bias, info, token, mate, out_mate, g_mate, u_mate, down_mate, b_mate = together_at(
        [far, in_g, x_ext, g1, g2, cos, sl, sr, bias, info, jnp.zeros((8, 128), F32),
         mate, out_mate, g_mate, u_mate, down_mate, b_mate]
    )
    farmate = to_core(far)
    out_far = to_chip(after(attn_out, token))
    g_far = to_chip(in_g)
    attn_parts = attn_in, mate, far, farmate
    nt, q, k, v, token = qkv_call(info, x_ext, g1, attn_parts, cos, sl, sr)
    out_far, g_far, in_u, token = together_at([out_far, g_far, in_u, token])
    out_farmate = to_core(out_far)
    out_farmate, in_u, down_own, token = together_at([out_farmate, in_u, ffn_out, token])
    u_far = to_chip(in_u)
    down_far = to_chip(down_own)
    out_parts = attn_out, out_mate, out_far, out_farmate
    mixed, middle, n2, out_w, lse, token = attend_call(info, bias, q, k, v, x, out_parts, g2, deps=(token,))
    u_far, down_far, in_b, token = together_at([u_far, down_far, in_b, token])
    g_farmate = to_core(g_far)
    b_far = to_chip(in_b)
    gate_parts = in_g, g_mate, g_far, g_farmate
    up_parts = in_u, u_mate, u_far, to_core(u_far)
    down_parts = ffn_out, down_mate, down_far, to_core(down_far)
    pout, pgn, keep, send, token = ffn_a_call(info, n2, cot, gate_parts, up_parts, down_parts, deps=(token,))
    chain_a = Chain(keep, send, 2)
    (b_far,), deps = boundary(info, token, (), (chain_a,), (b_far,))
    b_parts = in_b, b_mate, b_far, to_core(b_far)
    _, deps = boundary(info, deps[0], (chain_a,))
    block_out, gmid, gmix, keep, send, token = ffn_b_call(
        info, n2, cot, b_parts, down_parts, pout, pgn, middle, mixed, out_w, g2, deps=deps
    )
    chain_b = Chain(keep, send, 1)
    grads, pieces = (), ()

    def back(p, at, width, deps):
        nonlocal grads, pieces
        if at == 0:
            pieces = ()
        out = attend_back_call(p, at, width, info, bias, q, k, v, gmix, mixed, lse, cos, sl, sr, nt, grads, pieces, deps)
        grads, pieces = out[:3], out[3:5]
        return out[5]

    _, deps = boundary(info, token, (chain_a,), (chain_b,))
    token = back(0, 0, 2 * QUAD, deps)
    _, deps = boundary(info, token, (chain_a, chain_b))
    token = back(1, 1, 2 * QUAD, deps)
    chain_c = Chain(*pieces, 1)
    _, deps = boundary(info, token, (chain_a,), (chain_c,))
    token = back(2, 0, QUAD, deps)
    chain_d = Chain(*pieces, 1, True)
    rims = [jnp.concatenate([a[r] for a in grads[1:]], axis=1) for r in (slice(0, HALF), slice(n + HALF, ext))]
    rims, deps = boundary(info, token, (chain_a, chain_b, chain_c), (chain_d,), rims)
    rim = jnp.concatenate([lax.ppermute(rims[1], "seq", up), lax.ppermute(rims[0], "seq", down)], axis=0)
    (rim,), deps = boundary(info, deps[0], (chain_d,), (), (rim,))
    grad_in, token = last_call(info, x_ext, grads, rim, gmid, attn_parts, g1, deps=deps)
    chains = (chain_a, chain_b, chain_c, chain_d)
    while not all(c.done() for c in chains):
        _, deps = boundary(info, token, chains)
        token = deps[0]
    sum_a, sum_b, sum_c, sum_d = (c.kept for c in chains)

    r = D // 4

    def blocks(a, *at):
        return jnp.concatenate([a[i * r : (i + 1) * r] for i in at], axis=1)

    ga, gb = blocks(sum_a, 0, 1), sum_b[:r]
    ua, ub = blocks(sum_a, 2, 3), sum_b[r : 2 * r]
    g_ffn_in = jnp.concatenate(
        [t for a, b in ((ga, gb), (ua, ub)) for s in range(4)
         for t in (a[:, s * some : (s + 1) * some], b[:, s * rest : (s + 1) * rest])], axis=1
    )
    g_ffn_out = jnp.concatenate(
        [blocks(sum_a, 4, 5), jnp.concatenate([sum_b[4 * r : 4 * r + rest], sum_b[4 * r + rest :]], axis=1)], axis=0
    )
    res_ffn_in = whole_adam(g_ffn_in, ffn_in, m_ffn_in, v_ffn_in)
    res_attn_out = whole_adam(blocks(sum_b, 2, 3), attn_out, m_attn_out, v_attn_out)
    res_ffn_out = whole_adam(g_ffn_out, ffn_out, m_ffn_out, v_ffn_out)
    own_attn = attn_in, m_attn_in, v_attn_in, QUAD
    most = adam_call(sum_c, lambda j: (j // 2, j % 2), *own_attn, 6, lambda j: 3 * (j // 2) + j % 2)
    res_attn_in = adam_call(sum_d, lambda j: (j, 0), *own_attn, 3, lambda j: 3 * j + 2, most[:4])
    res_attn_in = list(res_attn_in[:4]) + [res_attn_in[4] + most[4]]
    results = [res_attn_in, res_attn_out, res_ffn_in, res_ffn_out]
    for res, own_gain, m, v_ in ((res_attn_in, norm_attn, m_norm_attn, v_norm_attn), (res_ffn_in, norm_ffn, m_norm_ffn, v_norm_ffn)):
        wide = own_gain.astype(F32)
        g = res[4][:, 0] / wide
        results.append((g,) + adam(wide, g, m, v_, 0.0))
    return (block_out[None], grad_in[None]) + tuple(res[i] for i in range(4) for res in results)


def solution(mesh):
    big = P("wshard", "seq", None)
    mat = P("wshard", None)
    vec = P("wshard")
    group = (mat, mat, mat, mat, vec, vec)
    in_specs = (big, big, mat, mat) + group * 3
    out_specs = (big, big) + group * 4
    return jax.shard_map(shards, mesh=mesh, in_specs=in_specs, out_specs=out_specs, check_vma=False)
```

```python
import functools

import jax
import jax.numpy as jnp
import numpy as np
from jax import lax
from jax.experimental import pallas as pl
from jax.experimental.pallas import tpu as pltpu
from jax.sharding import PartitionSpec as P

D = 768
FF = 1152
HEADS = 12
HD = 64
HALF = 64
STEP = 10
PAIR = 2 * HD
QB = 128
TILE = 256
WIDE = 384
QUAD = 4 * HD

NORM_EPS = 1e-05
BETA_ONE = 0.9
BETA_TWO = 0.98
LEARN_RATE = 0.05
WEIGHT_DECAY = 0.01
ADAM_EPS = 1e-06
NEG_FILL = -1e30
THETA = 10000.0
BF = jnp.bfloat16
F32 = jnp.float32


def dot(left, right):
    return lax.dot_general(left, right, (((1,), (0,)), ((), ())), preferred_element_type=F32)


def dot_bt(left, right):
    return lax.dot_general(left, right, (((1,), (1,)), ((), ())), preferred_element_type=F32)


def dot_at(left, right):
    return lax.dot_general(left, right, (((0,), (0,)), ((), ())), preferred_element_type=F32)


def call(body, args, in_specs, out_specs, out_shape, megabytes, deps=(), aliases=None, **kw):
    first = len(args)
    n_out = len(out_shape)

    def wrapped(*refs):
        refs = refs[:first] + refs[first + len(deps) :]
        token = refs[first + n_out]
        token[...] = jnp.zeros_like(token)
        body(*refs[: first + n_out], *refs[first + n_out + 1 :])

    return pl.pallas_call(
        wrapped,
        in_specs=list(in_specs) + [pl.BlockSpec(memory_space=pl.ANY)] * len(deps),
        out_specs=list(out_specs) + [full((8, 128))],
        out_shape=list(out_shape) + [jax.ShapeDtypeStruct((8, 128), F32)],
        input_output_aliases=aliases or {},
        compiler_params=pltpu.CompilerParams(
            dimension_semantics=("arbitrary",), vmem_limit_bytes=megabytes * 1024 * 1024
        ),
        **kw,
    )(*args, *deps)


def full(shape):
    return pl.BlockSpec(shape, lambda i: (0,) * len(shape))


def rows(tile, width):
    return pl.BlockSpec((tile, width), lambda i: (i, 0))


def cost(microseconds):
    return pl.CostEstimate(flops=int(microseconds * 1.1e9), bytes_accessed=0, transcendentals=0)


def normalize(x):
    mean = jnp.mean(x, axis=-1, keepdims=True)
    centered = x - mean
    var = jnp.mean(centered * centered, axis=-1, keepdims=True)
    r = lax.rsqrt(var + NORM_EPS)
    return centered * r, r


def signed(sin):
    first = lax.broadcasted_iota(jnp.int32, sin.shape, 1) % HD < HD // 2
    zero = jnp.zeros_like(sin)
    return jnp.where(first, -sin, zero), jnp.where(first, zero, sin)


def turn(u, cos, sin_left, sin_right):
    return u * cos + pltpu.roll(u, PAIR - HD // 2, 1) * sin_left + pltpu.roll(u, HD // 2, 1) * sin_right


def blocks_of(info_ref):
    return (info_ref.shape[0] - 2) // 2


def sides(info_ref):
    count = blocks_of(info_ref)
    at = info_ref[1]
    own = info_ref[2 + at]
    left = (at > 0) & (info_ref[2 + jnp.maximum(at - 1, 0)] == own)
    right = (at < count - 1) & (info_ref[2 + jnp.minimum(at + 1, count - 1)] == own)
    return left, right


def bias_of(b, last, left, right):
    shape = (QB + 2 * HALF, QB)
    key = lax.broadcasted_iota(jnp.int32, shape, 0)
    off = key - lax.broadcasted_iota(jnp.int32, shape, 1)
    low = jnp.where((b > 0) | left, 0, HALF)
    high = jnp.where((b < last) | right, QB + 2 * HALF, QB + HALF)
    ok = (off >= 0) & (off <= 2 * HALF) & (key >= low) & (key < high)
    return jnp.where(ok, 0.0, NEG_FILL)


def lay(w, parts, out_ref, bit=0):
    r = out_ref.shape[0] // 4
    for i, ref in enumerate(parts):
        start = (w ^ i) * r
        if isinstance(ref, tuple):
            half = r // 2
            for j, a in enumerate(ref):
                out_ref[pl.ds(pl.multiple_of(start + (bit ^ j) * half, 16), half), :] = a[...]
        else:
            out_ref[pl.ds(pl.multiple_of(start, 32), r), :] = ref[...]


def deal(w, acc, cols, keep_ref, send_ref, at):
    r = acc.shape[0] // 4
    c = w & 1
    for x in range(2):
        keep_ref[x, at : at + r, :] = acc[pl.ds(pl.multiple_of((2 * x + c) * r, 32), r), cols].astype(BF)
        send_ref[x, at : at + r, :] = acc[pl.ds(pl.multiple_of((2 * x + 1 - c) * r, 32), r), cols].astype(BF)


def smem():
    return pl.BlockSpec(memory_space=pltpu.SMEM)


def piece(n_rows):
    return jax.ShapeDtypeStruct((2, n_rows, WIDE), BF)


def qkv_body(info_ref, x_ref, low_ref, high_ref, gain_a, gain_b, gain_c, gain_d, wa, wb, wc, wd, far_ref, near_ref,
             nt_ref, q_ref, k_ref, v_ref, cos_ref, sin_ref, gain_ref, w_ref, x_ext):
    t = q_ref.shape[0]
    i = pl.program_id(0)

    @pl.when(i == 0)
    def _():
        lay(info_ref[0], (wa, wb, wc, wd), w_ref)
        end = x_ext.shape[0] - HALF
        x_ext[:HALF, :] = low_ref[...]
        x_ext[HALF:end, :] = x_ref[...]
        x_ext[end:, :] = high_ref[...]
        r = D // 4
        for p, ref in enumerate((gain_a, gain_b, gain_c, gain_d)):
            gains = ref[...].astype(F32)
            for owner in range(4):

                @pl.when((info_ref[0] ^ p) == owner)
                def _():
                    gain_ref[:2, owner * r : (owner + 1) * r] = gains


    place = info_ref[2 + blocks_of(info_ref) + info_ref[1]]
    c2, s2 = far_ref[0, pl.ds(place, 1), :], far_ref[1, pl.ds(place, 1), :]
    c1, s1 = near_ref[0], near_ref[1]
    cos = c1 * c2 - s1 * s2
    sin = s1 * c2 + c1 * s2
    cos_ref[...] = cos
    sin_ref[...] = sin
    sl, sr = signed(sin)
    n, _ = normalize(x_ext[pl.ds(pl.multiple_of(i * t, 128), t), :].astype(F32))
    normed = (n * gain_ref[0:1, :]).astype(BF)
    nt_ref[...] = normed.T
    for part, ref, scale in ((0, q_ref, HD**-0.5), (1, k_ref, 1.0)):
        u = dot(normed, w_ref[:, part * D : (part + 1) * D])
        for p in range(D // PAIR):
            r = turn(u[:, p * PAIR : (p + 1) * PAIR], cos, sl, sr)
            ref[:, p * PAIR : (p + 1) * PAIR] = (r * scale).astype(BF)
    v_ref[...] = dot(normed, w_ref[:, 2 * D :]).astype(BF)


def angle_tables(n, ext):
    freq = THETA ** (-2.0 * (np.arange(PAIR) % (HD // 2)) / HD)

    def table(positions):
        angle = positions[:, None] * freq[None, :]
        return jnp.asarray(np.stack([np.cos(angle), np.sin(angle)]).astype(np.float32))

    return table(np.arange(4.0) * n), table(np.arange(float(ext)) - HALF)


def qkv_call(info, x, low, high, gains, w_parts, deps=()):
    n = x.shape[0]
    ext = n + 2 * HALF
    t = ext // 3
    out = jax.ShapeDtypeStruct((ext, D), BF)
    table = jax.ShapeDtypeStruct((ext, PAIR), F32)
    far, near = angle_tables(n, ext)
    return call(
        qkv_body,
        [info, x, low, high, *gains, *w_parts, far, near],
        grid=(3,),
        in_specs=[smem(), full((n, D)), full((HALF, D)), full((HALF, D))] + [full((2, D // 4))] * 4 + [full((D // 4, 3 * D))] * 4
        + [full(far.shape), pl.BlockSpec((2, t, PAIR), lambda i: (0, i, 0))],
        out_specs=[pl.BlockSpec((D, t), lambda i: (0, i))] + [rows(t, D)] * 3 + [rows(t, PAIR)] * 2 + [full((8, D))],
        out_shape=[jax.ShapeDtypeStruct((D, ext), BF)] + [out] * 3 + [table] * 2 + [jax.ShapeDtypeStruct((8, D), F32)],
        scratch_shapes=[pltpu.VMEM((D, 3 * D), BF), pltpu.VMEM((ext, D), BF)],
        megabytes=20,
        deps=deps,
        cost_estimate=cost(9),
        name="qkv",
    )


def apart(u):
    head = lax.broadcasted_iota(jnp.int32, u.shape, 1) // HD
    zero = jnp.zeros_like(u)
    return jnp.concatenate([jnp.where(head == h, u, zero) for h in range(4)], axis=0)


def together(u):
    r = u.shape[0] // 4
    head = lax.broadcasted_iota(jnp.int32, (r, QUAD), 1) // HD
    out = u[:r]
    for h in range(1, 4):
        out = jnp.where(head == h, u[h * r : (h + 1) * r], out)
    return out


def repeat(u):
    return jnp.concatenate([u] * 4, axis=1)


def attend_body(info_ref, q_ref, k_ref, v_ref, x_ref, wa, wb, wc, wd, gain_ref,
                mixed_ref, middle_ref, n2_ref, w_ref, lse_ref):
    i = pl.program_id(0)
    last = pl.num_programs(0) * (TILE // QB) - 1
    left, right = sides(info_ref)

    @pl.when(i == 0)
    def _():
        lay(info_ref[0], (wa, wb, wc, wd), w_ref)

    for s in range(TILE // QB):
        b = i * (TILE // QB) + s
        start = pl.multiple_of(b * QB, QB)
        bias = repeat(bias_of(b, last, left, right))
        for g in range(D // QUAD):
            cols = slice(g * QUAD, (g + 1) * QUAD)
            win = pl.ds(start, QB + 2 * HALF)
            q4 = apart(q_ref[pl.ds(start + HALF, QB), cols])
            scores = dot_bt(k_ref[win, cols], q4) + bias
            most = jnp.max(scores, axis=0, keepdims=True)
            e = jnp.exp(scores - most)
            total = jnp.sum(e, axis=0, keepdims=True)
            probs = (e * (1.0 / total)).astype(BF)
            o = together(dot_at(probs, v_ref[win, cols]))
            mixed_ref[s * QB : (s + 1) * QB, cols] = o.astype(BF)
            lse = most + jnp.log(total)
            for h in range(4):
                lse_ref[g, h : h + 1, s * QB : (s + 1) * QB] = lse[:, h * QB : (h + 1) * QB]
    middle = x_ref[...].astype(F32) + dot(mixed_ref[...], w_ref[...])
    middle_ref[...] = middle.astype(BF)
    n, _ = normalize(middle)
    n2_ref[...] = (n * gain_ref[1:2, :]).astype(BF)


def attend_call(info, q, k, v, x, w_parts, gain, deps=()):
    n = x.shape[0]
    ext = q.shape[0]
    groups = D // QUAD
    return call(
        attend_body,
        [info, q, k, v, x, *w_parts, gain],
        grid=(n // TILE,),
        in_specs=[smem()] + [full((ext, D))] * 3 + [rows(TILE, D)] + [full((D // 4, D))] * 4 + [full((8, D))],
        out_specs=[rows(TILE, D)] * 3 + [full((D, D)), pl.BlockSpec((groups, 4, TILE), lambda i: (0, 0, i))],
        out_shape=[
            jax.ShapeDtypeStruct((n, D), BF), jax.ShapeDtypeStruct((n, D), BF), jax.ShapeDtypeStruct((n, D), BF),
            jax.ShapeDtypeStruct((D, D), BF), jax.ShapeDtypeStruct((groups, 4, n), F32),
        ],
        megabytes=12,
        deps=deps,
        cost_estimate=cost(11),
        name="attend",
    )


def hidden(n2, cot, wg, wu, wd):
    gate = dot(n2, wg)
    up = dot(n2, wu)
    ga = dot_bt(cot, wd)
    phi = 0.5 + 0.5 * lax.erf(gate * (2.0**-0.5))
    gelu = gate * phi
    act = (gelu * up).astype(BF)
    slope = phi + gate * (jnp.exp(-0.5 * gate * gate) * 0.3989422804014327)
    dgate = (ga * up * slope).astype(BF)
    dup = (ga * gelu).astype(BF)
    out = dot(act, wd)
    gn = dot_bt(dgate, wg) + dot_bt(dup, wu)
    return act, dgate, dup, out, gn


def ffn_a_body(info_ref, n2_ref, cot_ref, ga, gb, gc, gd, ge, gf, ua, ub, uc, ud, oa, ob, oc, od,
               out_ref, gn_ref, keep_ref, send_ref, wg_ref, wu_ref, wd_ref, acc, ad):
    i = pl.program_id(0)

    @pl.when(i == 0)
    def _():
        lay(info_ref[0], (ga, gb, (gc, gd), (ge, gf)), wg_ref, info_ref[1] & 1)
        lay(info_ref[0], (ua, ub, uc, ud), wu_ref)
        lay(info_ref[0], (oa, ob, oc, od), wd_ref)
        acc[...] = jnp.zeros_like(acc)
        ad[...] = jnp.zeros_like(ad)

    n2 = n2_ref[...]
    cot = cot_ref[...]
    nt = n2.T
    total_out = jnp.zeros((TILE, D), F32)
    total_gn = jnp.zeros((TILE, D), F32)
    for h in range(2):
        g, u = slice(h * WIDE, (h + 1) * WIDE), slice(D + h * WIDE, D + (h + 1) * WIDE)
        act, dgate, dup, out, gn = hidden(n2, cot, wg_ref[:, g], wu_ref[:, g], wd_ref[g, :])
        total_out += out
        total_gn += gn
        acc[:, g] += dot(nt, dgate)
        acc[:, u] += dot(nt, dup)
        ad[g, :] += dot_at(act, cot)
    out_ref[...] = total_out.astype(BF)
    gn_ref[...] = total_gn.astype(BF)

    @pl.when(i == pl.num_programs(0) - 1)
    def _():
        for b in range(4):
            deal(info_ref[0], acc, slice(b * WIDE, (b + 1) * WIDE), keep_ref, send_ref, b * D // 4)
        for b in range(2):
            deal(info_ref[0], ad, slice(b * WIDE, (b + 1) * WIDE), keep_ref, send_ref, (4 + b) * D // 4)


def ffn_a_call(info, n2, cot, gate_parts, up_parts, down_parts, deps=()):
    n = n2.shape[0]
    part = jax.ShapeDtypeStruct((n, D), BF)
    size = 6 * D // 4
    return call(
        ffn_a_body,
        [info, n2, cot, *gate_parts, *up_parts, *down_parts],
        grid=(n // TILE,),
        in_specs=[smem()] + [rows(TILE, D)] * 2 + [full((D // 4, D))] * 2 + [full((D // 8, D))] * 4
        + [full((D // 4, D))] * 8,
        out_specs=[rows(TILE, D)] * 2 + [full((2, size, WIDE))] * 2,
        out_shape=[part, part, piece(size), piece(size)],
        scratch_shapes=[pltpu.VMEM((D, D), BF)] * 3 + [pltpu.VMEM((D, 2 * D), F32), pltpu.VMEM((D, D), F32)],
        megabytes=24,
        deps=deps,
        cost_estimate=cost(18),
        name="ffn_a",
    )


def norm_back(grad, n, r, gain):
    e = grad * gain
    return r * (e - jnp.mean(e, axis=-1, keepdims=True) - n * jnp.mean(e * n, axis=-1, keepdims=True))


def ffn_b_body(info_ref, n2_ref, cot_ref, ia, ib, ic, id_, oa, ob, oc, od, pout_ref, pgn_ref, mid_ref, mixed_ref, wo_ref, gain_ref,
               out_ref, gmid_ref, gmix_ref, keep_ref, send_ref, w_ref, wd_ref, acc, ad, ao):
    i = pl.program_id(0)

    @pl.when(i == 0)
    def _():
        lay(info_ref[0], (ia, ib, ic, id_), w_ref)
        lay(info_ref[0], (oa, ob, oc, od), wd_ref)
        acc[...] = jnp.zeros_like(acc)
        ao[...] = jnp.zeros_like(ao)
        ad[...] = jnp.zeros_like(ad)

    n2 = n2_ref[...]
    cot = cot_ref[...]
    act, dgate, dup, out, gn = hidden(n2, cot, w_ref[:, :WIDE], w_ref[:, WIDE:], wd_ref[...])
    nt = n2.T
    acc[:, :WIDE] += dot(nt, dgate)
    acc[:, WIDE:] += dot(nt, dup)
    ad[...] += dot_at(act, cot)
    middle = mid_ref[...].astype(F32)
    out_ref[...] = (middle + pout_ref[...].astype(F32) + out).astype(BF)
    n, r = normalize(middle)
    branch = (cot.astype(F32) + norm_back(pgn_ref[...].astype(F32) + gn, n, r, gain_ref[1:2, :])).astype(BF)
    gmid_ref[...] = branch
    gmix_ref[...] = dot_bt(branch, wo_ref[...]).astype(BF)
    ao[...] += dot_at(mixed_ref[...], branch)

    @pl.when(i == pl.num_programs(0) - 1)
    def _():
        w = info_ref[0]
        r = D // 4
        for b in range(2):
            cols = slice(b * WIDE, (b + 1) * WIDE)
            deal(w, acc, cols, keep_ref, send_ref, b * r)
            deal(w, ao, cols, keep_ref, send_ref, (2 + b) * r)
            deal(w, ad, cols, keep_ref, send_ref, 4 * r + b * r // 2)


def ffn_b_call(info, n2, cot, in_parts, down_parts, pout, pgn, middle, mixed, wo, gain, deps=()):
    n = n2.shape[0]
    size = 5 * D // 4
    return call(
        ffn_b_body,
        [info, n2, cot, *in_parts, *down_parts, pout, pgn, middle, mixed, wo, gain],
        grid=(n // TILE,),
        in_specs=[smem()] + [rows(TILE, D)] * 2 + [full((D // 4, D))] * 4 + [full((WIDE // 4, D))] * 4
        + [rows(TILE, D)] * 4 + [full((D, D)), full((8, D))],
        out_specs=[rows(TILE, D)] * 3 + [full((2, size, WIDE))] * 2,
        out_shape=[jax.ShapeDtypeStruct((n, D), BF)] * 3 + [piece(size), piece(size)],
        scratch_shapes=[pltpu.VMEM((D, D), BF), pltpu.VMEM((WIDE, D), BF),
                        pltpu.VMEM((D, D), F32), pltpu.VMEM((WIDE, D), F32), pltpu.VMEM((D, D), F32)],
        megabytes=24,
        deps=deps,
        cost_estimate=cost(14),
        name="ffn_b",
    )


def attend_back_body(info_ref, q_ref, k_ref, v_ref, g_ref, mixed_ref, lse_ref, cos_ref, sin_ref, nt_ref, *rest):
    dq_ref, dk_ref, dv_ref, keep_ref, send_ref, ak, av, aw = rest[-8:]
    ext = ak.shape[0]
    blocks = (ext - 2 * HALF) // QB
    left, right = sides(info_ref)
    ak[...] = jnp.zeros_like(ak)
    av[...] = jnp.zeros_like(av)
    zero = jnp.zeros((HALF, QUAD), BF)
    dq_ref[:HALF, :] = zero
    dq_ref[ext - HALF :, :] = zero
    prod = mixed_ref[...].astype(F32) * g_ref[...].astype(F32)
    head = lax.broadcasted_iota(jnp.int32, (8, QUAD), 1) // HD
    pick = jnp.where(head == lax.broadcasted_iota(jnp.int32, (8, QUAD), 0), 1.0, 0.0).astype(BF)
    high = prod.astype(BF)
    delta = dot_bt(pick, high) + dot_bt(pick, (prod - high.astype(F32)).astype(BF))

    def of_heads(a, start):
        return jnp.concatenate([a[h : h + 1, start : start + QB] for h in range(4)], axis=1)

    def unturn(u, at):
        cos = cos_ref[at, :]
        sl, sr = signed(-sin_ref[at, :])
        return jnp.concatenate([turn(u[:, c : c + PAIR], cos, sl, sr) for c in (0, PAIR)], axis=1).astype(BF)

    for b in range(blocks):
        start = b * QB
        win = slice(start, start + QB + 2 * HALF)
        here = slice(start + HALF, start + HALF + QB)
        bias = repeat(bias_of(b, blocks - 1, left, right))
        q4 = apart(q_ref[here, :])
        g4 = apart(g_ref[start : start + QB, :])
        kw = k_ref[win, :]
        probs = jnp.exp(dot_bt(kw, q4) + bias - of_heads(lse_ref[0], start))
        ds = (probs * (dot_bt(v_ref[win, :], g4) - of_heads(delta, start))).astype(BF)
        ak[win, :] += dot(ds, q4)
        av[win, :] += dot(probs.astype(BF), g4)
        dq_ref[here, :] = unturn(together(dot_at(ds, kw)) * HD**-0.5, here)
    dk_ref[...] = unturn(ak[...], slice(0, ext))
    dv_ref[...] = av[...].astype(BF)
    for part, ref in enumerate((dq_ref, dk_ref, dv_ref)):
        aw[...] = dot(nt_ref[...], ref[...])
        deal(info_ref[0], aw, slice(0, QUAD), keep_ref, send_ref, part * D // 4)


def attend_back_call(p, at, width, info, q, k, v, g, mixed, lse, cos, sin, nt, sofar, pieces, deps=()):
    n = g.shape[0]
    ext = q.shape[0]
    cols = pl.BlockSpec((ext, QUAD), lambda i: (0, p))
    inner = pl.BlockSpec((n, QUAD), lambda i: (0, p))
    own = jax.ShapeDtypeStruct((ext, D), BF)
    out = jax.ShapeDtypeStruct((2, 3 * D // 4, width), BF)
    args = [info, q, k, v, g, mixed, lse, cos, sin, nt]
    extra = list(sofar) + list(pieces)
    aliases = {}
    for i in range(len(sofar)):
        aliases[len(args) + i] = i
    for i in range(len(pieces)):
        aliases[len(args) + len(sofar) + i] = 3 + i
    mine = pl.BlockSpec((2, 3 * D // 4, QUAD), lambda i: (0, 0, at))
    return call(
        attend_back_body,
        args + extra,
        grid=(1,),
        in_specs=[smem(), cols, cols, cols, inner, inner, pl.BlockSpec((1, 4, n), lambda i: (p, 0, 0))]
        + [full((ext, PAIR))] * 2 + [full((D, ext))] + [pl.BlockSpec(memory_space=pl.ANY)] * len(extra),
        out_specs=[cols] * 3 + [mine] * 2,
        out_shape=[own, own, own, out, out],
        scratch_shapes=[pltpu.VMEM((ext, QUAD), F32), pltpu.VMEM((ext, QUAD), F32), pltpu.VMEM((D, QUAD), F32)],
        aliases=aliases,
        megabytes=12,
        deps=deps,
        cost_estimate=cost(4),
        name="attend_back",
    )


def last_body(info_ref, x_ref, dq_ref, dk_ref, dv_ref, rim_low, rim_high, gmid_ref, wa, wb, wc, wd, gain_ref, gin_ref, w_ref, *both):
    i = pl.program_id(0)
    start = pl.multiple_of(i * TILE, TILE)
    here = pl.ds(start + HALF, TILE)
    ext = dk_ref.shape[0]

    @pl.when(i == 0)
    def _():
        lay(info_ref[0], (wa, wb, wc, wd), w_ref)
        for j, ref in enumerate((dk_ref, dv_ref)):
            cols = slice(j * D, (j + 1) * D)
            both[j][...] = ref[...]
            both[j][HALF : 2 * HALF, :] += rim_low[:, cols]
            both[j][ext - 2 * HALF : ext - HALF, :] += rim_high[:, cols]

    total = jnp.zeros((TILE, D), F32)
    for j, ref in enumerate((dq_ref, *both)):
        total += dot_bt(ref[here, :], w_ref[:, j * D : (j + 1) * D])
    n, r = normalize(x_ref[...].astype(F32))
    gin_ref[...] = (gmid_ref[...].astype(F32) + norm_back(total, n, r, gain_ref[0:1, :])).astype(BF)


def last_call(info, x, grads, rims, gmid, w_parts, gain, deps=()):
    n = gmid.shape[0]
    ext = grads[0].shape[0]
    return call(
        last_body,
        [info, x, *grads, *rims, gmid, *w_parts, gain],
        grid=(n // TILE,),
        in_specs=[smem(), rows(TILE, D)] + [full((ext, D))] * 3 + [full((HALF, 2 * D))] * 2 + [rows(TILE, D)]
        + [full((D // 4, 3 * D))] * 4 + [full((8, D))],
        out_specs=[rows(TILE, D)],
        out_shape=[jax.ShapeDtypeStruct((n, D), BF)],
        scratch_shapes=[pltpu.VMEM((D, 3 * D), BF)] + [pltpu.VMEM((ext, D), BF)] * 2,
        megabytes=16,
        deps=deps,
        cost_estimate=cost(7),
        name="last",
    )


def adam(weight, grad, first_old, second, decay_rate):
    new_first = BETA_ONE * first_old + (1.0 - BETA_ONE) * grad
    new_second = BETA_TWO * second + (1.0 - BETA_TWO) * grad * grad
    root = jnp.sqrt(new_second * (1.0 / (1.0 - BETA_TWO**STEP))) + ADAM_EPS
    change = (-LEARN_RATE / (1.0 - BETA_ONE**STEP)) * (new_first / root)
    if decay_rate:
        change = change - (LEARN_RATE * decay_rate) * weight
    return (new_first, new_second, change)


def adam_body(count, *refs):
    grads, (w_ref, m_ref, v_ref, g_ref, nm_ref, nv_ref, st_ref, dots_ref) = refs[:count], refs[count:]
    g = jnp.concatenate([r[...] for r in grads], axis=1).astype(F32)
    w = w_ref[...].astype(F32)
    g_ref[...] = g
    nm_ref[...], nv_ref[...], st_ref[...] = adam(w, g, m_ref[...], v_ref[...], WEIGHT_DECAY)

    @pl.when(pl.program_id(0) == 0)
    def _():
        dots_ref[...] = jnp.zeros_like(dots_ref)

    dots_ref[...] += jnp.sum(w * g, axis=1, keepdims=True)


def adam_call(grads, weight, first, second, megabytes=60):
    r, width = weight.shape
    own = pl.BlockSpec((r, D), lambda j: (0, j))
    out = jax.ShapeDtypeStruct((r, width), F32)
    return pl.pallas_call(
        functools.partial(adam_body, len(grads)),
        grid=(width // D,),
        in_specs=[pl.BlockSpec((r, wide), at) for _, wide, at in grads] + [own] * 3,
        out_specs=[own] * 4 + [full((r, 1))],
        out_shape=[out] * 4 + [jax.ShapeDtypeStruct((r, 1), F32)],
        compiler_params=pltpu.CompilerParams(dimension_semantics=("arbitrary",), vmem_limit_bytes=megabytes * 1024 * 1024),
        cost_estimate=cost(3),
        name="adam",
    )(*[g for g, _, _ in grads], weight, first, second)


CORES = [(0, 1), (1, 0), (2, 3), (3, 2)]
CHIPS = [(0, 2), (2, 0), (1, 3), (3, 1)]


def to_core(a):
    return lax.ppermute(a, "wshard", CORES)


def to_chip(a):
    return lax.ppermute(a, "wshard", CHIPS)


def copy_body(*refs):
    for a, b in zip(refs[: len(refs) // 2], refs[len(refs) // 2 :]):
        b[...] = a[...]


def copies(arrays):
    return pl.pallas_call(
        copy_body,
        grid=(1,),
        in_specs=[full(a.shape) for a in arrays],
        out_specs=[full(a.shape) for a in arrays],
        out_shape=[jax.ShapeDtypeStruct(a.shape, a.dtype) for a in arrays],
        compiler_params=pltpu.CompilerParams(vmem_limit_bytes=8 * 1024 * 1024),
        name="copies",
    )(*arrays)


def after(a, first):
    return together_at([a, first])[0]


class Chain:
    def __init__(self, keep, send):
        count = lax.axis_size("seq")
        whole = []
        shift = 2
        while 1 << shift < count:
            whole.append(("whole", shift))
            shift += 1
        self.plan = [("core", 0), ("one", 0), ("two", 0), ("half", 1)] + whole + [("back", 1), ("end", 0)]
        self.at = 0
        self.kept = [keep]
        self.sends = [send]
        self.rows, self.columns = keep.shape[1:]

    def done(self):
        return self.at == len(self.plan)

    def start(self):
        if self.done():
            return
        kind, shift = self.plan[self.at]

        def along_seq(a):
            count = lax.axis_size("seq")
            return lax.ppermute(a, "seq", [(i, i ^ (1 << shift)) for i in range(count)])

        if kind == "core":
            ways = [to_core]
        elif kind == "one":
            ways = [to_chip, along_seq]
        elif kind == "two":
            ways = [along_seq, to_chip]
        else:
            ways = [along_seq]
        self.flights = [way(a) for way, a in zip(ways, self.sends)]

    def landing(self):
        kind, _ = self.plan[self.at]
        q, c = self.rows // 4, self.columns
        shapes = {
            "core": [(2 * q, c), (2, q, c)] * 2, "one": [(q, c)] * 4, "two": [(q, c)] * 2,
            "half": [(q, c)], "whole": [(q, c)], "back": [(2 * q, c)], "end": [(4 * q, c)],
        }[kind]

        def body(info_ref, ins, outs):
            bx, by, bz = (info_ref[0] >> 1) & 1, info_ref[1] & 1, (info_ref[1] >> 1) & 1

            def at(i, base=0):
                return pl.ds(pl.multiple_of(base + i * q, 16), q)

            if kind == "core":
                keep, got = ins
                for out, i in ((outs[0], bx), (outs[2], 1 - bx)):
                    out[...] = sum_of(keep[i, : 2 * q, :], got[i, : 2 * q, :])
                for out, i in ((outs[1], by), (outs[3], 1 - by)):
                    out[...] = sum_of(keep[:, at(i, 2 * q), :], got[:, at(i, 2 * q), :])
            elif kind == "one":
                for out, i in ((outs[0], by), (outs[2], 1 - by)):
                    out[...] = sum_of(ins[0][at(i), :], ins[2][at(i), :])
                for out, i in ((outs[1], bx), (outs[3], 1 - bx)):
                    out[...] = sum_of(ins[1][i], ins[3][i])
            elif kind == "two":
                first = sum_of(ins[0][...], ins[2][...])
                second = sum_of(ins[1][...], ins[3][...])
                put_by(bz, outs, first, second, slice(0, c))
            elif kind == "back":
                outs[0][at(bz), :] = ins[0][...]
                outs[0][at(1 - bz), :] = ins[1][...]
            elif kind == "end":
                for half in range(2):
                    outs[0][at(by, 2 * q * half), :] = ins[0][half * q : (half + 1) * q, :]
                    outs[0][at(1 - by, 2 * q * half), :] = ins[1][half * q : (half + 1) * q, :]
            else:
                outs[0][...] = sum_of(ins[0][...], ins[1][...])

        return self.kept + self.flights, shapes, body

    def landed(self, outs):
        kind, _ = self.plan[self.at]
        self.at += 1
        pairs = {"core": 2, "one": 2, "two": 1}.get(kind)
        self.kept = outs[:pairs] if pairs else outs
        self.sends = outs[pairs:] if pairs else outs


def put_by(bit, outs, first, second, cols):
    @pl.when(bit == 0)
    def _():
        outs[0][:, cols] = first
        outs[1][:, cols] = second

    @pl.when(bit != 0)
    def _():
        outs[0][:, cols] = second
        outs[1][:, cols] = first


class Joined(Chain):
    def __init__(self, first, second):
        self.both = (first, second)
        self.plan, self.at, self.rows = second.plan, second.at, second.rows
        self.columns = first.columns + second.columns

    def landing(self):
        if self.both is None:
            return Chain.landing(self)
        plans = [c.landing() for c in self.both]
        q = self.rows // 4

        def body(info_ref, ins, outs):
            bz = (info_ref[1] >> 1) & 1
            start = 0
            for i, c in enumerate(self.widths):
                a = ins[4 * i : 4 * i + 4]
                first = sum_of(a[0][...], a[2][...])
                second = sum_of(a[1][...], a[3][...])
                put_by(bz, outs, first, second, slice(start, start + c))
                start += c

        self.widths = [c.columns for c in self.both]
        return plans[0][0] + plans[1][0], [(q, self.columns)] * 2, body

    def landed(self, outs):
        self.both = None
        Chain.landed(self, outs)


def sum_of(a, b):
    return (a.astype(F32) + b.astype(F32)).astype(BF)


def nothing(*refs):
    pass


def together_at(arrays, seen=()):
    hbm = pl.BlockSpec(memory_space=pl.ANY)
    return pl.pallas_call(
        nothing,
        in_specs=[hbm] * (len(arrays) + len(seen)),
        out_specs=[hbm] * len(arrays),
        out_shape=[jax.ShapeDtypeStruct(a.shape, a.dtype) for a in arrays],
        input_output_aliases={i: i for i in range(len(arrays))},
        compiler_params=pltpu.CompilerParams(vmem_limit_bytes=1024 * 1024),
        name="boundary",
    )(*arrays, *seen)


def boundary(info, token, landing=(), starting=(), also=()):
    landing = [c for c in landing if not c.done()]
    plans = [c.landing() for c in landing]
    args = [info] + [a for p in plans for a in p[0]]
    through = [c.sends[0] for c in starting] + list(also) + [token]
    shapes = [jax.ShapeDtypeStruct(t, BF) for p in plans for t in p[1]]
    count = len(args)

    def body(*refs):
        ins = list(refs[1:count])
        outs = list(refs[count + len(through) :])
        for operands, shapes_i, land in plans:
            land(refs[0], [ins.pop(0) for _ in operands], [outs.pop(0) for _ in shapes_i])

    hbm = pl.BlockSpec(memory_space=pl.ANY)
    outs = pl.pallas_call(
        body,
        grid=(1,),
        in_specs=[smem()] + [full(a.shape) for a in args[1:]] + [hbm] * len(through),
        out_specs=[full(t.shape) for t in shapes] + [hbm] * len(through),
        out_shape=shapes + [jax.ShapeDtypeStruct(a.shape, a.dtype) for a in through],
        input_output_aliases={count + i: len(shapes) + i for i in range(len(through))},
        compiler_params=pltpu.CompilerParams(vmem_limit_bytes=16 * 1024 * 1024),
        cost_estimate=cost(1),
        name="land",
    )(*args, *through)
    outs = list(outs)
    for c, p in zip(landing, plans):
        c.landed([outs.pop(0) for _ in p[1]])
    for c in starting:
        c.sends = [outs.pop(0)]
    waits = [outs[-1]]
    for c in landing + list(starting):
        waits.append(c.sends[0])
        c.start()
    return outs[:-1], tuple(waits)


def neighbours(count):
    up = [(i, i + 1) for i in range(count - 1)]
    return up, [(j, i) for i, j in up]


def shards(
    hidden_in, cotangent, block_seq, block_place, attn_in, attn_out, ffn_in, ffn_out, norm_attn, norm_ffn,
    m_attn_in, m_attn_out, m_ffn_in, m_ffn_out, m_norm_attn, m_norm_ffn,
    v_attn_in, v_attn_out, v_ffn_in, v_ffn_out, v_norm_attn, v_norm_ffn,
):
    x = hidden_in[0]
    cot = cotangent[0]
    n = x.shape[0]
    ext = n + 2 * HALF
    w = lax.axis_index("wshard")
    count = lax.axis_size("seq")
    at = lax.axis_index("seq")
    up, down = neighbours(count)

    far = to_chip(attn_in)
    mate = to_core(attn_in)
    gain_own = jnp.stack([norm_attn, norm_ffn])
    gain_far, gain_mate = to_chip(gain_own), to_core(gain_own)
    x_low, x_high = lax.ppermute(x[n - HALF :], "seq", up), lax.ppermute(x[:HALF], "seq", down)
    attn_out_own, down_a, down_b = copies([attn_out, ffn_out[: D // 4], ffn_out[D // 4 :]])
    info = jnp.concatenate([jnp.stack([w, at]).astype(jnp.int32), block_seq[0], block_place[0]])
    some, rest = D // 4, FF // 4 - D // 4

    def units(start, first, size):
        return [ffn_in[:, start + s * (FF // 4) + first :][:, :size] for s in range(4)]

    in_g = jnp.concatenate(units(0, 0, some), axis=1)
    in_u = jnp.concatenate(units(FF, 0, some), axis=1)
    in_b = jnp.concatenate(units(0, some, rest) + units(FF, some, rest), axis=1)
    out_mate, g_mate, u_mate, da_mate, db_mate, b_mate = (to_core(a) for a in (attn_out_own, in_g, in_u, down_a, down_b, in_b))

    g_half = lax.dynamic_slice_in_dim(in_g, (at & 1) * (D // 8), D // 8, 0)
    (token,) = together_at(
        [jnp.zeros((8, 128), F32)], [x_low, x_high, info, mate, out_mate, g_mate, u_mate, da_mate, db_mate, b_mate]
    )
    far, g_half, attn_out_own, token = together_at([far, g_half, attn_out_own, token], [gain_far, gain_mate])
    farmate = to_core(far)
    out_far = to_chip(attn_out_own)
    g_mine = to_chip(g_half)
    attn_parts = attn_in, mate, far, farmate
    gains = gain_own, gain_mate, gain_far, to_core(gain_far)
    nt, q, k, v, cos, sin, gain, token = qkv_call(info, x, x_low, x_high, gains, attn_parts)
    out_far, g_mine, in_u, token = together_at([out_far, g_mine, in_u, token])
    out_farmate = to_core(out_far)
    out_farmate, in_u, down_a, token = together_at([out_farmate, in_u, down_a, token])
    u_far = to_chip(in_u)
    da_far = to_chip(down_a)
    g_other = lax.ppermute(g_mine, "seq", [(i, i ^ 1) for i in range(count)])
    out_parts = attn_out, out_mate, out_far, out_farmate
    mixed, middle, n2, out_w, lse, token = attend_call(info, q, k, v, x, out_parts, gain, deps=(token,))
    g_other, u_far, da_far, in_b, down_b, token = together_at([g_other, u_far, da_far, in_b, down_b, token])
    b_far = to_chip(in_b)
    db_far = to_chip(down_b)
    gate_parts = in_g, g_mate, g_mine, g_other, to_core(g_mine), to_core(g_other)
    up_parts = in_u, u_mate, u_far, to_core(u_far)
    down_parts = down_a, da_mate, da_far, to_core(da_far)
    pout, pgn, keep, send, token = ffn_a_call(info, n2, cot, gate_parts, up_parts, down_parts, deps=(token,))
    chain_a = Chain(keep, send)
    (b_far, db_far), deps = boundary(info, token, (), (chain_a,), (b_far, db_far))
    b_parts = in_b, b_mate, b_far, to_core(b_far)
    db_parts = down_b, db_mate, db_far, to_core(db_far)
    _, deps = boundary(info, deps[0], (chain_a,))
    block_out, gmid, gmix, keep, send, token = ffn_b_call(
        info, n2, cot, b_parts, db_parts, pout, pgn, middle, mixed, out_w, gain, deps=deps
    )
    chain_b = Chain(keep, send)
    grads, pieces = (), ()

    def back(p, at, width, deps):
        nonlocal grads, pieces
        if at == 0:
            pieces = ()
        out = attend_back_call(p, at, width, info, q, k, v, gmix, mixed, lse, cos, sin, nt, grads, pieces, deps)
        grads, pieces = out[:3], out[3:5]
        return out[5]

    _, deps = boundary(info, token, (chain_a,), (chain_b,))
    token = back(0, 0, 2 * QUAD, deps)
    _, deps = boundary(info, token, (chain_a, chain_b))
    token = back(1, 1, 2 * QUAD, deps)
    chain_c = Chain(*pieces)
    _, deps = boundary(info, token, (chain_a, chain_b), (chain_c,))
    token = back(2, 0, QUAD, deps)
    chain_d = Chain(*pieces)
    _, deps = boundary(info, token, (chain_a, chain_b, chain_c), (chain_d,))
    rims = [jnp.concatenate([a[r] for a in grads[1:]], axis=1) for r in (slice(0, HALF), slice(n + HALF, ext))]
    rims, deps = boundary(info, deps[0], (chain_b, chain_c, chain_d), (), rims)
    rims = lax.ppermute(rims[1], "seq", up), lax.ppermute(rims[0], "seq", down)
    rims, deps = boundary(info, deps[0], (chain_a, chain_b, chain_d), (), rims)
    grad_in, token = last_call(info, x, grads, rims, gmid, attn_parts, gain, deps=deps)
    chains = (chain_a, chain_b, Joined(chain_c, chain_d))
    sum_b = late_b = sum_a = None
    while not all(c.done() for c in chains):
        also = ()
        if chain_a.done() and chain_b.done():
            also = (chain_b.kept[0], chain_a.kept[0])
        through, deps = boundary(info, token, chains, (), also)
        token = deps[0]
        if also:
            chain_b.kept, chain_a.kept = through[:1], through[1:2]
            sum_b = through[0] if sum_b is None else sum_b
            if not chains[2].done():
                late_b, sum_a = through
    sum_c = chains[2].kept[0]

    r = D // 4

    def blocks(a, *at):
        return jnp.concatenate([a[i * r : (i + 1) * r] for i in at], axis=1)

    ga, gb = blocks(sum_a, 0, 1), late_b[:r]
    ua, ub = blocks(sum_a, 2, 3), late_b[r : 2 * r]
    g_ffn_in = jnp.concatenate(
        [t for a, b in ((ga, gb), (ua, ub)) for s in range(4)
         for t in (a[:, s * some : (s + 1) * some], b[:, s * rest : (s + 1) * rest])], axis=1
    )
    g_ffn_out = jnp.concatenate(
        [blocks(sum_a, 4, 5), jnp.concatenate([sum_b[4 * r : 4 * r + rest], sum_b[4 * r + rest :]], axis=1)], axis=0
    )
    res_ffn_in = adam_call([(g_ffn_in, D, lambda j: (0, j))], ffn_in, m_ffn_in, v_ffn_in)
    res_attn_out = adam_call([(blocks(sum_b, 2, 3), D, lambda j: (0, j))], attn_out, m_attn_out, v_attn_out)
    res_ffn_out = adam_call([(g_ffn_out, D, lambda j: (0, j))], ffn_out, m_ffn_out, v_ffn_out)
    res_attn_in = adam_call([(sum_c, D, lambda j: (j, 0))], attn_in, m_attn_in, v_attn_in, 20)
    results = [res_attn_in, res_attn_out, res_ffn_in, res_ffn_out]
    for res, own_gain, m, v_ in ((res_attn_in, norm_attn, m_norm_attn, v_norm_attn), (res_ffn_in, norm_ffn, m_norm_ffn, v_norm_ffn)):
        wide = own_gain.astype(F32)
        g = res[4][:, 0] / wide
        results.append((g,) + adam(wide, g, m, v_, 0.0))
    return (block_out[None], grad_in[None]) + tuple(res[i] for i in range(4) for res in results)


def solution(mesh):
    big = P("wshard", "seq", None)
    mat = P("wshard", None)
    vec = P("wshard")
    group = (mat, mat, mat, mat, vec, vec)
    in_specs = (big, big, mat, mat) + group * 3
    out_specs = (big, big) + group * 4
    return jax.shard_map(shards, mesh=mesh, in_specs=in_specs, out_specs=out_specs, check_vma=False)
```

```python
import functools

import jax
import jax.numpy as jnp
import numpy as np
from jax import lax
from jax.experimental import pallas as pl
from jax.experimental.pallas import tpu as pltpu
from jax.sharding import PartitionSpec as P

D = 768
FF = 1152
HEADS = 12
HD = 64
HALF = 64
STEP = 10
PAIR = 2 * HD
QB = 128
TILE = 256
WIDE = 384
ADAM_MB = 60
QUAD = 4 * HD

NORM_EPS = 1e-05
BETA_ONE = 0.9
BETA_TWO = 0.98
LEARN_RATE = 0.05
WEIGHT_DECAY = 0.01
ADAM_EPS = 1e-06
NEG_FILL = -1e30
THETA = 10000.0
BF = jnp.bfloat16
F32 = jnp.float32


def dot(left, right):
    return lax.dot_general(left, right, (((1,), (0,)), ((), ())), preferred_element_type=F32)


def dot_bt(left, right):
    return lax.dot_general(left, right, (((1,), (1,)), ((), ())), preferred_element_type=F32)


def dot_at(left, right):
    return lax.dot_general(left, right, (((0,), (0,)), ((), ())), preferred_element_type=F32)


def call(body, args, in_specs, out_specs, out_shape, megabytes, deps=(), aliases=None, **kw):
    first = len(args)
    n_out = len(out_shape)

    def wrapped(*refs):
        refs = refs[:first] + refs[first + len(deps) :]
        token = refs[first + n_out]
        token[...] = jnp.zeros_like(token)
        body(*refs[: first + n_out], *refs[first + n_out + 1 :])

    return pl.pallas_call(
        wrapped,
        in_specs=list(in_specs) + [pl.BlockSpec(memory_space=pl.ANY)] * len(deps),
        out_specs=list(out_specs) + [full((8, 128))],
        out_shape=list(out_shape) + [jax.ShapeDtypeStruct((8, 128), F32)],
        input_output_aliases=aliases or {},
        compiler_params=pltpu.CompilerParams(
            dimension_semantics=("arbitrary",), vmem_limit_bytes=megabytes * 1024 * 1024
        ),
        **kw,
    )(*args, *deps)


def full(shape):
    return pl.BlockSpec(shape, lambda i: (0,) * len(shape))


def rows(tile, width):
    return pl.BlockSpec((tile, width), lambda i: (i, 0))


def cost(microseconds):
    return pl.CostEstimate(flops=int(microseconds * 1.1e9), bytes_accessed=0, transcendentals=0)


def normalize(x):
    mean = jnp.mean(x, axis=-1, keepdims=True)
    centered = x - mean
    var = jnp.mean(centered * centered, axis=-1, keepdims=True)
    r = lax.rsqrt(var + NORM_EPS)
    return centered * r, r


def signed(sin):
    first = lax.broadcasted_iota(jnp.int32, sin.shape, 1) % HD < HD // 2
    zero = jnp.zeros_like(sin)
    return jnp.where(first, -sin, zero), jnp.where(first, zero, sin)


def turn(u, cos, sin_left, sin_right):
    return u * cos + pltpu.roll(u, PAIR - HD // 2, 1) * sin_left + pltpu.roll(u, HD // 2, 1) * sin_right


def blocks_of(info_ref):
    return (info_ref.shape[0] - 2) // 2


def sides(info_ref):
    count = blocks_of(info_ref)
    at = info_ref[1]
    own = info_ref[2 + at]
    left = (at > 0) & (info_ref[2 + jnp.maximum(at - 1, 0)] == own)
    right = (at < count - 1) & (info_ref[2 + jnp.minimum(at + 1, count - 1)] == own)
    return left, right


def bias_of(b, last, left, right):
    shape = (QB + 2 * HALF, QB)
    key = lax.broadcasted_iota(jnp.int32, shape, 0)
    off = key - lax.broadcasted_iota(jnp.int32, shape, 1)
    low = jnp.where((b > 0) | left, 0, HALF)
    high = jnp.where((b < last) | right, QB + 2 * HALF, QB + HALF)
    ok = (off >= 0) & (off <= 2 * HALF) & (key >= low) & (key < high)
    return jnp.where(ok, 0.0, NEG_FILL)


def lay(w, parts, out_ref, bit=0):
    r = out_ref.shape[0] // 4
    for i, ref in enumerate(parts):
        start = (w ^ i) * r
        if isinstance(ref, tuple):
            half = r // 2
            for j, a in enumerate(ref):
                out_ref[pl.ds(pl.multiple_of(start + (bit ^ j) * half, 16), half), :] = a[...]
        else:
            out_ref[pl.ds(pl.multiple_of(start, 32), r), :] = ref[...]


def deal(w, acc, cols, keep_ref, send_ref, at):
    r = acc.shape[0] // 4
    c = w & 1
    for x in range(2):
        keep_ref[x, at : at + r, :] = acc[pl.ds(pl.multiple_of((2 * x + c) * r, 32), r), cols].astype(BF)
        send_ref[x, at : at + r, :] = acc[pl.ds(pl.multiple_of((2 * x + 1 - c) * r, 32), r), cols].astype(BF)


def smem():
    return pl.BlockSpec(memory_space=pltpu.SMEM)


def piece(n_rows):
    return jax.ShapeDtypeStruct((2, n_rows, WIDE), BF)


def qkv_body(info_ref, x_ref, low_ref, high_ref, gain_a, gain_b, gain_c, gain_d, wa, wb, wc, wd, far_ref, near_ref,
             nt_ref, q_ref, k_ref, v_ref, cos_ref, sin_ref, gain_ref, w_ref, x_ext):
    t = q_ref.shape[0]
    i = pl.program_id(0)

    @pl.when(i == 0)
    def _():
        lay(info_ref[0], (wa, wb, wc, wd), w_ref)
        end = x_ext.shape[0] - HALF
        x_ext[:HALF, :] = low_ref[...]
        x_ext[HALF:end, :] = x_ref[...]
        x_ext[end:, :] = high_ref[...]
        r = D // 4
        for p, ref in enumerate((gain_a, gain_b, gain_c, gain_d)):
            gains = ref[...].astype(F32)
            for owner in range(4):

                @pl.when((info_ref[0] ^ p) == owner)
                def _():
                    gain_ref[:2, owner * r : (owner + 1) * r] = gains


    place = info_ref[2 + blocks_of(info_ref) + info_ref[1]]
    c2, s2 = far_ref[0, pl.ds(place, 1), :], far_ref[1, pl.ds(place, 1), :]
    c1, s1 = near_ref[0], near_ref[1]
    cos = c1 * c2 - s1 * s2
    sin = s1 * c2 + c1 * s2
    cos_ref[...] = cos
    sin_ref[...] = sin
    sl, sr = signed(sin)
    n, _ = normalize(x_ext[pl.ds(pl.multiple_of(i * t, 128), t), :].astype(F32))
    normed = (n * gain_ref[0:1, :]).astype(BF)
    nt_ref[...] = normed.T
    for part, ref, scale in ((0, q_ref, HD**-0.5), (1, k_ref, 1.0)):
        u = dot(normed, w_ref[:, part * D : (part + 1) * D])
        for p in range(D // PAIR):
            r = turn(u[:, p * PAIR : (p + 1) * PAIR], cos, sl, sr)
            ref[:, p * PAIR : (p + 1) * PAIR] = (r * scale).astype(BF)
    v_ref[...] = dot(normed, w_ref[:, 2 * D :]).astype(BF)


def angle_tables(n, ext):
    freq = THETA ** (-2.0 * (np.arange(PAIR) % (HD // 2)) / HD)

    def table(positions):
        angle = positions[:, None] * freq[None, :]
        return jnp.asarray(np.stack([np.cos(angle), np.sin(angle)]).astype(np.float32))

    return table(np.arange(4.0) * n), table(np.arange(float(ext)) - HALF)


def qkv_call(info, x, low, high, gains, w_parts, deps=()):
    n = x.shape[0]
    ext = n + 2 * HALF
    t = ext // 3
    out = jax.ShapeDtypeStruct((ext, D), BF)
    table = jax.ShapeDtypeStruct((ext, PAIR), F32)
    far, near = angle_tables(n, ext)
    return call(
        qkv_body,
        [info, x, low, high, *gains, *w_parts, far, near],
        grid=(3,),
        in_specs=[smem(), full((n, D)), full((HALF, D)), full((HALF, D))] + [full((2, D // 4))] * 4 + [full((D // 4, 3 * D))] * 4
        + [full(far.shape), pl.BlockSpec((2, t, PAIR), lambda i: (0, i, 0))],
        out_specs=[pl.BlockSpec((D, t), lambda i: (0, i))] + [rows(t, D)] * 3 + [rows(t, PAIR)] * 2 + [full((8, D))],
        out_shape=[jax.ShapeDtypeStruct((D, ext), BF)] + [out] * 3 + [table] * 2 + [jax.ShapeDtypeStruct((8, D), F32)],
        scratch_shapes=[pltpu.VMEM((D, 3 * D), BF), pltpu.VMEM((ext, D), BF)],
        megabytes=20,
        deps=deps,
        cost_estimate=cost(9),
        name="qkv",
    )


def apart(u):
    head = lax.broadcasted_iota(jnp.int32, u.shape, 1) // HD
    zero = jnp.zeros_like(u)
    return jnp.concatenate([jnp.where(head == h, u, zero) for h in range(4)], axis=0)


def together(u):
    r = u.shape[0] // 4
    head = lax.broadcasted_iota(jnp.int32, (r, QUAD), 1) // HD
    out = u[:r]
    for h in range(1, 4):
        out = jnp.where(head == h, u[h * r : (h + 1) * r], out)
    return out


def repeat(u):
    return jnp.concatenate([u] * 4, axis=1)


def attend_body(info_ref, q_ref, k_ref, v_ref, x_ref, wa, wb, wc, wd, gain_ref,
                mixed_ref, middle_ref, n2_ref, w_ref, lse_ref):
    i = pl.program_id(0)
    last = pl.num_programs(0) * (TILE // QB) - 1
    left, right = sides(info_ref)

    @pl.when(i == 0)
    def _():
        lay(info_ref[0], (wa, wb, wc, wd), w_ref)

    for s in range(TILE // QB):
        b = i * (TILE // QB) + s
        start = pl.multiple_of(b * QB, QB)
        bias = repeat(bias_of(b, last, left, right))
        for g in range(D // QUAD):
            cols = slice(g * QUAD, (g + 1) * QUAD)
            win = pl.ds(start, QB + 2 * HALF)
            q4 = apart(q_ref[pl.ds(start + HALF, QB), cols])
            scores = dot_bt(k_ref[win, cols], q4) + bias
            most = jnp.max(scores, axis=0, keepdims=True)
            e = jnp.exp(scores - most)
            total = jnp.sum(e, axis=0, keepdims=True)
            probs = (e * (1.0 / total)).astype(BF)
            o = together(dot_at(probs, v_ref[win, cols]))
            mixed_ref[s * QB : (s + 1) * QB, cols] = o.astype(BF)
            lse = most + jnp.log(total)
            for h in range(4):
                lse_ref[g, h : h + 1, s * QB : (s + 1) * QB] = lse[:, h * QB : (h + 1) * QB]
    middle = x_ref[...].astype(F32) + dot(mixed_ref[...], w_ref[...])
    middle_ref[...] = middle.astype(BF)
    n, _ = normalize(middle)
    n2_ref[...] = (n * gain_ref[1:2, :]).astype(BF)


def attend_call(info, q, k, v, x, w_parts, gain, deps=()):
    n = x.shape[0]
    ext = q.shape[0]
    groups = D // QUAD
    return call(
        attend_body,
        [info, q, k, v, x, *w_parts, gain],
        grid=(n // TILE,),
        in_specs=[smem()] + [full((ext, D))] * 3 + [rows(TILE, D)] + [full((D // 4, D))] * 4 + [full((8, D))],
        out_specs=[rows(TILE, D)] * 3 + [full((D, D)), pl.BlockSpec((groups, 4, TILE), lambda i: (0, 0, i))],
        out_shape=[
            jax.ShapeDtypeStruct((n, D), BF), jax.ShapeDtypeStruct((n, D), BF), jax.ShapeDtypeStruct((n, D), BF),
            jax.ShapeDtypeStruct((D, D), BF), jax.ShapeDtypeStruct((groups, 4, n), F32),
        ],
        megabytes=12,
        deps=deps,
        cost_estimate=cost(11),
        name="attend",
    )


def hidden(n2, cot, wg, wu, wd):
    gate = dot(n2, wg)
    up = dot(n2, wu)
    ga = dot_bt(cot, wd)
    phi = 0.5 + 0.5 * lax.erf(gate * (2.0**-0.5))
    gelu = gate * phi
    act = (gelu * up).astype(BF)
    slope = phi + gate * (jnp.exp(-0.5 * gate * gate) * 0.3989422804014327)
    dgate = (ga * up * slope).astype(BF)
    dup = (ga * gelu).astype(BF)
    out = dot(act, wd)
    gn = dot_bt(dgate, wg) + dot_bt(dup, wu)
    return act, dgate, dup, out, gn


def ffn_a_body(info_ref, n2_ref, cot_ref, ga, gb, gc, gd, ge, gf, ua, ub, uc, ud, oa, ob, oc, od,
               out_ref, gn_ref, keep_ref, send_ref, wg_ref, wu_ref, wd_ref, acc, ad):
    i = pl.program_id(0)

    @pl.when(i == 0)
    def _():
        lay(info_ref[0], (ga, gb, (gc, gd), (ge, gf)), wg_ref, info_ref[1] & 1)
        lay(info_ref[0], (ua, ub, uc, ud), wu_ref)
        lay(info_ref[0], (oa, ob, oc, od), wd_ref)
        acc[...] = jnp.zeros_like(acc)
        ad[...] = jnp.zeros_like(ad)

    n2 = n2_ref[...]
    cot = cot_ref[...]
    nt = n2.T
    total_out = jnp.zeros((TILE, D), F32)
    total_gn = jnp.zeros((TILE, D), F32)
    for h in range(2):
        g, u = slice(h * WIDE, (h + 1) * WIDE), slice(D + h * WIDE, D + (h + 1) * WIDE)
        act, dgate, dup, out, gn = hidden(n2, cot, wg_ref[:, g], wu_ref[:, g], wd_ref[g, :])
        total_out += out
        total_gn += gn
        acc[:, g] += dot(nt, dgate)
        acc[:, u] += dot(nt, dup)
        ad[g, :] += dot_at(act, cot)
    out_ref[...] = total_out.astype(BF)
    gn_ref[...] = total_gn.astype(BF)

    @pl.when(i == pl.num_programs(0) - 1)
    def _():
        for b in range(4):
            deal(info_ref[0], acc, slice(b * WIDE, (b + 1) * WIDE), keep_ref, send_ref, b * D // 4)
        for b in range(2):
            deal(info_ref[0], ad, slice(b * WIDE, (b + 1) * WIDE), keep_ref, send_ref, (4 + b) * D // 4)


def ffn_a_call(info, n2, cot, gate_parts, up_parts, down_parts, deps=()):
    n = n2.shape[0]
    part = jax.ShapeDtypeStruct((n, D), BF)
    size = 6 * D // 4
    return call(
        ffn_a_body,
        [info, n2, cot, *gate_parts, *up_parts, *down_parts],
        grid=(n // TILE,),
        in_specs=[smem()] + [rows(TILE, D)] * 2 + [full((D // 4, D))] * 2 + [full((D // 8, D))] * 4
        + [full((D // 4, D))] * 8,
        out_specs=[rows(TILE, D)] * 2 + [full((2, size, WIDE))] * 2,
        out_shape=[part, part, piece(size), piece(size)],
        scratch_shapes=[pltpu.VMEM((D, D), BF)] * 3 + [pltpu.VMEM((D, 2 * D), F32), pltpu.VMEM((D, D), F32)],
        megabytes=24,
        deps=deps,
        cost_estimate=cost(18),
        name="ffn_a",
    )


def norm_back(grad, n, r, gain):
    e = grad * gain
    return r * (e - jnp.mean(e, axis=-1, keepdims=True) - n * jnp.mean(e * n, axis=-1, keepdims=True))


def ffn_b_body(info_ref, n2_ref, cot_ref, ia, ib, ic, id_, oa, ob, oc, od, pout_ref, pgn_ref, mid_ref, mixed_ref, wo_ref, gain_ref,
               out_ref, gmid_ref, gmix_ref, keep_ref, send_ref, w_ref, wd_ref, acc, ad, ao):
    i = pl.program_id(0)

    @pl.when(i == 0)
    def _():
        lay(info_ref[0], (ia, ib, ic, id_), w_ref)
        lay(info_ref[0], (oa, ob, oc, od), wd_ref)
        acc[...] = jnp.zeros_like(acc)
        ao[...] = jnp.zeros_like(ao)
        ad[...] = jnp.zeros_like(ad)

    n2 = n2_ref[...]
    cot = cot_ref[...]
    act, dgate, dup, out, gn = hidden(n2, cot, w_ref[:, :WIDE], w_ref[:, WIDE:], wd_ref[...])
    nt = n2.T
    acc[:, :WIDE] += dot(nt, dgate)
    acc[:, WIDE:] += dot(nt, dup)
    ad[...] += dot_at(act, cot)
    middle = mid_ref[...].astype(F32)
    out_ref[...] = (middle + pout_ref[...].astype(F32) + out).astype(BF)
    n, r = normalize(middle)
    branch = (cot.astype(F32) + norm_back(pgn_ref[...].astype(F32) + gn, n, r, gain_ref[1:2, :])).astype(BF)
    gmid_ref[...] = branch
    gmix_ref[...] = dot_bt(branch, wo_ref[...]).astype(BF)
    ao[...] += dot_at(mixed_ref[...], branch)

    @pl.when(i == pl.num_programs(0) - 1)
    def _():
        w = info_ref[0]
        r = D // 4
        for b in range(2):
            cols = slice(b * WIDE, (b + 1) * WIDE)
            deal(w, acc, cols, keep_ref, send_ref, b * r)
            deal(w, ao, cols, keep_ref, send_ref, (2 + b) * r)
            deal(w, ad, cols, keep_ref, send_ref, 4 * r + b * r // 2)


def ffn_b_call(info, n2, cot, in_parts, down_parts, pout, pgn, middle, mixed, wo, gain, deps=()):
    n = n2.shape[0]
    size = 5 * D // 4
    return call(
        ffn_b_body,
        [info, n2, cot, *in_parts, *down_parts, pout, pgn, middle, mixed, wo, gain],
        grid=(n // TILE,),
        in_specs=[smem()] + [rows(TILE, D)] * 2 + [full((D // 4, D))] * 4 + [full((WIDE // 4, D))] * 4
        + [rows(TILE, D)] * 4 + [full((D, D)), full((8, D))],
        out_specs=[rows(TILE, D)] * 3 + [full((2, size, WIDE))] * 2,
        out_shape=[jax.ShapeDtypeStruct((n, D), BF)] * 3 + [piece(size), piece(size)],
        scratch_shapes=[pltpu.VMEM((D, D), BF), pltpu.VMEM((WIDE, D), BF),
                        pltpu.VMEM((D, D), F32), pltpu.VMEM((WIDE, D), F32), pltpu.VMEM((D, D), F32)],
        megabytes=24,
        deps=deps,
        cost_estimate=cost(14),
        name="ffn_b",
    )


def attend_back_body(info_ref, q_ref, k_ref, v_ref, g_ref, mixed_ref, lse_ref, cos_ref, sin_ref, nt_ref, *rest):
    dq_ref, dk_ref, dv_ref, keep_ref, send_ref, ak, av, aw = rest[-8:]
    ext = ak.shape[0]
    blocks = (ext - 2 * HALF) // QB
    left, right = sides(info_ref)
    ak[...] = jnp.zeros_like(ak)
    av[...] = jnp.zeros_like(av)
    zero = jnp.zeros((HALF, QUAD), BF)
    dq_ref[:HALF, :] = zero
    dq_ref[ext - HALF :, :] = zero
    prod = mixed_ref[...].astype(F32) * g_ref[...].astype(F32)
    head = lax.broadcasted_iota(jnp.int32, (8, QUAD), 1) // HD
    pick = jnp.where(head == lax.broadcasted_iota(jnp.int32, (8, QUAD), 0), 1.0, 0.0).astype(BF)
    high = prod.astype(BF)
    delta = dot_bt(pick, high) + dot_bt(pick, (prod - high.astype(F32)).astype(BF))

    def of_heads(a, start):
        return jnp.concatenate([a[h : h + 1, start : start + QB] for h in range(4)], axis=1)

    def unturn(u, at):
        cos = cos_ref[at, :]
        sl, sr = signed(-sin_ref[at, :])
        return jnp.concatenate([turn(u[:, c : c + PAIR], cos, sl, sr) for c in (0, PAIR)], axis=1).astype(BF)

    for b in range(blocks):
        start = b * QB
        win = slice(start, start + QB + 2 * HALF)
        here = slice(start + HALF, start + HALF + QB)
        bias = repeat(bias_of(b, blocks - 1, left, right))
        q4 = apart(q_ref[here, :])
        g4 = apart(g_ref[start : start + QB, :])
        kw = k_ref[win, :]
        probs = jnp.exp(dot_bt(kw, q4) + bias - of_heads(lse_ref[0], start))
        ds = (probs * (dot_bt(v_ref[win, :], g4) - of_heads(delta, start))).astype(BF)
        ak[win, :] += dot(ds, q4)
        av[win, :] += dot(probs.astype(BF), g4)
        dq_ref[here, :] = unturn(together(dot_at(ds, kw)) * HD**-0.5, here)
    dk_ref[...] = unturn(ak[...], slice(0, ext))
    dv_ref[...] = av[...].astype(BF)
    for part, ref in enumerate((dq_ref, dk_ref, dv_ref)):
        aw[...] = dot(nt_ref[...], ref[...])
        deal(info_ref[0], aw, slice(0, QUAD), keep_ref, send_ref, part * D // 4)


def attend_back_call(p, at, width, info, q, k, v, g, mixed, lse, cos, sin, nt, sofar, pieces, deps=()):
    n = g.shape[0]
    ext = q.shape[0]
    cols = pl.BlockSpec((ext, QUAD), lambda i: (0, p))
    inner = pl.BlockSpec((n, QUAD), lambda i: (0, p))
    own = jax.ShapeDtypeStruct((ext, D), BF)
    out = jax.ShapeDtypeStruct((2, 3 * D // 4, width), BF)
    args = [info, q, k, v, g, mixed, lse, cos, sin, nt]
    extra = list(sofar) + list(pieces)
    aliases = {}
    for i in range(len(sofar)):
        aliases[len(args) + i] = i
    for i in range(len(pieces)):
        aliases[len(args) + len(sofar) + i] = 3 + i
    mine = pl.BlockSpec((2, 3 * D // 4, QUAD), lambda i: (0, 0, at))
    return call(
        attend_back_body,
        args + extra,
        grid=(1,),
        in_specs=[smem(), cols, cols, cols, inner, inner, pl.BlockSpec((1, 4, n), lambda i: (p, 0, 0))]
        + [full((ext, PAIR))] * 2 + [full((D, ext))] + [pl.BlockSpec(memory_space=pl.ANY)] * len(extra),
        out_specs=[cols] * 3 + [mine] * 2,
        out_shape=[own, own, own, out, out],
        scratch_shapes=[pltpu.VMEM((ext, QUAD), F32), pltpu.VMEM((ext, QUAD), F32), pltpu.VMEM((D, QUAD), F32)],
        aliases=aliases,
        megabytes=12,
        deps=deps,
        cost_estimate=cost(4),
        name="attend_back",
    )


def last_body(info_ref, x_ref, dq_ref, dk_ref, dv_ref, rim_low, rim_high, gmid_ref, wa, wb, wc, wd, gain_ref, gin_ref, w_ref, *both):
    i = pl.program_id(0)
    start = pl.multiple_of(i * TILE, TILE)
    here = pl.ds(start + HALF, TILE)
    ext = dk_ref.shape[0]

    @pl.when(i == 0)
    def _():
        lay(info_ref[0], (wa, wb, wc, wd), w_ref)
        for j, ref in enumerate((dk_ref, dv_ref)):
            cols = slice(j * D, (j + 1) * D)
            both[j][...] = ref[...]
            both[j][HALF : 2 * HALF, :] += rim_low[:, cols]
            both[j][ext - 2 * HALF : ext - HALF, :] += rim_high[:, cols]

    total = jnp.zeros((TILE, D), F32)
    for j, ref in enumerate((dq_ref, *both)):
        total += dot_bt(ref[here, :], w_ref[:, j * D : (j + 1) * D])
    n, r = normalize(x_ref[...].astype(F32))
    gin_ref[...] = (gmid_ref[...].astype(F32) + norm_back(total, n, r, gain_ref[0:1, :])).astype(BF)


def last_call(info, x, grads, rims, gmid, w_parts, gain, deps=()):
    n = gmid.shape[0]
    ext = grads[0].shape[0]
    return call(
        last_body,
        [info, x, *grads, *rims, gmid, *w_parts, gain],
        grid=(n // TILE,),
        in_specs=[smem(), rows(TILE, D)] + [full((ext, D))] * 3 + [full((HALF, 2 * D))] * 2 + [rows(TILE, D)]
        + [full((D // 4, 3 * D))] * 4 + [full((8, D))],
        out_specs=[rows(TILE, D)],
        out_shape=[jax.ShapeDtypeStruct((n, D), BF)],
        scratch_shapes=[pltpu.VMEM((D, 3 * D), BF)] + [pltpu.VMEM((ext, D), BF)] * 2,
        megabytes=16,
        deps=deps,
        cost_estimate=cost(7),
        name="last",
    )


def adam(weight, grad, first_old, second, decay_rate):
    new_first = BETA_ONE * first_old + (1.0 - BETA_ONE) * grad
    new_second = BETA_TWO * second + (1.0 - BETA_TWO) * grad * grad
    root = jnp.sqrt(new_second * (1.0 / (1.0 - BETA_TWO**STEP))) + ADAM_EPS
    change = (-LEARN_RATE / (1.0 - BETA_ONE**STEP)) * (new_first / root)
    if decay_rate:
        change = change - (LEARN_RATE * decay_rate) * weight
    return (new_first, new_second, change)


def adam_call(info, assemble, grads, weight, first, second, rows_at_once, deps=()):
    r, width = weight.shape
    own = rows(rows_at_once, width)
    out = jax.ShapeDtypeStruct((r, width), F32)
    count = len(grads)

    def body(info_ref, *refs):
        blocks = refs[:count]
        w_ref, m_ref, v_ref = refs[count : count + 3]
        g_ref, nm_ref, nv_ref, st_ref, dots_ref = refs[-5:]
        assemble(pl.program_id(0), info_ref, blocks, g_ref)
        g = g_ref[...]
        w = w_ref[...].astype(F32)
        nm_ref[...], nv_ref[...], st_ref[...] = adam(w, g, m_ref[...], v_ref[...], WEIGHT_DECAY)
        dots_ref[...] = jnp.sum(w * g, axis=1, keepdims=True)

    return pl.pallas_call(
        body,
        grid=(r // rows_at_once,),
        in_specs=[smem()] + [pl.BlockSpec(shape, at) for _, shape, at in grads] + [own] * 3
        + [pl.BlockSpec(memory_space=pl.ANY)] * len(deps),
        out_specs=[own] * 4 + [rows(rows_at_once, 1)],
        out_shape=[out] * 4 + [jax.ShapeDtypeStruct((r, 1), F32)],
        compiler_params=pltpu.CompilerParams(dimension_semantics=("arbitrary",), vmem_limit_bytes=ADAM_MB * 1024 * 1024),
        cost_estimate=cost(3),
        name="adam",
    )(info, *[g for g, _, _ in grads], weight, first, second, *deps)


CORES = [(0, 1), (1, 0), (2, 3), (3, 2)]
CHIPS = [(0, 2), (2, 0), (1, 3), (3, 1)]


def to_core(a):
    return lax.ppermute(a, "wshard", CORES)


def to_chip(a):
    return lax.ppermute(a, "wshard", CHIPS)


def copy_body(*refs):
    for a, b in zip(refs[: len(refs) // 2], refs[len(refs) // 2 :]):
        b[...] = a[...]


def copies(arrays):
    return pl.pallas_call(
        copy_body,
        grid=(1,),
        in_specs=[full(a.shape) for a in arrays],
        out_specs=[full(a.shape) for a in arrays],
        out_shape=[jax.ShapeDtypeStruct(a.shape, a.dtype) for a in arrays],
        compiler_params=pltpu.CompilerParams(vmem_limit_bytes=8 * 1024 * 1024),
        name="copies",
    )(*arrays)


def after(a, first):
    return together_at([a, first])[0]


class Chain:
    def __init__(self, keep, send):
        count = lax.axis_size("seq")
        whole = []
        shift = 2
        while 1 << shift < count:
            whole.append(("whole", shift))
            shift += 1
        self.plan = [("core", 0), ("one", 0), ("two", 0), ("half", 1)] + whole + [("back", 1), ("end", 0)]
        self.at = 0
        self.kept = [keep]
        self.sends = [send]
        self.rows, self.columns = keep.shape[1:]

    def done(self):
        return self.at == len(self.plan)

    def start(self):
        if self.done():
            return
        kind, shift = self.plan[self.at]

        def along_seq(a):
            count = lax.axis_size("seq")
            return lax.ppermute(a, "seq", [(i, i ^ (1 << shift)) for i in range(count)])

        if kind == "core":
            ways = [to_core]
        elif kind == "one":
            ways = [to_chip, along_seq]
        elif kind == "two":
            ways = [along_seq, to_chip]
        else:
            ways = [along_seq]
        self.flights = [way(a) for way, a in zip(ways, self.sends)]

    def landing(self):
        kind, _ = self.plan[self.at]
        q, c = self.rows // 4, self.columns
        shapes = {
            "core": [(2 * q, c), (2, q, c)] * 2, "one": [(q, c)] * 4, "two": [(q, c)] * 2,
            "half": [(q, c)], "whole": [(q, c)], "back": [(2 * q, c)], "end": [(4 * q, c)],
        }[kind]

        def body(info_ref, ins, outs):
            bx, by, bz = (info_ref[0] >> 1) & 1, info_ref[1] & 1, (info_ref[1] >> 1) & 1

            def at(i, base=0):
                return pl.ds(pl.multiple_of(base + i * q, 16), q)

            if kind == "core":
                keep, got = ins
                for out, i in ((outs[0], bx), (outs[2], 1 - bx)):
                    out[...] = sum_of(keep[i, : 2 * q, :], got[i, : 2 * q, :])
                for out, i in ((outs[1], by), (outs[3], 1 - by)):
                    out[...] = sum_of(keep[:, at(i, 2 * q), :], got[:, at(i, 2 * q), :])
            elif kind == "one":
                for out, i in ((outs[0], by), (outs[2], 1 - by)):
                    out[...] = sum_of(ins[0][at(i), :], ins[2][at(i), :])
                for out, i in ((outs[1], bx), (outs[3], 1 - bx)):
                    out[...] = sum_of(ins[1][i], ins[3][i])
            elif kind == "two":
                first = sum_of(ins[0][...], ins[2][...])
                second = sum_of(ins[1][...], ins[3][...])
                put_by(bz, outs, first, second, slice(0, c))
            elif kind == "back":
                outs[0][at(bz), :] = ins[0][...]
                outs[0][at(1 - bz), :] = ins[1][...]
            elif kind == "end":
                for half in range(2):
                    outs[0][at(by, 2 * q * half), :] = ins[0][half * q : (half + 1) * q, :]
                    outs[0][at(1 - by, 2 * q * half), :] = ins[1][half * q : (half + 1) * q, :]
            else:
                outs[0][...] = sum_of(ins[0][...], ins[1][...])

        return self.kept + self.flights, shapes, body

    def landed(self, outs):
        kind, _ = self.plan[self.at]
        self.at += 1
        pairs = {"core": 2, "one": 2, "two": 1}.get(kind)
        self.kept = outs[:pairs] if pairs else outs
        self.sends = outs[pairs:] if pairs else outs


def put_by(bit, outs, first, second, cols):
    @pl.when(bit == 0)
    def _():
        outs[0][:, cols] = first
        outs[1][:, cols] = second

    @pl.when(bit != 0)
    def _():
        outs[0][:, cols] = second
        outs[1][:, cols] = first


class Joined(Chain):
    def __init__(self, first, second):
        self.both = (first, second)
        self.plan, self.at, self.rows = second.plan, second.at, second.rows
        self.columns = first.columns + second.columns

    def landing(self):
        if self.both is None:
            return Chain.landing(self)
        plans = [c.landing() for c in self.both]
        q = self.rows // 4

        def body(info_ref, ins, outs):
            bz = (info_ref[1] >> 1) & 1
            start = 0
            for i, c in enumerate(self.widths):
                a = ins[4 * i : 4 * i + 4]
                first = sum_of(a[0][...], a[2][...])
                second = sum_of(a[1][...], a[3][...])
                put_by(bz, outs, first, second, slice(start, start + c))
                start += c

        self.widths = [c.columns for c in self.both]
        return plans[0][0] + plans[1][0], [(q, self.columns)] * 2, body

    def landed(self, outs):
        self.both = None
        Chain.landed(self, outs)


def sum_of(a, b):
    return (a.astype(F32) + b.astype(F32)).astype(BF)


def nothing(*refs):
    pass


def together_at(arrays, seen=()):
    hbm = pl.BlockSpec(memory_space=pl.ANY)
    return pl.pallas_call(
        nothing,
        in_specs=[hbm] * (len(arrays) + len(seen)),
        out_specs=[hbm] * len(arrays),
        out_shape=[jax.ShapeDtypeStruct(a.shape, a.dtype) for a in arrays],
        input_output_aliases={i: i for i in range(len(arrays))},
        compiler_params=pltpu.CompilerParams(vmem_limit_bytes=1024 * 1024),
        name="boundary",
    )(*arrays, *seen)


def boundary(info, token, landing=(), starting=(), also=()):
    landing = [c for c in landing if not c.done()]
    plans = [c.landing() for c in landing]
    args = [info] + [a for p in plans for a in p[0]]
    through = [c.sends[0] for c in starting] + list(also) + [token]
    shapes = [jax.ShapeDtypeStruct(t, BF) for p in plans for t in p[1]]
    count = len(args)

    def body(*refs):
        ins = list(refs[1:count])
        outs = list(refs[count + len(through) :])
        for operands, shapes_i, land in plans:
            land(refs[0], [ins.pop(0) for _ in operands], [outs.pop(0) for _ in shapes_i])

    hbm = pl.BlockSpec(memory_space=pl.ANY)
    outs = pl.pallas_call(
        body,
        grid=(1,),
        in_specs=[smem()] + [full(a.shape) for a in args[1:]] + [hbm] * len(through),
        out_specs=[full(t.shape) for t in shapes] + [hbm] * len(through),
        out_shape=shapes + [jax.ShapeDtypeStruct(a.shape, a.dtype) for a in through],
        input_output_aliases={count + i: len(shapes) + i for i in range(len(through))},
        compiler_params=pltpu.CompilerParams(vmem_limit_bytes=16 * 1024 * 1024),
        cost_estimate=cost(1),
        name="land",
    )(*args, *through)
    outs = list(outs)
    for c, p in zip(landing, plans):
        c.landed([outs.pop(0) for _ in p[1]])
    for c in starting:
        c.sends = [outs.pop(0)]
    waits = [outs[-1]]
    for c in landing + list(starting):
        waits.append(c.sends[0])
        c.start()
    return outs[:-1], tuple(waits)


def neighbours(count):
    up = [(i, i + 1) for i in range(count - 1)]
    return up, [(j, i) for i, j in up]


def shards(
    hidden_in, cotangent, block_seq, block_place, attn_in, attn_out, ffn_in, ffn_out, norm_attn, norm_ffn,
    m_attn_in, m_attn_out, m_ffn_in, m_ffn_out, m_norm_attn, m_norm_ffn,
    v_attn_in, v_attn_out, v_ffn_in, v_ffn_out, v_norm_attn, v_norm_ffn,
):
    x = hidden_in[0]
    cot = cotangent[0]
    n = x.shape[0]
    ext = n + 2 * HALF
    w = lax.axis_index("wshard")
    count = lax.axis_size("seq")
    at = lax.axis_index("seq")
    up, down = neighbours(count)

    far = to_chip(attn_in)
    mate = to_core(attn_in)
    gain_own = jnp.stack([norm_attn, norm_ffn])
    gain_far, gain_mate = to_chip(gain_own), to_core(gain_own)
    x_low, x_high = lax.ppermute(x[n - HALF :], "seq", up), lax.ppermute(x[:HALF], "seq", down)
    attn_out_own, down_a, down_b = copies([attn_out, ffn_out[: D // 4], ffn_out[D // 4 :]])
    info = jnp.concatenate([jnp.stack([w, at]).astype(jnp.int32), block_seq[0], block_place[0]])
    some, rest = D // 4, FF // 4 - D // 4

    def units(start, first, size):
        return [ffn_in[:, start + s * (FF // 4) + first :][:, :size] for s in range(4)]

    in_g = jnp.concatenate(units(0, 0, some), axis=1)
    in_u = jnp.concatenate(units(FF, 0, some), axis=1)
    in_b = jnp.concatenate(units(0, some, rest) + units(FF, some, rest), axis=1)
    out_mate, g_mate, u_mate, da_mate, db_mate, b_mate = (to_core(a) for a in (attn_out_own, in_g, in_u, down_a, down_b, in_b))

    g_half = lax.dynamic_slice_in_dim(in_g, (at & 1) * (D // 8), D // 8, 0)
    (token,) = together_at(
        [jnp.zeros((8, 128), F32)], [x_low, x_high, info, mate, out_mate, g_mate, u_mate, da_mate, db_mate, b_mate]
    )
    far, g_half, attn_out_own, token = together_at([far, g_half, attn_out_own, token], [gain_far, gain_mate])
    farmate = to_core(far)
    out_far = to_chip(attn_out_own)
    g_mine = to_chip(g_half)
    attn_parts = attn_in, mate, far, farmate
    gains = gain_own, gain_mate, gain_far, to_core(gain_far)
    nt, q, k, v, cos, sin, gain, token = qkv_call(info, x, x_low, x_high, gains, attn_parts)
    out_far, g_mine, in_u, token = together_at([out_far, g_mine, in_u, token])
    out_farmate = to_core(out_far)
    out_farmate, in_u, down_a, token = together_at([out_farmate, in_u, down_a, token])
    u_far = to_chip(in_u)
    da_far = to_chip(down_a)
    g_other = lax.ppermute(g_mine, "seq", [(i, i ^ 1) for i in range(count)])
    out_parts = attn_out, out_mate, out_far, out_farmate
    mixed, middle, n2, out_w, lse, token = attend_call(info, q, k, v, x, out_parts, gain, deps=(token,))
    g_other, u_far, da_far, in_b, down_b, token = together_at([g_other, u_far, da_far, in_b, down_b, token])
    b_far = to_chip(in_b)
    db_far = to_chip(down_b)
    gate_parts = in_g, g_mate, g_mine, g_other, to_core(g_mine), to_core(g_other)
    up_parts = in_u, u_mate, u_far, to_core(u_far)
    down_parts = down_a, da_mate, da_far, to_core(da_far)
    pout, pgn, keep, send, token = ffn_a_call(info, n2, cot, gate_parts, up_parts, down_parts, deps=(token,))
    chain_a = Chain(keep, send)
    (b_far, db_far), deps = boundary(info, token, (), (chain_a,), (b_far, db_far))
    b_parts = in_b, b_mate, b_far, to_core(b_far)
    db_parts = down_b, db_mate, db_far, to_core(db_far)
    _, deps = boundary(info, deps[0], (chain_a,))
    block_out, gmid, gmix, keep, send, token = ffn_b_call(
        info, n2, cot, b_parts, db_parts, pout, pgn, middle, mixed, out_w, gain, deps=deps
    )
    chain_b = Chain(keep, send)
    grads, pieces = (), ()

    def back(p, at, width, deps):
        nonlocal grads, pieces
        if at == 0:
            pieces = ()
        out = attend_back_call(p, at, width, info, q, k, v, gmix, mixed, lse, cos, sin, nt, grads, pieces, deps)
        grads, pieces = out[:3], out[3:5]
        return out[5]

    _, deps = boundary(info, token, (chain_a,), (chain_b,))
    token = back(0, 0, 2 * QUAD, deps)
    _, deps = boundary(info, token, (chain_a, chain_b))
    token = back(1, 1, 2 * QUAD, deps)
    chain_c = Chain(*pieces)
    _, deps = boundary(info, token, (chain_a, chain_b), (chain_c,))
    token = back(2, 0, QUAD, deps)
    chain_d = Chain(*pieces)
    _, deps = boundary(info, token, (chain_b, chain_c), (chain_d,))
    rims = [jnp.concatenate([a[r] for a in grads[1:]], axis=1) for r in (slice(0, HALF), slice(n + HALF, ext))]
    rims, deps = boundary(info, deps[0], (chain_a, chain_b, chain_c, chain_d), (), rims)
    rims = lax.ppermute(rims[1], "seq", up), lax.ppermute(rims[0], "seq", down)
    rims, deps = boundary(info, deps[0], (chain_a, chain_b, chain_d), (), rims)
    grad_in, token = last_call(info, x, grads, rims, gmid, attn_parts, gain, deps=deps)
    chain_c = Joined(chain_c, chain_d)
    chains = (chain_a, chain_b, chain_c)
    while chain_c.at < len(chain_c.plan) - 1:
        _, deps = boundary(info, token, chains)
        token = deps[0]
    sum_a, sum_b = chain_a.kept[0], chain_b.kept[0]

    r = D // 4
    third = FF // 12

    def block_rows(a, first, step, columns):
        return a, (step, columns), lambda i: (first // step + i, 0)

    def lay_out(i, info_ref, refs, out):
        for b, ref in enumerate(refs):
            out[:, b * WIDE : (b + 1) * WIDE] = ref[...].astype(F32)

    res_attn_out = adam_call(
        info, lay_out, [block_rows(sum_b, (2 + b) * r, r // 2, WIDE) for b in range(2)], attn_out, m_attn_out, v_attn_out, r // 2
    )

    def lay_down(i, info_ref, refs, out):
        for b in range(2):
            out[:, b * WIDE : (b + 1) * WIDE] = jnp.where(i < 2, refs[b][...], refs[2 + b][...]).astype(F32)

    res_ffn_out = adam_call(
        info, lay_down,
        [(sum_a, (third, WIDE), lambda i, b=b: ((4 + b) * (r // third) + jnp.minimum(i, 1), 0)) for b in range(2)]
        + [(sum_b, (third, WIDE), lambda i, b=b: (4 * (r // third) + b, 0)) for b in range(2)],
        ffn_out, m_ffn_out, v_ffn_out, third,
    )

    def lay_units(i, info_ref, refs, out):
        for half in range(2):
            of_a = jnp.concatenate([refs[2 * half][...], refs[2 * half + 1][...]], axis=1).astype(F32)
            of_b = refs[4 + half][...].astype(F32)
            for s in range(4):
                start = half * FF + s * (some + rest)
                out[:, start : start + some] = of_a[:, s * some : (s + 1) * some]
                out[:, start + some : start + some + rest] = of_b[:, s * rest : (s + 1) * rest]

    step = r // 4
    res_ffn_in = adam_call(
        info, lay_units,
        [block_rows(sum_a, b * r, step, WIDE) for b in range(4)] + [block_rows(sum_b, b * r, step, WIDE) for b in range(2)],
        ffn_in, m_ffn_in, v_ffn_in, step, deps=(token,),
    )

    def row_of(part, i):
        at = part * r + i * step
        return at // (2 * r * 3 // 4), (at % (2 * r * 3 // 4)) // (r * 3 // 4), at % (r * 3 // 4)

    def source(part):
        def at(i):
            half, _, row = row_of(part, i)
            return (half * (r * 3 // 4) + row) // step, 0

        return at

    def lay_parts(i, info_ref, refs, out):
        for part in range(3):
            mine = row_of(part, i)[1] == (info_ref[1] & 1)
            out[:, part * D : (part + 1) * D] = jnp.where(mine, refs[part][...], refs[3 + part][...]).astype(F32)

    res_attn_in = adam_call(
        info, lay_parts,
        [(a, (step, D), source(part)) for a in (chain_c.kept[0], chain_c.flights[0]) for part in range(3)],
        attn_in, m_attn_in, v_attn_in, step,
    )
    results = [res_attn_in, res_attn_out, res_ffn_in, res_ffn_out]
    for res, own_gain, m, v_ in ((res_attn_in, norm_attn, m_norm_attn, v_norm_attn), (res_ffn_in, norm_ffn, m_norm_ffn, v_norm_ffn)):
        wide = own_gain.astype(F32)
        g = res[4][:, 0] / wide
        results.append((g,) + adam(wide, g, m, v_, 0.0))
    return (block_out[None], grad_in[None]) + tuple(res[i] for i in range(4) for res in results)


def solution(mesh):
    big = P("wshard", "seq", None)
    mat = P("wshard", None)
    vec = P("wshard")
    group = (mat, mat, mat, mat, vec, vec)
    in_specs = (big, big, mat, mat) + group * 3
    out_specs = (big, big) + group * 4
    return jax.shard_map(shards, mesh=mesh, in_specs=in_specs, out_specs=out_specs, check_vma=False)
```

```python
import functools

import jax
import jax.numpy as jnp
import numpy as np
from jax import lax
from jax.experimental import pallas as pl
from jax.experimental.pallas import tpu as pltpu
from jax.sharding import PartitionSpec as P

D = 768
FF = 1152
HEADS = 12
HD = 64
HALF = 64
STEP = 10
PAIR = 2 * HD
QB = 128
TILE = 256
WIDE = 384
ADAM_MB = 60
QUAD = 4 * HD

NORM_EPS = 1e-05
BETA_ONE = 0.9
BETA_TWO = 0.98
LEARN_RATE = 0.05
WEIGHT_DECAY = 0.01
ADAM_EPS = 1e-06
NEG_FILL = -1e30
THETA = 10000.0
BF = jnp.bfloat16
F32 = jnp.float32


def dot(left, right):
    return lax.dot_general(left, right, (((1,), (0,)), ((), ())), preferred_element_type=F32)


def dot_bt(left, right):
    return lax.dot_general(left, right, (((1,), (1,)), ((), ())), preferred_element_type=F32)


def dot_at(left, right):
    return lax.dot_general(left, right, (((0,), (0,)), ((), ())), preferred_element_type=F32)


def call(body, args, in_specs, out_specs, out_shape, megabytes, deps=(), aliases=None, **kw):
    first = len(args)
    n_out = len(out_shape)

    def wrapped(*refs):
        refs = refs[:first] + refs[first + len(deps) :]
        token = refs[first + n_out]
        token[...] = jnp.zeros_like(token)
        body(*refs[: first + n_out], *refs[first + n_out + 1 :])

    return pl.pallas_call(
        wrapped,
        in_specs=list(in_specs) + [pl.BlockSpec(memory_space=pl.ANY)] * len(deps),
        out_specs=list(out_specs) + [full((8, 128))],
        out_shape=list(out_shape) + [jax.ShapeDtypeStruct((8, 128), F32)],
        input_output_aliases=aliases or {},
        compiler_params=pltpu.CompilerParams(
            dimension_semantics=("arbitrary",), vmem_limit_bytes=megabytes * 1024 * 1024
        ),
        **kw,
    )(*args, *deps)


def full(shape):
    return pl.BlockSpec(shape, lambda i: (0,) * len(shape))


def rows(tile, width):
    return pl.BlockSpec((tile, width), lambda i: (i, 0))


def cost(microseconds):
    return pl.CostEstimate(flops=int(microseconds * 1.1e9), bytes_accessed=0, transcendentals=0)


def normalize(x):
    mean = jnp.mean(x, axis=-1, keepdims=True)
    centered = x - mean
    var = jnp.mean(centered * centered, axis=-1, keepdims=True)
    r = lax.rsqrt(var + NORM_EPS)
    return centered * r, r


def signed(sin):
    first = lax.broadcasted_iota(jnp.int32, sin.shape, 1) % HD < HD // 2
    zero = jnp.zeros_like(sin)
    return jnp.where(first, -sin, zero), jnp.where(first, zero, sin)


def turn(u, cos, sin_left, sin_right):
    return u * cos + pltpu.roll(u, PAIR - HD // 2, 1) * sin_left + pltpu.roll(u, HD // 2, 1) * sin_right


def blocks_of(info_ref):
    return (info_ref.shape[0] - 2) // 2


def sides(info_ref):
    count = blocks_of(info_ref)
    at = info_ref[1]
    own = info_ref[2 + at]
    left = (at > 0) & (info_ref[2 + jnp.maximum(at - 1, 0)] == own)
    right = (at < count - 1) & (info_ref[2 + jnp.minimum(at + 1, count - 1)] == own)
    return left, right


def bias_of(b, last, left, right):
    shape = (QB + 2 * HALF, QB)
    key = lax.broadcasted_iota(jnp.int32, shape, 0)
    off = key - lax.broadcasted_iota(jnp.int32, shape, 1)
    low = jnp.where((b > 0) | left, 0, HALF)
    high = jnp.where((b < last) | right, QB + 2 * HALF, QB + HALF)
    ok = (off >= 0) & (off <= 2 * HALF) & (key >= low) & (key < high)
    return jnp.where(ok, 0.0, NEG_FILL)


def lay(w, parts, out_ref, bit=0):
    r = out_ref.shape[0] // 4
    for i, ref in enumerate(parts):
        start = (w ^ i) * r
        if isinstance(ref, tuple):
            half = r // 2
            for j, a in enumerate(ref):
                out_ref[pl.ds(pl.multiple_of(start + (bit ^ j) * half, 16), half), :] = a[...]
        else:
            out_ref[pl.ds(pl.multiple_of(start, 32), r), :] = ref[...]


def deal(w, acc, cols, keep_ref, send_ref, at):
    r = acc.shape[0] // 4
    c = w & 1
    for x in range(2):
        keep_ref[x, at : at + r, :] = acc[pl.ds(pl.multiple_of((2 * x + c) * r, 32), r), cols].astype(BF)
        send_ref[x, at : at + r, :] = acc[pl.ds(pl.multiple_of((2 * x + 1 - c) * r, 32), r), cols].astype(BF)


def smem():
    return pl.BlockSpec(memory_space=pltpu.SMEM)


def piece(n_rows):
    return jax.ShapeDtypeStruct((2, n_rows, WIDE), BF)


def qkv_body(info_ref, x_ref, low_ref, high_ref, gain_a, gain_b, gain_c, gain_d, wa, wb, wc, wd, far_ref, near_ref,
             nt_ref, q_ref, k_ref, v_ref, cos_ref, sin_ref, gain_ref, w_ref, x_ext):
    t = q_ref.shape[0]
    i = pl.program_id(0)

    @pl.when(i == 0)
    def _():
        lay(info_ref[0], (wa, wb, wc, wd), w_ref)
        end = x_ext.shape[0] - HALF
        x_ext[:HALF, :] = low_ref[...]
        x_ext[HALF:end, :] = x_ref[...]
        x_ext[end:, :] = high_ref[...]
        r = D // 4
        for p, ref in enumerate((gain_a, gain_b, gain_c, gain_d)):
            gains = ref[...].astype(F32)
            for owner in range(4):

                @pl.when((info_ref[0] ^ p) == owner)
                def _():
                    gain_ref[:2, owner * r : (owner + 1) * r] = gains


    place = info_ref[2 + blocks_of(info_ref) + info_ref[1]]
    c2, s2 = far_ref[0, pl.ds(place, 1), :], far_ref[1, pl.ds(place, 1), :]
    c1, s1 = near_ref[0], near_ref[1]
    cos = c1 * c2 - s1 * s2
    sin = s1 * c2 + c1 * s2
    cos_ref[...] = cos
    sin_ref[...] = sin
    sl, sr = signed(sin)
    n, _ = normalize(x_ext[pl.ds(pl.multiple_of(i * t, 128), t), :].astype(F32))
    normed = (n * gain_ref[0:1, :]).astype(BF)
    nt_ref[...] = normed.T
    for part, ref, scale in ((0, q_ref, HD**-0.5), (1, k_ref, 1.0)):
        u = dot(normed, w_ref[:, part * D : (part + 1) * D])
        for p in range(D // PAIR):
            r = turn(u[:, p * PAIR : (p + 1) * PAIR], cos, sl, sr)
            ref[:, p * PAIR : (p + 1) * PAIR] = (r * scale).astype(BF)
    v_ref[...] = dot(normed, w_ref[:, 2 * D :]).astype(BF)


def angle_tables(n, ext):
    freq = THETA ** (-2.0 * (np.arange(PAIR) % (HD // 2)) / HD)

    def table(positions):
        angle = positions[:, None] * freq[None, :]
        return jnp.asarray(np.stack([np.cos(angle), np.sin(angle)]).astype(np.float32))

    return table(np.arange(4.0) * n), table(np.arange(float(ext)) - HALF)


def qkv_call(info, x, low, high, gains, w_parts, deps=()):
    n = x.shape[0]
    ext = n + 2 * HALF
    t = ext // 3
    out = jax.ShapeDtypeStruct((ext, D), BF)
    table = jax.ShapeDtypeStruct((ext, PAIR), F32)
    far, near = angle_tables(n, ext)
    return call(
        qkv_body,
        [info, x, low, high, *gains, *w_parts, far, near],
        grid=(3,),
        in_specs=[smem(), full((n, D)), full((HALF, D)), full((HALF, D))] + [full((2, D // 4))] * 4 + [full((D // 4, 3 * D))] * 4
        + [full(far.shape), pl.BlockSpec((2, t, PAIR), lambda i: (0, i, 0))],
        out_specs=[pl.BlockSpec((D, t), lambda i: (0, i))] + [rows(t, D)] * 3 + [rows(t, PAIR)] * 2 + [full((8, D))],
        out_shape=[jax.ShapeDtypeStruct((D, ext), BF)] + [out] * 3 + [table] * 2 + [jax.ShapeDtypeStruct((8, D), F32)],
        scratch_shapes=[pltpu.VMEM((D, 3 * D), BF), pltpu.VMEM((ext, D), BF)],
        megabytes=20,
        deps=deps,
        cost_estimate=cost(9),
        name="qkv",
    )


def apart(u):
    head = lax.broadcasted_iota(jnp.int32, u.shape, 1) // HD
    zero = jnp.zeros_like(u)
    return jnp.concatenate([jnp.where(head == h, u, zero) for h in range(4)], axis=0)


def together(u):
    r = u.shape[0] // 4
    head = lax.broadcasted_iota(jnp.int32, (r, QUAD), 1) // HD
    out = u[:r]
    for h in range(1, 4):
        out = jnp.where(head == h, u[h * r : (h + 1) * r], out)
    return out


def repeat(u):
    return jnp.concatenate([u] * 4, axis=1)


def attend_body(info_ref, q_ref, k_ref, v_ref, x_ref, wa, wb, wc, wd, gain_ref,
                mixed_ref, middle_ref, n2_ref, w_ref, lse_ref):
    i = pl.program_id(0)
    last = pl.num_programs(0) * (TILE // QB) - 1
    left, right = sides(info_ref)

    @pl.when(i == 0)
    def _():
        lay(info_ref[0], (wa, wb, wc, wd), w_ref)

    for s in range(TILE // QB):
        b = i * (TILE // QB) + s
        start = pl.multiple_of(b * QB, QB)
        bias = repeat(bias_of(b, last, left, right))
        for g in range(D // QUAD):
            cols = slice(g * QUAD, (g + 1) * QUAD)
            win = pl.ds(start, QB + 2 * HALF)
            q4 = apart(q_ref[pl.ds(start + HALF, QB), cols])
            scores = dot_bt(k_ref[win, cols], q4) + bias
            most = jnp.max(scores, axis=0, keepdims=True)
            e = jnp.exp(scores - most)
            total = jnp.sum(e, axis=0, keepdims=True)
            probs = (e * (1.0 / total)).astype(BF)
            o = together(dot_at(probs, v_ref[win, cols]))
            mixed_ref[s * QB : (s + 1) * QB, cols] = o.astype(BF)
            lse = most + jnp.log(total)
            for h in range(4):
                lse_ref[g, h : h + 1, s * QB : (s + 1) * QB] = lse[:, h * QB : (h + 1) * QB]
    middle = x_ref[...].astype(F32) + dot(mixed_ref[...], w_ref[...])
    middle_ref[...] = middle.astype(BF)
    n, _ = normalize(middle)
    n2_ref[...] = (n * gain_ref[1:2, :]).astype(BF)


def attend_call(info, q, k, v, x, w_parts, gain, deps=()):
    n = x.shape[0]
    ext = q.shape[0]
    groups = D // QUAD
    return call(
        attend_body,
        [info, q, k, v, x, *w_parts, gain],
        grid=(n // TILE,),
        in_specs=[smem()] + [full((ext, D))] * 3 + [rows(TILE, D)] + [full((D // 4, D))] * 4 + [full((8, D))],
        out_specs=[rows(TILE, D)] * 3 + [full((D, D)), pl.BlockSpec((groups, 4, TILE), lambda i: (0, 0, i))],
        out_shape=[
            jax.ShapeDtypeStruct((n, D), BF), jax.ShapeDtypeStruct((n, D), BF), jax.ShapeDtypeStruct((n, D), BF),
            jax.ShapeDtypeStruct((D, D), BF), jax.ShapeDtypeStruct((groups, 4, n), F32),
        ],
        megabytes=12,
        deps=deps,
        cost_estimate=cost(11),
        name="attend",
    )


def hidden(n2, cot, both, wd):
    gate_up = jnp.concatenate([dot(n2, w[...]) for w in both], axis=1)
    half = gate_up.shape[1] // 2
    gate, up = gate_up[:, :half], gate_up[:, half:]
    ga = dot_bt(cot, wd)
    phi = 0.5 + 0.5 * lax.erf(gate * (2.0**-0.5))
    gelu = gate * phi
    act = (gelu * up).astype(BF)
    slope = phi + gate * (jnp.exp(-0.5 * gate * gate) * 0.3989422804014327)
    grads = jnp.concatenate([(ga * up * slope).astype(BF), (ga * gelu).astype(BF)], axis=1)
    out = dot(act, wd)
    size = grads.shape[1] // len(both)
    gn = sum(dot_bt(grads[:, i * size : (i + 1) * size], w[...]) for i, w in enumerate(both))
    return act, grads, out, gn


def ffn_a_body(info_ref, n2_ref, cot_ref, ga, gb, gc, gd, ge, gf, ua, ub, uc, ud, oa, ob, oc, od,
               out_ref, gn_ref, keep_ref, send_ref, wg_ref, wu_ref, wd_ref, acc, ad):
    i = pl.program_id(0)

    @pl.when(i == 0)
    def _():
        lay(info_ref[0], (ga, gb, (gc, gd), (ge, gf)), wg_ref, info_ref[1] & 1)
        lay(info_ref[0], (ua, ub, uc, ud), wu_ref)
        lay(info_ref[0], (oa, ob, oc, od), wd_ref)
        acc[...] = jnp.zeros_like(acc)
        ad[...] = jnp.zeros_like(ad)

    n2 = n2_ref[...]
    cot = cot_ref[...]
    nt = n2.T
    act, grads, total_out, total_gn = hidden(n2, cot, (wg_ref, wu_ref), wd_ref[...])
    acc[...] += dot(nt, grads)
    ad[...] += dot_at(act, cot)
    out_ref[...] = total_out.astype(BF)
    gn_ref[...] = total_gn.astype(BF)

    @pl.when(i == pl.num_programs(0) - 1)
    def _():
        for b in range(4):
            deal(info_ref[0], acc, slice(b * WIDE, (b + 1) * WIDE), keep_ref, send_ref, b * D // 4)
        for b in range(2):
            deal(info_ref[0], ad, slice(b * WIDE, (b + 1) * WIDE), keep_ref, send_ref, (4 + b) * D // 4)


def ffn_a_call(info, n2, cot, gate_parts, up_parts, down_parts, deps=()):
    n = n2.shape[0]
    part = jax.ShapeDtypeStruct((n, D), BF)
    size = 6 * D // 4
    return call(
        ffn_a_body,
        [info, n2, cot, *gate_parts, *up_parts, *down_parts],
        grid=(n // TILE,),
        in_specs=[smem()] + [rows(TILE, D)] * 2 + [full((D // 4, D))] * 2 + [full((D // 8, D))] * 4
        + [full((D // 4, D))] * 8,
        out_specs=[rows(TILE, D)] * 2 + [full((2, size, WIDE))] * 2,
        out_shape=[part, part, piece(size), piece(size)],
        scratch_shapes=[pltpu.VMEM((D, D), BF)] * 3 + [pltpu.VMEM((D, 2 * D), F32), pltpu.VMEM((D, D), F32)],
        megabytes=24,
        deps=deps,
        cost_estimate=cost(18),
        name="ffn_a",
    )


def norm_back(grad, n, r, gain):
    e = grad * gain
    return r * (e - jnp.mean(e, axis=-1, keepdims=True) - n * jnp.mean(e * n, axis=-1, keepdims=True))


def ffn_b_body(info_ref, n2_ref, cot_ref, ia, ib, ic, id_, oa, ob, oc, od, pout_ref, pgn_ref, mid_ref, mixed_ref, wo_ref, gain_ref,
               out_ref, gmid_ref, gmix_ref, keep_ref, send_ref, w_ref, wd_ref, acc, ad, ao):
    i = pl.program_id(0)

    @pl.when(i == 0)
    def _():
        lay(info_ref[0], (ia, ib, ic, id_), w_ref)
        lay(info_ref[0], (oa, ob, oc, od), wd_ref)
        acc[...] = jnp.zeros_like(acc)
        ao[...] = jnp.zeros_like(ao)
        ad[...] = jnp.zeros_like(ad)

    n2 = n2_ref[...]
    cot = cot_ref[...]
    act, grads, out, gn = hidden(n2, cot, (w_ref,), wd_ref[...])
    acc[...] += dot(n2.T, grads)
    ad[...] += dot_at(act, cot)
    middle = mid_ref[...].astype(F32)
    out_ref[...] = (middle + pout_ref[...].astype(F32) + out).astype(BF)
    n, r = normalize(middle)
    branch = (cot.astype(F32) + norm_back(pgn_ref[...].astype(F32) + gn, n, r, gain_ref[1:2, :])).astype(BF)
    gmid_ref[...] = branch
    gmix_ref[...] = dot_bt(branch, wo_ref[...]).astype(BF)
    ao[...] += dot_at(mixed_ref[...], branch)

    @pl.when(i == pl.num_programs(0) - 1)
    def _():
        w = info_ref[0]
        r = D // 4
        for b in range(2):
            cols = slice(b * WIDE, (b + 1) * WIDE)
            deal(w, acc, cols, keep_ref, send_ref, b * r)
            deal(w, ao, cols, keep_ref, send_ref, (2 + b) * r)
            deal(w, ad, cols, keep_ref, send_ref, 4 * r + b * r // 2)


def ffn_b_call(info, n2, cot, in_parts, down_parts, pout, pgn, middle, mixed, wo, gain, deps=()):
    n = n2.shape[0]
    size = 5 * D // 4
    return call(
        ffn_b_body,
        [info, n2, cot, *in_parts, *down_parts, pout, pgn, middle, mixed, wo, gain],
        grid=(n // TILE,),
        in_specs=[smem()] + [rows(TILE, D)] * 2 + [full((D // 4, D))] * 4 + [full((WIDE // 4, D))] * 4
        + [rows(TILE, D)] * 4 + [full((D, D)), full((8, D))],
        out_specs=[rows(TILE, D)] * 3 + [full((2, size, WIDE))] * 2,
        out_shape=[jax.ShapeDtypeStruct((n, D), BF)] * 3 + [piece(size), piece(size)],
        scratch_shapes=[pltpu.VMEM((D, D), BF), pltpu.VMEM((WIDE, D), BF),
                        pltpu.VMEM((D, D), F32), pltpu.VMEM((WIDE, D), F32), pltpu.VMEM((D, D), F32)],
        megabytes=24,
        deps=deps,
        cost_estimate=cost(14),
        name="ffn_b",
    )


def attend_back_body(info_ref, q_ref, k_ref, v_ref, g_ref, mixed_ref, lse_ref, cos_ref, sin_ref, nt_ref, *rest):
    dq_ref, dk_ref, dv_ref, keep_ref, send_ref, ak, av, aw = rest[-8:]
    ext = ak.shape[0]
    blocks = (ext - 2 * HALF) // QB
    left, right = sides(info_ref)
    ak[...] = jnp.zeros_like(ak)
    av[...] = jnp.zeros_like(av)
    zero = jnp.zeros((HALF, QUAD), BF)
    dq_ref[:HALF, :] = zero
    dq_ref[ext - HALF :, :] = zero
    prod = mixed_ref[...].astype(F32) * g_ref[...].astype(F32)
    head = lax.broadcasted_iota(jnp.int32, (8, QUAD), 1) // HD
    pick = jnp.where(head == lax.broadcasted_iota(jnp.int32, (8, QUAD), 0), 1.0, 0.0).astype(BF)
    high = prod.astype(BF)
    delta = dot_bt(pick, high) + dot_bt(pick, (prod - high.astype(F32)).astype(BF))

    def of_heads(a, start):
        return jnp.concatenate([a[h : h + 1, start : start + QB] for h in range(4)], axis=1)

    def unturn(u, at):
        cos = cos_ref[at, :]
        sl, sr = signed(-sin_ref[at, :])
        return jnp.concatenate([turn(u[:, c : c + PAIR], cos, sl, sr) for c in (0, PAIR)], axis=1).astype(BF)

    for b in range(blocks):
        start = b * QB
        win = slice(start, start + QB + 2 * HALF)
        here = slice(start + HALF, start + HALF + QB)
        bias = repeat(bias_of(b, blocks - 1, left, right))
        q4 = apart(q_ref[here, :])
        g4 = apart(g_ref[start : start + QB, :])
        kw = k_ref[win, :]
        probs = jnp.exp(dot_bt(kw, q4) + bias - of_heads(lse_ref[0], start))
        ds = (probs * (dot_bt(v_ref[win, :], g4) - of_heads(delta, start))).astype(BF)
        ak[win, :] += dot(ds, q4)
        av[win, :] += dot(probs.astype(BF), g4)
        dq_ref[here, :] = unturn(together(dot_at(ds, kw)) * HD**-0.5, here)
    dk_ref[...] = unturn(ak[...], slice(0, ext))
    dv_ref[...] = av[...].astype(BF)
    for part, ref in enumerate((dq_ref, dk_ref, dv_ref)):
        aw[...] = dot(nt_ref[...], ref[...])
        deal(info_ref[0], aw, slice(0, QUAD), keep_ref, send_ref, part * D // 4)


def attend_back_call(p, at, width, info, q, k, v, g, mixed, lse, cos, sin, nt, sofar, pieces, deps=()):
    n = g.shape[0]
    ext = q.shape[0]
    cols = pl.BlockSpec((ext, QUAD), lambda i: (0, p))
    inner = pl.BlockSpec((n, QUAD), lambda i: (0, p))
    own = jax.ShapeDtypeStruct((ext, D), BF)
    out = jax.ShapeDtypeStruct((2, 3 * D // 4, width), BF)
    args = [info, q, k, v, g, mixed, lse, cos, sin, nt]
    extra = list(sofar) + list(pieces)
    aliases = {}
    for i in range(len(sofar)):
        aliases[len(args) + i] = i
    for i in range(len(pieces)):
        aliases[len(args) + len(sofar) + i] = 3 + i
    mine = pl.BlockSpec((2, 3 * D // 4, QUAD), lambda i: (0, 0, at))
    return call(
        attend_back_body,
        args + extra,
        grid=(1,),
        in_specs=[smem(), cols, cols, cols, inner, inner, pl.BlockSpec((1, 4, n), lambda i: (p, 0, 0))]
        + [full((ext, PAIR))] * 2 + [full((D, ext))] + [pl.BlockSpec(memory_space=pl.ANY)] * len(extra),
        out_specs=[cols] * 3 + [mine] * 2,
        out_shape=[own, own, own, out, out],
        scratch_shapes=[pltpu.VMEM((ext, QUAD), F32), pltpu.VMEM((ext, QUAD), F32), pltpu.VMEM((D, QUAD), F32)],
        aliases=aliases,
        megabytes=12,
        deps=deps,
        cost_estimate=cost(4),
        name="attend_back",
    )


def last_body(info_ref, x_ref, dq_ref, dk_ref, dv_ref, rim_low, rim_high, gmid_ref, wa, wb, wc, wd, gain_ref, gin_ref, w_ref, *both):
    i = pl.program_id(0)
    start = pl.multiple_of(i * TILE, TILE)
    here = pl.ds(start + HALF, TILE)
    ext = dk_ref.shape[0]

    @pl.when(i == 0)
    def _():
        lay(info_ref[0], (wa, wb, wc, wd), w_ref)
        for j, ref in enumerate((dk_ref, dv_ref)):
            cols = slice(j * D, (j + 1) * D)
            both[j][...] = ref[...]
            both[j][HALF : 2 * HALF, :] += rim_low[:, cols]
            both[j][ext - 2 * HALF : ext - HALF, :] += rim_high[:, cols]

    total = jnp.zeros((TILE, D), F32)
    for j, ref in enumerate((dq_ref, *both)):
        total += dot_bt(ref[here, :], w_ref[:, j * D : (j + 1) * D])
    n, r = normalize(x_ref[...].astype(F32))
    gin_ref[...] = (gmid_ref[...].astype(F32) + norm_back(total, n, r, gain_ref[0:1, :])).astype(BF)


def last_call(info, x, grads, rims, gmid, w_parts, gain, deps=()):
    n = gmid.shape[0]
    ext = grads[0].shape[0]
    return call(
        last_body,
        [info, x, *grads, *rims, gmid, *w_parts, gain],
        grid=(n // TILE,),
        in_specs=[smem(), rows(TILE, D)] + [full((ext, D))] * 3 + [full((HALF, 2 * D))] * 2 + [rows(TILE, D)]
        + [full((D // 4, 3 * D))] * 4 + [full((8, D))],
        out_specs=[rows(TILE, D)],
        out_shape=[jax.ShapeDtypeStruct((n, D), BF)],
        scratch_shapes=[pltpu.VMEM((D, 3 * D), BF)] + [pltpu.VMEM((ext, D), BF)] * 2,
        megabytes=16,
        deps=deps,
        cost_estimate=cost(7),
        name="last",
    )


def adam(weight, grad, first_old, second, decay_rate):
    new_first = BETA_ONE * first_old + (1.0 - BETA_ONE) * grad
    new_second = BETA_TWO * second + (1.0 - BETA_TWO) * grad * grad
    root = jnp.sqrt(new_second * (1.0 / (1.0 - BETA_TWO**STEP))) + ADAM_EPS
    change = (-LEARN_RATE / (1.0 - BETA_ONE**STEP)) * (new_first / root)
    if decay_rate:
        change = change - (LEARN_RATE * decay_rate) * weight
    return (new_first, new_second, change)


def adam_call(info, assemble, grads, weight, first, second, rows_at_once, deps=()):
    r, width = weight.shape
    own = rows(rows_at_once, width)
    out = jax.ShapeDtypeStruct((r, width), F32)
    count = len(grads)

    def body(info_ref, *refs):
        blocks = refs[:count]
        w_ref, m_ref, v_ref = refs[count : count + 3]
        g_ref, nm_ref, nv_ref, st_ref, dots_ref = refs[-5:]
        assemble(pl.program_id(0), info_ref, blocks, g_ref)
        g = g_ref[...]
        w = w_ref[...].astype(F32)
        nm_ref[...], nv_ref[...], st_ref[...] = adam(w, g, m_ref[...], v_ref[...], WEIGHT_DECAY)
        dots_ref[...] = jnp.sum(w * g, axis=1, keepdims=True)

    return pl.pallas_call(
        body,
        grid=(r // rows_at_once,),
        in_specs=[smem()] + [pl.BlockSpec(shape, at) for _, shape, at in grads] + [own] * 3
        + [pl.BlockSpec(memory_space=pl.ANY)] * len(deps),
        out_specs=[own] * 4 + [rows(rows_at_once, 1)],
        out_shape=[out] * 4 + [jax.ShapeDtypeStruct((r, 1), F32)],
        compiler_params=pltpu.CompilerParams(dimension_semantics=("arbitrary",), vmem_limit_bytes=ADAM_MB * 1024 * 1024),
        cost_estimate=cost(3),
        name="adam",
    )(info, *[g for g, _, _ in grads], weight, first, second, *deps)


CORES = [(0, 1), (1, 0), (2, 3), (3, 2)]
CHIPS = [(0, 2), (2, 0), (1, 3), (3, 1)]


def to_core(a):
    return lax.ppermute(a, "wshard", CORES)


def to_chip(a):
    return lax.ppermute(a, "wshard", CHIPS)


def copy_body(*refs):
    for a, b in zip(refs[: len(refs) // 2], refs[len(refs) // 2 :]):
        b[...] = a[...]


def copies(arrays):
    return pl.pallas_call(
        copy_body,
        grid=(1,),
        in_specs=[full(a.shape) for a in arrays],
        out_specs=[full(a.shape) for a in arrays],
        out_shape=[jax.ShapeDtypeStruct(a.shape, a.dtype) for a in arrays],
        compiler_params=pltpu.CompilerParams(vmem_limit_bytes=8 * 1024 * 1024),
        name="copies",
    )(*arrays)


def after(a, first):
    return together_at([a, first])[0]


class Chain:
    def __init__(self, keep, send):
        count = lax.axis_size("seq")
        whole = []
        shift = 2
        while 1 << shift < count:
            whole.append(("whole", shift))
            shift += 1
        self.plan = [("core", 0), ("one", 0), ("two", 0), ("half", 1)] + whole + [("back", 1), ("end", 0)]
        self.at = 0
        self.kept = [keep]
        self.sends = [send]
        self.rows, self.columns = keep.shape[1:]

    def done(self):
        return self.at == len(self.plan)

    def start(self):
        if self.done():
            return
        kind, shift = self.plan[self.at]

        def along_seq(a):
            count = lax.axis_size("seq")
            return lax.ppermute(a, "seq", [(i, i ^ (1 << shift)) for i in range(count)])

        if kind == "core":
            ways = [to_core]
        elif kind == "one":
            ways = [to_chip, along_seq]
        elif kind == "two":
            ways = [along_seq, to_chip]
        else:
            ways = [along_seq]
        self.flights = [way(a) for way, a in zip(ways, self.sends)]

    def landing(self):
        kind, _ = self.plan[self.at]
        q, c = self.rows // 4, self.columns
        shapes = {
            "core": [(2 * q, c), (2, q, c)] * 2, "one": [(q, c)] * 4, "two": [(q, c)] * 2,
            "half": [(q, c)], "whole": [(q, c)], "back": [(2 * q, c)], "end": [(4 * q, c)],
        }[kind]

        def body(info_ref, ins, outs):
            bx, by, bz = (info_ref[0] >> 1) & 1, info_ref[1] & 1, (info_ref[1] >> 1) & 1

            def at(i, base=0):
                return pl.ds(pl.multiple_of(base + i * q, 16), q)

            if kind == "core":
                keep, got = ins
                for out, i in ((outs[0], bx), (outs[2], 1 - bx)):
                    out[...] = sum_of(keep[i, : 2 * q, :], got[i, : 2 * q, :])
                for out, i in ((outs[1], by), (outs[3], 1 - by)):
                    out[...] = sum_of(keep[:, at(i, 2 * q), :], got[:, at(i, 2 * q), :])
            elif kind == "one":
                for out, i in ((outs[0], by), (outs[2], 1 - by)):
                    out[...] = sum_of(ins[0][at(i), :], ins[2][at(i), :])
                for out, i in ((outs[1], bx), (outs[3], 1 - bx)):
                    out[...] = sum_of(ins[1][i], ins[3][i])
            elif kind == "two":
                first = sum_of(ins[0][...], ins[2][...])
                second = sum_of(ins[1][...], ins[3][...])
                put_by(bz, outs, first, second, slice(0, c))
            elif kind == "back":
                outs[0][at(bz), :] = ins[0][...]
                outs[0][at(1 - bz), :] = ins[1][...]
            elif kind == "end":
                for half in range(2):
                    outs[0][at(by, 2 * q * half), :] = ins[0][half * q : (half + 1) * q, :]
                    outs[0][at(1 - by, 2 * q * half), :] = ins[1][half * q : (half + 1) * q, :]
            else:
                outs[0][...] = sum_of(ins[0][...], ins[1][...])

        return self.kept + self.flights, shapes, body

    def landed(self, outs):
        kind, _ = self.plan[self.at]
        self.at += 1
        pairs = {"core": 2, "one": 2, "two": 1}.get(kind)
        self.kept = outs[:pairs] if pairs else outs
        self.sends = outs[pairs:] if pairs else outs


def put_by(bit, outs, first, second, cols):
    @pl.when(bit == 0)
    def _():
        outs[0][:, cols] = first
        outs[1][:, cols] = second

    @pl.when(bit != 0)
    def _():
        outs[0][:, cols] = second
        outs[1][:, cols] = first


class Joined(Chain):
    def __init__(self, first, second):
        self.both = (first, second)
        self.plan, self.at, self.rows = second.plan, second.at, second.rows
        self.columns = first.columns + second.columns

    def landing(self):
        if self.both is None:
            return Chain.landing(self)
        plans = [c.landing() for c in self.both]
        q = self.rows // 4

        def body(info_ref, ins, outs):
            bz = (info_ref[1] >> 1) & 1
            start = 0
            for i, c in enumerate(self.widths):
                a = ins[4 * i : 4 * i + 4]
                first = sum_of(a[0][...], a[2][...])
                second = sum_of(a[1][...], a[3][...])
                put_by(bz, outs, first, second, slice(start, start + c))
                start += c

        self.widths = [c.columns for c in self.both]
        return plans[0][0] + plans[1][0], [(q, self.columns)] * 2, body

    def landed(self, outs):
        self.both = None
        Chain.landed(self, outs)


def sum_of(a, b):
    return (a.astype(F32) + b.astype(F32)).astype(BF)


def nothing(*refs):
    pass


def together_at(arrays, seen=()):
    hbm = pl.BlockSpec(memory_space=pl.ANY)
    return pl.pallas_call(
        nothing,
        in_specs=[hbm] * (len(arrays) + len(seen)),
        out_specs=[hbm] * len(arrays),
        out_shape=[jax.ShapeDtypeStruct(a.shape, a.dtype) for a in arrays],
        input_output_aliases={i: i for i in range(len(arrays))},
        compiler_params=pltpu.CompilerParams(vmem_limit_bytes=1024 * 1024),
        name="boundary",
    )(*arrays, *seen)


def boundary(info, token, landing=(), starting=(), also=()):
    landing = [c for c in landing if not c.done()]
    plans = [c.landing() for c in landing]
    args = [info] + [a for p in plans for a in p[0]]
    through = [c.sends[0] for c in starting] + list(also) + [token]
    shapes = [jax.ShapeDtypeStruct(t, BF) for p in plans for t in p[1]]
    count = len(args)

    def body(*refs):
        ins = list(refs[1:count])
        outs = list(refs[count + len(through) :])
        for operands, shapes_i, land in plans:
            land(refs[0], [ins.pop(0) for _ in operands], [outs.pop(0) for _ in shapes_i])

    hbm = pl.BlockSpec(memory_space=pl.ANY)
    outs = pl.pallas_call(
        body,
        grid=(1,),
        in_specs=[smem()] + [full(a.shape) for a in args[1:]] + [hbm] * len(through),
        out_specs=[full(t.shape) for t in shapes] + [hbm] * len(through),
        out_shape=shapes + [jax.ShapeDtypeStruct(a.shape, a.dtype) for a in through],
        input_output_aliases={count + i: len(shapes) + i for i in range(len(through))},
        compiler_params=pltpu.CompilerParams(vmem_limit_bytes=16 * 1024 * 1024),
        cost_estimate=cost(1),
        name="land",
    )(*args, *through)
    outs = list(outs)
    for c, p in zip(landing, plans):
        c.landed([outs.pop(0) for _ in p[1]])
    for c in starting:
        c.sends = [outs.pop(0)]
    waits = [outs[-1]]
    for c in landing + list(starting):
        waits.append(c.sends[0])
        c.start()
    return outs[:-1], tuple(waits)


def neighbours(count):
    up = [(i, i + 1) for i in range(count - 1)]
    return up, [(j, i) for i, j in up]


def shards(
    hidden_in, cotangent, block_seq, block_place, attn_in, attn_out, ffn_in, ffn_out, norm_attn, norm_ffn,
    m_attn_in, m_attn_out, m_ffn_in, m_ffn_out, m_norm_attn, m_norm_ffn,
    v_attn_in, v_attn_out, v_ffn_in, v_ffn_out, v_norm_attn, v_norm_ffn,
):
    x = hidden_in[0]
    cot = cotangent[0]
    n = x.shape[0]
    ext = n + 2 * HALF
    w = lax.axis_index("wshard")
    count = lax.axis_size("seq")
    at = lax.axis_index("seq")
    up, down = neighbours(count)

    far = to_chip(attn_in)
    mate = to_core(attn_in)
    gain_own = jnp.stack([norm_attn, norm_ffn])
    gain_far, gain_mate = to_chip(gain_own), to_core(gain_own)
    x_low, x_high = lax.ppermute(x[n - HALF :], "seq", up), lax.ppermute(x[:HALF], "seq", down)
    attn_out_own, down_a, down_b = copies([attn_out, ffn_out[: D // 4], ffn_out[D // 4 :]])
    info = jnp.concatenate([jnp.stack([w, at]).astype(jnp.int32), block_seq[0], block_place[0]])
    some, rest = D // 4, FF // 4 - D // 4

    def units(start, first, size):
        return [ffn_in[:, start + s * (FF // 4) + first :][:, :size] for s in range(4)]

    in_g = jnp.concatenate(units(0, 0, some), axis=1)
    in_u = jnp.concatenate(units(FF, 0, some), axis=1)
    in_b = jnp.concatenate(units(0, some, rest) + units(FF, some, rest), axis=1)
    out_mate, g_mate, u_mate, da_mate, db_mate, b_mate = (to_core(a) for a in (attn_out_own, in_g, in_u, down_a, down_b, in_b))

    g_half = lax.dynamic_slice_in_dim(in_g, (at & 1) * (D // 8), D // 8, 0)
    (token,) = together_at(
        [jnp.zeros((8, 128), F32)], [x_low, x_high, info, mate, out_mate, g_mate, u_mate, da_mate, db_mate, b_mate]
    )
    far, g_half, attn_out_own, token = together_at([far, g_half, attn_out_own, token], [gain_far, gain_mate])
    farmate = to_core(far)
    out_far = to_chip(attn_out_own)
    g_mine = to_chip(g_half)
    attn_parts = attn_in, mate, far, farmate
    gains = gain_own, gain_mate, gain_far, to_core(gain_far)
    nt, q, k, v, cos, sin, gain, token = qkv_call(info, x, x_low, x_high, gains, attn_parts)
    out_far, g_mine, in_u, token = together_at([out_far, g_mine, in_u, token])
    out_farmate = to_core(out_far)
    out_farmate, in_u, down_a, token = together_at([out_farmate, in_u, down_a, token])
    u_far = to_chip(in_u)
    da_far = to_chip(down_a)
    g_other = lax.ppermute(g_mine, "seq", [(i, i ^ 1) for i in range(count)])
    out_parts = attn_out, out_mate, out_far, out_farmate
    mixed, middle, n2, out_w, lse, token = attend_call(info, q, k, v, x, out_parts, gain, deps=(token,))
    g_other, u_far, da_far, in_b, down_b, token = together_at([g_other, u_far, da_far, in_b, down_b, token])
    b_far = to_chip(in_b)
    db_far = to_chip(down_b)
    gate_parts = in_g, g_mate, g_mine, g_other, to_core(g_mine), to_core(g_other)
    up_parts = in_u, u_mate, u_far, to_core(u_far)
    down_parts = down_a, da_mate, da_far, to_core(da_far)
    pout, pgn, keep, send, token = ffn_a_call(info, n2, cot, gate_parts, up_parts, down_parts, deps=(token,))
    chain_a = Chain(keep, send)
    (b_far, db_far), deps = boundary(info, token, (), (chain_a,), (b_far, db_far))
    b_parts = in_b, b_mate, b_far, to_core(b_far)
    db_parts = down_b, db_mate, db_far, to_core(db_far)
    _, deps = boundary(info, deps[0], (chain_a,))
    block_out, gmid, gmix, keep, send, token = ffn_b_call(
        info, n2, cot, b_parts, db_parts, pout, pgn, middle, mixed, out_w, gain, deps=deps
    )
    chain_b = Chain(keep, send)
    grads, pieces = (), ()

    def back(p, at, width, deps):
        nonlocal grads, pieces
        if at == 0:
            pieces = ()
        out = attend_back_call(p, at, width, info, q, k, v, gmix, mixed, lse, cos, sin, nt, grads, pieces, deps)
        grads, pieces = out[:3], out[3:5]
        return out[5]

    _, deps = boundary(info, token, (chain_a,), (chain_b,))
    token = back(0, 0, 2 * QUAD, deps)
    _, deps = boundary(info, token, (chain_a, chain_b))
    token = back(1, 1, 2 * QUAD, deps)
    chain_c = Chain(*pieces)
    _, deps = boundary(info, token, (chain_a, chain_b), (chain_c,))
    token = back(2, 0, QUAD, deps)
    chain_d = Chain(*pieces)
    _, deps = boundary(info, token, (chain_b, chain_c), (chain_d,))
    rims = [jnp.concatenate([a[r] for a in grads[1:]], axis=1) for r in (slice(0, HALF), slice(n + HALF, ext))]
    rims, deps = boundary(info, deps[0], (chain_a, chain_b, chain_c, chain_d), (), rims)
    rims = lax.ppermute(rims[1], "seq", up), lax.ppermute(rims[0], "seq", down)
    rims, deps = boundary(info, deps[0], (chain_a, chain_b, chain_d), (), rims)
    grad_in, token = last_call(info, x, grads, rims, gmid, attn_parts, gain, deps=deps)
    chain_c = Joined(chain_c, chain_d)
    chains = (chain_a, chain_b, chain_c)
    while chain_c.at < len(chain_c.plan) - 1:
        _, deps = boundary(info, token, chains)
        token = deps[0]
    sum_a, sum_b = chain_a.kept[0], chain_b.kept[0]

    r = D // 4
    third = FF // 12

    def block_rows(a, first, step, columns):
        return a, (step, columns), lambda i: (first // step + i, 0)

    def lay_out(i, info_ref, refs, out):
        for b, ref in enumerate(refs):
            out[:, b * WIDE : (b + 1) * WIDE] = ref[...].astype(F32)

    res_attn_out = adam_call(
        info, lay_out, [block_rows(sum_b, (2 + b) * r, r // 2, WIDE) for b in range(2)], attn_out, m_attn_out, v_attn_out, r // 2
    )

    def lay_down(i, info_ref, refs, out):
        for b in range(2):
            out[:, b * WIDE : (b + 1) * WIDE] = jnp.where(i < 2, refs[b][...], refs[2 + b][...]).astype(F32)

    res_ffn_out = adam_call(
        info, lay_down,
        [(sum_a, (third, WIDE), lambda i, b=b: ((4 + b) * (r // third) + jnp.minimum(i, 1), 0)) for b in range(2)]
        + [(sum_b, (third, WIDE), lambda i, b=b: (4 * (r // third) + b, 0)) for b in range(2)],
        ffn_out, m_ffn_out, v_ffn_out, third,
    )

    def lay_units(i, info_ref, refs, out):
        for half in range(2):
            of_a = jnp.concatenate([refs[2 * half][...], refs[2 * half + 1][...]], axis=1).astype(F32)
            of_b = refs[4 + half][...].astype(F32)
            for s in range(4):
                start = half * FF + s * (some + rest)
                out[:, start : start + some] = of_a[:, s * some : (s + 1) * some]
                out[:, start + some : start + some + rest] = of_b[:, s * rest : (s + 1) * rest]

    step = r // 4
    res_ffn_in = adam_call(
        info, lay_units,
        [block_rows(sum_a, b * r, step, WIDE) for b in range(4)] + [block_rows(sum_b, b * r, step, WIDE) for b in range(2)],
        ffn_in, m_ffn_in, v_ffn_in, step, deps=(token,),
    )

    def row_of(part, i):
        at = part * r + i * step
        return at // (2 * r * 3 // 4), (at % (2 * r * 3 // 4)) // (r * 3 // 4), at % (r * 3 // 4)

    def source(part):
        def at(i):
            half, _, row = row_of(part, i)
            return (half * (r * 3 // 4) + row) // step, 0

        return at

    def lay_parts(i, info_ref, refs, out):
        for part in range(3):
            mine = row_of(part, i)[1] == (info_ref[1] & 1)
            out[:, part * D : (part + 1) * D] = jnp.where(mine, refs[part][...], refs[3 + part][...]).astype(F32)

    res_attn_in = adam_call(
        info, lay_parts,
        [(a, (step, D), source(part)) for a in (chain_c.kept[0], chain_c.flights[0]) for part in range(3)],
        attn_in, m_attn_in, v_attn_in, step,
    )
    results = [res_attn_in, res_attn_out, res_ffn_in, res_ffn_out]
    for res, own_gain, m, v_ in ((res_attn_in, norm_attn, m_norm_attn, v_norm_attn), (res_ffn_in, norm_ffn, m_norm_ffn, v_norm_ffn)):
        wide = own_gain.astype(F32)
        g = res[4][:, 0] / wide
        results.append((g,) + adam(wide, g, m, v_, 0.0))
    return (block_out[None], grad_in[None]) + tuple(res[i] for i in range(4) for res in results)


def solution(mesh):
    big = P("wshard", "seq", None)
    mat = P("wshard", None)
    vec = P("wshard")
    group = (mat, mat, mat, mat, vec, vec)
    in_specs = (big, big, mat, mat) + group * 3
    out_specs = (big, big) + group * 4
    return jax.shard_map(shards, mesh=mesh, in_specs=in_specs, out_specs=out_specs, check_vma=False)
```

```python
import functools

import jax
import jax.numpy as jnp
import numpy as np
from jax import lax
from jax.experimental import pallas as pl
from jax.experimental.pallas import tpu as pltpu
from jax.sharding import PartitionSpec as P

D = 768
FF = 1152
HEADS = 12
HD = 64
HALF = 64
STEP = 10
PAIR = 2 * HD
QB = 128
TILE = 256
ATILE = 512
WIDE = 384
ADAM_MB = 60
QUAD = 4 * HD

NORM_EPS = 1e-05
BETA_ONE = 0.9
BETA_TWO = 0.98
LEARN_RATE = 0.05
WEIGHT_DECAY = 0.01
ADAM_EPS = 1e-06
NEG_FILL = -1e30
THETA = 10000.0
BF = jnp.bfloat16
F32 = jnp.float32


def dot(left, right):
    return lax.dot_general(left, right, (((1,), (0,)), ((), ())), preferred_element_type=F32)


def dot_bt(left, right):
    return lax.dot_general(left, right, (((1,), (1,)), ((), ())), preferred_element_type=F32)


def dot_at(left, right):
    return lax.dot_general(left, right, (((0,), (0,)), ((), ())), preferred_element_type=F32)


def call(body, args, in_specs, out_specs, out_shape, megabytes, deps=(), aliases=None, **kw):
    first = len(args)
    n_out = len(out_shape)

    def wrapped(*refs):
        refs = refs[:first] + refs[first + len(deps) :]
        token = refs[first + n_out]
        token[...] = jnp.zeros_like(token)
        body(*refs[: first + n_out], *refs[first + n_out + 1 :])

    return pl.pallas_call(
        wrapped,
        in_specs=list(in_specs) + [pl.BlockSpec(memory_space=pl.ANY)] * len(deps),
        out_specs=list(out_specs) + [full((8, 128))],
        out_shape=list(out_shape) + [jax.ShapeDtypeStruct((8, 128), F32)],
        input_output_aliases=aliases or {},
        compiler_params=pltpu.CompilerParams(
            dimension_semantics=("arbitrary",), vmem_limit_bytes=megabytes * 1024 * 1024
        ),
        **kw,
    )(*args, *deps)


def full(shape):
    return pl.BlockSpec(shape, lambda i: (0,) * len(shape))


def rows(tile, width):
    return pl.BlockSpec((tile, width), lambda i: (i, 0))


def cost(microseconds):
    return pl.CostEstimate(flops=int(microseconds * 1.1e9), bytes_accessed=0, transcendentals=0)


def normalize(x):
    mean = jnp.mean(x, axis=-1, keepdims=True)
    centered = x - mean
    var = jnp.mean(centered * centered, axis=-1, keepdims=True)
    r = lax.rsqrt(var + NORM_EPS)
    return centered * r, r


def signed(sin):
    first = lax.broadcasted_iota(jnp.int32, sin.shape, 1) % HD < HD // 2
    zero = jnp.zeros_like(sin)
    return jnp.where(first, -sin, zero), jnp.where(first, zero, sin)


def turn(u, cos, sin_left, sin_right):
    return u * cos + pltpu.roll(u, PAIR - HD // 2, 1) * sin_left + pltpu.roll(u, HD // 2, 1) * sin_right


def blocks_of(info_ref):
    return (info_ref.shape[0] - 2) // 2


def sides(info_ref):
    count = blocks_of(info_ref)
    at = info_ref[1]
    own = info_ref[2 + at]
    left = (at > 0) & (info_ref[2 + jnp.maximum(at - 1, 0)] == own)
    right = (at < count - 1) & (info_ref[2 + jnp.minimum(at + 1, count - 1)] == own)
    return left, right


def bias_of(b, last, left, right):
    shape = (QB + 2 * HALF, QB)
    key = lax.broadcasted_iota(jnp.int32, shape, 0)
    off = key - lax.broadcasted_iota(jnp.int32, shape, 1)
    low = jnp.where((b > 0) | left, 0, HALF)
    high = jnp.where((b < last) | right, QB + 2 * HALF, QB + HALF)
    ok = (off >= 0) & (off <= 2 * HALF) & (key >= low) & (key < high)
    return jnp.where(ok, 0.0, NEG_FILL)


def lay(w, parts, out_ref, bit=0):
    r = out_ref.shape[0] // 4
    for i, ref in enumerate(parts):
        start = (w ^ i) * r
        if isinstance(ref, tuple):
            half = r // 2
            for j, a in enumerate(ref):
                out_ref[pl.ds(pl.multiple_of(start + (bit ^ j) * half, 16), half), :] = a[...]
        else:
            out_ref[pl.ds(pl.multiple_of(start, 32), r), :] = ref[...]


def deal(w, acc, cols, keep_ref, send_ref, at):
    r = acc.shape[0] // 4
    c = w & 1
    for x in range(2):
        keep_ref[x, at : at + r, :] = acc[pl.ds(pl.multiple_of((2 * x + c) * r, 32), r), cols].astype(BF)
        send_ref[x, at : at + r, :] = acc[pl.ds(pl.multiple_of((2 * x + 1 - c) * r, 32), r), cols].astype(BF)


def smem():
    return pl.BlockSpec(memory_space=pltpu.SMEM)


def piece(n_rows):
    return jax.ShapeDtypeStruct((2, n_rows, WIDE), BF)


def qkv_body(info_ref, x_ref, low_ref, high_ref, gain_a, gain_b, gain_c, gain_d, wa, wb, wc, wd, far_ref, near_ref,
             nt_ref, q_ref, k_ref, v_ref, cos_ref, sin_ref, gain_ref, w_ref, x_ext):
    t = q_ref.shape[0]
    i = pl.program_id(0)

    @pl.when(i == 0)
    def _():
        lay(info_ref[0], (wa, wb, wc, wd), w_ref)
        end = x_ext.shape[0] - HALF
        x_ext[:HALF, :] = low_ref[...]
        x_ext[HALF:end, :] = x_ref[...]
        x_ext[end:, :] = high_ref[...]
        r = D // 4
        for p, ref in enumerate((gain_a, gain_b, gain_c, gain_d)):
            gains = ref[...].astype(F32)
            for owner in range(4):

                @pl.when((info_ref[0] ^ p) == owner)
                def _():
                    gain_ref[:2, owner * r : (owner + 1) * r] = gains


    place = info_ref[2 + blocks_of(info_ref) + info_ref[1]]
    c2, s2 = far_ref[0, pl.ds(place, 1), :], far_ref[1, pl.ds(place, 1), :]
    c1, s1 = near_ref[0], near_ref[1]
    cos = c1 * c2 - s1 * s2
    sin = s1 * c2 + c1 * s2
    cos_ref[...] = cos
    sin_ref[...] = sin
    sl, sr = signed(sin)
    n, _ = normalize(x_ext[pl.ds(pl.multiple_of(i * t, 128), t), :].astype(F32))
    normed = (n * gain_ref[0:1, :]).astype(BF)
    nt_ref[...] = normed.T
    for part, ref, scale in ((0, q_ref, HD**-0.5), (1, k_ref, 1.0)):
        u = dot(normed, w_ref[:, part * D : (part + 1) * D])
        for p in range(D // PAIR):
            r = turn(u[:, p * PAIR : (p + 1) * PAIR], cos, sl, sr)
            ref[:, p * PAIR : (p + 1) * PAIR] = (r * scale).astype(BF)
    v_ref[...] = dot(normed, w_ref[:, 2 * D :]).astype(BF)


def angle_tables(n, ext):
    freq = THETA ** (-2.0 * (np.arange(PAIR) % (HD // 2)) / HD)

    def table(positions):
        angle = positions[:, None] * freq[None, :]
        return jnp.asarray(np.stack([np.cos(angle), np.sin(angle)]).astype(np.float32))

    return table(np.arange(4.0) * n), table(np.arange(float(ext)) - HALF)


def qkv_call(info, x, low, high, gains, w_parts, deps=()):
    n = x.shape[0]
    ext = n + 2 * HALF
    t = ext // 3
    out = jax.ShapeDtypeStruct((ext, D), BF)
    table = jax.ShapeDtypeStruct((ext, PAIR), F32)
    far, near = angle_tables(n, ext)
    return call(
        qkv_body,
        [info, x, low, high, *gains, *w_parts, far, near],
        grid=(3,),
        in_specs=[smem(), full((n, D)), full((HALF, D)), full((HALF, D))] + [full((2, D // 4))] * 4 + [full((D // 4, 3 * D))] * 4
        + [full(far.shape), pl.BlockSpec((2, t, PAIR), lambda i: (0, i, 0))],
        out_specs=[pl.BlockSpec((D, t), lambda i: (0, i))] + [rows(t, D)] * 3 + [rows(t, PAIR)] * 2 + [full((8, D))],
        out_shape=[jax.ShapeDtypeStruct((D, ext), BF)] + [out] * 3 + [table] * 2 + [jax.ShapeDtypeStruct((8, D), F32)],
        scratch_shapes=[pltpu.VMEM((D, 3 * D), BF), pltpu.VMEM((ext, D), BF)],
        megabytes=20,
        deps=deps,
        cost_estimate=cost(9),
        name="qkv",
    )


def apart(u):
    head = lax.broadcasted_iota(jnp.int32, u.shape, 1) // HD
    zero = jnp.zeros_like(u)
    return jnp.concatenate([jnp.where(head == h, u, zero) for h in range(4)], axis=0)


def together(u):
    r = u.shape[0] // 4
    head = lax.broadcasted_iota(jnp.int32, (r, QUAD), 1) // HD
    out = u[:r]
    for h in range(1, 4):
        out = jnp.where(head == h, u[h * r : (h + 1) * r], out)
    return out


def repeat(u):
    return jnp.concatenate([u] * 4, axis=1)


def attend_body(info_ref, q_ref, k_ref, v_ref, x_ref, wa, wb, wc, wd, gain_ref,
                mixed_ref, middle_ref, n2_ref, w_ref, lse_ref):
    i = pl.program_id(0)
    last = pl.num_programs(0) * (ATILE // QB) - 1
    left, right = sides(info_ref)

    @pl.when(i == 0)
    def _():
        lay(info_ref[0], (wa, wb, wc, wd), w_ref)

    for s in range(ATILE // QB):
        b = i * (ATILE // QB) + s
        start = pl.multiple_of(b * QB, QB)
        bias = repeat(bias_of(b, last, left, right))
        for g in range(D // QUAD):
            cols = slice(g * QUAD, (g + 1) * QUAD)
            win = pl.ds(start, QB + 2 * HALF)
            q4 = apart(q_ref[pl.ds(start + HALF, QB), cols])
            scores = dot_bt(k_ref[win, cols], q4) + bias
            most = jnp.max(scores, axis=0, keepdims=True)
            e = jnp.exp(scores - most)
            total = jnp.sum(e, axis=0, keepdims=True)
            probs = (e * (1.0 / total)).astype(BF)
            o = together(dot_at(probs, v_ref[win, cols]))
            mixed_ref[s * QB : (s + 1) * QB, cols] = o.astype(BF)
            lse = most + jnp.log(total)
            for h in range(4):
                lse_ref[g, h : h + 1, s * QB : (s + 1) * QB] = lse[:, h * QB : (h + 1) * QB]
    middle = x_ref[...].astype(F32) + dot(mixed_ref[...], w_ref[...])
    middle_ref[...] = middle.astype(BF)
    n, _ = normalize(middle)
    n2_ref[...] = (n * gain_ref[1:2, :]).astype(BF)


def attend_call(info, q, k, v, x, w_parts, gain, deps=()):
    n = x.shape[0]
    ext = q.shape[0]
    groups = D // QUAD
    return call(
        attend_body,
        [info, q, k, v, x, *w_parts, gain],
        grid=(n // ATILE,),
        in_specs=[smem()] + [full((ext, D))] * 3 + [rows(ATILE, D)] + [full((D // 4, D))] * 4 + [full((8, D))],
        out_specs=[rows(ATILE, D)] * 3 + [full((D, D)), pl.BlockSpec((groups, 4, ATILE), lambda i: (0, 0, i))],
        out_shape=[
            jax.ShapeDtypeStruct((n, D), BF), jax.ShapeDtypeStruct((n, D), BF), jax.ShapeDtypeStruct((n, D), BF),
            jax.ShapeDtypeStruct((D, D), BF), jax.ShapeDtypeStruct((groups, 4, n), F32),
        ],
        megabytes=16,
        deps=deps,
        cost_estimate=cost(11),
        name="attend",
    )


def hidden(n2, cot, both, wd):
    gate_up = jnp.concatenate([dot(n2, w[...]) for w in both], axis=1)
    half = gate_up.shape[1] // 2
    gate, up = gate_up[:, :half], gate_up[:, half:]
    ga = dot_bt(cot, wd)
    phi = 0.5 + 0.5 * lax.erf(gate * (2.0**-0.5))
    gelu = gate * phi
    act = (gelu * up).astype(BF)
    slope = phi + gate * (jnp.exp(-0.5 * gate * gate) * 0.3989422804014327)
    grads = jnp.concatenate([(ga * up * slope).astype(BF), (ga * gelu).astype(BF)], axis=1)
    out = dot(act, wd)
    size = grads.shape[1] // len(both)
    gn = sum(dot_bt(grads[:, i * size : (i + 1) * size], w[...]) for i, w in enumerate(both))
    return act, grads, out, gn


def ffn_a_body(info_ref, n2_ref, cot_ref, ga, gb, gc, gd, ge, gf, ua, ub, uc, ud, oa, ob, oc, od,
               out_ref, gn_ref, keep_ref, send_ref, wg_ref, wu_ref, wd_ref, acc, ad):
    i = pl.program_id(0)

    @pl.when(i == 0)
    def _():
        lay(info_ref[0], (ga, gb, (gc, gd), (ge, gf)), wg_ref, info_ref[1] & 1)
        lay(info_ref[0], (ua, ub, uc, ud), wu_ref)
        lay(info_ref[0], (oa, ob, oc, od), wd_ref)
        acc[...] = jnp.zeros_like(acc)
        ad[...] = jnp.zeros_like(ad)

    n2 = n2_ref[...]
    cot = cot_ref[...]
    nt = n2.T
    act, grads, total_out, total_gn = hidden(n2, cot, (wg_ref, wu_ref), wd_ref[...])
    acc[...] += dot(nt, grads)
    ad[...] += dot_at(act, cot)
    out_ref[...] = total_out.astype(BF)
    gn_ref[...] = total_gn.astype(BF)

    @pl.when(i == pl.num_programs(0) - 1)
    def _():
        for b in range(4):
            deal(info_ref[0], acc, slice(b * WIDE, (b + 1) * WIDE), keep_ref, send_ref, b * D // 4)
        for b in range(2):
            deal(info_ref[0], ad, slice(b * WIDE, (b + 1) * WIDE), keep_ref, send_ref, (4 + b) * D // 4)


def ffn_a_call(info, n2, cot, gate_parts, up_parts, down_parts, deps=()):
    n = n2.shape[0]
    part = jax.ShapeDtypeStruct((n, D), BF)
    size = 6 * D // 4
    return call(
        ffn_a_body,
        [info, n2, cot, *gate_parts, *up_parts, *down_parts],
        grid=(n // TILE,),
        in_specs=[smem()] + [rows(TILE, D)] * 2 + [full((D // 4, D))] * 2 + [full((D // 8, D))] * 4
        + [full((D // 4, D))] * 8,
        out_specs=[rows(TILE, D)] * 2 + [full((2, size, WIDE))] * 2,
        out_shape=[part, part, piece(size), piece(size)],
        scratch_shapes=[pltpu.VMEM((D, D), BF)] * 3 + [pltpu.VMEM((D, 2 * D), F32), pltpu.VMEM((D, D), F32)],
        megabytes=24,
        deps=deps,
        cost_estimate=cost(18),
        name="ffn_a",
    )


def norm_back(grad, n, r, gain):
    e = grad * gain
    return r * (e - jnp.mean(e, axis=-1, keepdims=True) - n * jnp.mean(e * n, axis=-1, keepdims=True))


def ffn_b_body(info_ref, n2_ref, cot_ref, ia, ib, ic, id_, oa, ob, oc, od, pout_ref, pgn_ref, mid_ref, mixed_ref, wo_ref, gain_ref,
               out_ref, gmid_ref, gmix_ref, keep_ref, send_ref, w_ref, wd_ref, acc, ad, ao):
    i = pl.program_id(0)

    @pl.when(i == 0)
    def _():
        lay(info_ref[0], (ia, ib, ic, id_), w_ref)
        lay(info_ref[0], (oa, ob, oc, od), wd_ref)
        acc[...] = jnp.zeros_like(acc)
        ao[...] = jnp.zeros_like(ao)
        ad[...] = jnp.zeros_like(ad)

    n2 = n2_ref[...]
    cot = cot_ref[...]
    act, grads, out, gn = hidden(n2, cot, (w_ref,), wd_ref[...])
    acc[...] += dot(n2.T, grads)
    ad[...] += dot_at(act, cot)
    middle = mid_ref[...].astype(F32)
    out_ref[...] = (middle + pout_ref[...].astype(F32) + out).astype(BF)
    n, r = normalize(middle)
    branch = (cot.astype(F32) + norm_back(pgn_ref[...].astype(F32) + gn, n, r, gain_ref[1:2, :])).astype(BF)
    gmid_ref[...] = branch
    gmix_ref[...] = dot_bt(branch, wo_ref[...]).astype(BF)
    ao[...] += dot_at(mixed_ref[...], branch)

    @pl.when(i == pl.num_programs(0) - 1)
    def _():
        w = info_ref[0]
        r = D // 4
        for b in range(2):
            cols = slice(b * WIDE, (b + 1) * WIDE)
            deal(w, acc, cols, keep_ref, send_ref, b * r)
            deal(w, ao, cols, keep_ref, send_ref, (2 + b) * r)
            deal(w, ad, cols, keep_ref, send_ref, 4 * r + b * r // 2)


def ffn_b_call(info, n2, cot, in_parts, down_parts, pout, pgn, middle, mixed, wo, gain, deps=()):
    n = n2.shape[0]
    size = 5 * D // 4
    return call(
        ffn_b_body,
        [info, n2, cot, *in_parts, *down_parts, pout, pgn, middle, mixed, wo, gain],
        grid=(n // TILE,),
        in_specs=[smem()] + [rows(TILE, D)] * 2 + [full((D // 4, D))] * 4 + [full((WIDE // 4, D))] * 4
        + [rows(TILE, D)] * 4 + [full((D, D)), full((8, D))],
        out_specs=[rows(TILE, D)] * 3 + [full((2, size, WIDE))] * 2,
        out_shape=[jax.ShapeDtypeStruct((n, D), BF)] * 3 + [piece(size), piece(size)],
        scratch_shapes=[pltpu.VMEM((D, D), BF), pltpu.VMEM((WIDE, D), BF),
                        pltpu.VMEM((D, D), F32), pltpu.VMEM((WIDE, D), F32), pltpu.VMEM((D, D), F32)],
        megabytes=24,
        deps=deps,
        cost_estimate=cost(14),
        name="ffn_b",
    )


def attend_back_body(info_ref, q_ref, k_ref, v_ref, g_ref, mixed_ref, lse_ref, cos_ref, sin_ref, nt_ref, *rest):
    dq_ref, dk_ref, dv_ref, keep_ref, send_ref, ak, av, aw = rest[-8:]
    ext = ak.shape[0]
    blocks = (ext - 2 * HALF) // QB
    left, right = sides(info_ref)
    ak[...] = jnp.zeros_like(ak)
    av[...] = jnp.zeros_like(av)
    zero = jnp.zeros((HALF, QUAD), BF)
    dq_ref[:HALF, :] = zero
    dq_ref[ext - HALF :, :] = zero
    prod = mixed_ref[...].astype(F32) * g_ref[...].astype(F32)
    head = lax.broadcasted_iota(jnp.int32, (8, QUAD), 1) // HD
    pick = jnp.where(head == lax.broadcasted_iota(jnp.int32, (8, QUAD), 0), 1.0, 0.0).astype(BF)
    high = prod.astype(BF)
    delta = dot_bt(pick, high) + dot_bt(pick, (prod - high.astype(F32)).astype(BF))

    def of_heads(a, start):
        return jnp.concatenate([a[h : h + 1, start : start + QB] for h in range(4)], axis=1)

    def unturn(u, at):
        cos = cos_ref[at, :]
        sl, sr = signed(-sin_ref[at, :])
        return jnp.concatenate([turn(u[:, c : c + PAIR], cos, sl, sr) for c in (0, PAIR)], axis=1).astype(BF)

    for b in range(blocks):
        start = b * QB
        win = slice(start, start + QB + 2 * HALF)
        here = slice(start + HALF, start + HALF + QB)
        bias = repeat(bias_of(b, blocks - 1, left, right))
        q4 = apart(q_ref[here, :])
        g4 = apart(g_ref[start : start + QB, :])
        kw = k_ref[win, :]
        probs = jnp.exp(dot_bt(kw, q4) + bias - of_heads(lse_ref[0], start))
        ds = (probs * (dot_bt(v_ref[win, :], g4) - of_heads(delta, start))).astype(BF)
        ak[win, :] += dot(ds, q4)
        av[win, :] += dot(probs.astype(BF), g4)
        dq_ref[here, :] = unturn(together(dot_at(ds, kw)) * HD**-0.5, here)
    dk_ref[...] = unturn(ak[...], slice(0, ext))
    dv_ref[...] = av[...].astype(BF)
    for part, ref in enumerate((dq_ref, dk_ref, dv_ref)):
        aw[...] = dot(nt_ref[...], ref[...])
        deal(info_ref[0], aw, slice(0, QUAD), keep_ref, send_ref, part * D // 4)


def attend_back_call(p, at, width, info, q, k, v, g, mixed, lse, cos, sin, nt, sofar, pieces, deps=()):
    n = g.shape[0]
    ext = q.shape[0]
    cols = pl.BlockSpec((ext, QUAD), lambda i: (0, p))
    inner = pl.BlockSpec((n, QUAD), lambda i: (0, p))
    own = jax.ShapeDtypeStruct((ext, D), BF)
    out = jax.ShapeDtypeStruct((2, 3 * D // 4, width), BF)
    args = [info, q, k, v, g, mixed, lse, cos, sin, nt]
    extra = list(sofar) + list(pieces)
    aliases = {}
    for i in range(len(sofar)):
        aliases[len(args) + i] = i
    for i in range(len(pieces)):
        aliases[len(args) + len(sofar) + i] = 3 + i
    mine = pl.BlockSpec((2, 3 * D // 4, QUAD), lambda i: (0, 0, at))
    return call(
        attend_back_body,
        args + extra,
        grid=(1,),
        in_specs=[smem(), cols, cols, cols, inner, inner, pl.BlockSpec((1, 4, n), lambda i: (p, 0, 0))]
        + [full((ext, PAIR))] * 2 + [full((D, ext))] + [pl.BlockSpec(memory_space=pl.ANY)] * len(extra),
        out_specs=[cols] * 3 + [mine] * 2,
        out_shape=[own, own, own, out, out],
        scratch_shapes=[pltpu.VMEM((ext, QUAD), F32), pltpu.VMEM((ext, QUAD), F32), pltpu.VMEM((D, QUAD), F32)],
        aliases=aliases,
        megabytes=12,
        deps=deps,
        cost_estimate=cost(4),
        name="attend_back",
    )


def last_body(info_ref, x_ref, dq_ref, dk_ref, dv_ref, rim_low, rim_high, gmid_ref, wa, wb, wc, wd, gain_ref, gin_ref, w_ref, *both):
    i = pl.program_id(0)
    start = pl.multiple_of(i * TILE, TILE)
    here = pl.ds(start + HALF, TILE)
    ext = dk_ref.shape[0]

    @pl.when(i == 0)
    def _():
        lay(info_ref[0], (wa, wb, wc, wd), w_ref)
        for j, ref in enumerate((dk_ref, dv_ref)):
            cols = slice(j * D, (j + 1) * D)
            both[j][...] = ref[...]
            both[j][HALF : 2 * HALF, :] += rim_low[:, cols]
            both[j][ext - 2 * HALF : ext - HALF, :] += rim_high[:, cols]

    total = jnp.zeros((TILE, D), F32)
    for j, ref in enumerate((dq_ref, *both)):
        total += dot_bt(ref[here, :], w_ref[:, j * D : (j + 1) * D])
    n, r = normalize(x_ref[...].astype(F32))
    gin_ref[...] = (gmid_ref[...].astype(F32) + norm_back(total, n, r, gain_ref[0:1, :])).astype(BF)


def last_call(info, x, grads, rims, gmid, w_parts, gain, deps=()):
    n = gmid.shape[0]
    ext = grads[0].shape[0]
    return call(
        last_body,
        [info, x, *grads, *rims, gmid, *w_parts, gain],
        grid=(n // TILE,),
        in_specs=[smem(), rows(TILE, D)] + [full((ext, D))] * 3 + [full((HALF, 2 * D))] * 2 + [rows(TILE, D)]
        + [full((D // 4, 3 * D))] * 4 + [full((8, D))],
        out_specs=[rows(TILE, D)],
        out_shape=[jax.ShapeDtypeStruct((n, D), BF)],
        scratch_shapes=[pltpu.VMEM((D, 3 * D), BF)] + [pltpu.VMEM((ext, D), BF)] * 2,
        megabytes=16,
        deps=deps,
        cost_estimate=cost(7),
        name="last",
    )


def adam(weight, grad, first_old, second, decay_rate):
    new_first = BETA_ONE * first_old + (1.0 - BETA_ONE) * grad
    new_second = BETA_TWO * second + (1.0 - BETA_TWO) * grad * grad
    root = jnp.sqrt(new_second * (1.0 / (1.0 - BETA_TWO**STEP))) + ADAM_EPS
    change = (-LEARN_RATE / (1.0 - BETA_ONE**STEP)) * (new_first / root)
    if decay_rate:
        change = change - (LEARN_RATE * decay_rate) * weight
    return (new_first, new_second, change)


def adam_call(info, assemble, grads, weight, first, second, rows_at_once, deps=()):
    r, width = weight.shape
    own = rows(rows_at_once, width)
    out = jax.ShapeDtypeStruct((r, width), F32)
    count = len(grads)

    def body(info_ref, *refs):
        blocks = refs[:count]
        w_ref, m_ref, v_ref = refs[count : count + 3]
        g_ref, nm_ref, nv_ref, st_ref, dots_ref = refs[-5:]
        assemble(pl.program_id(0), info_ref, blocks, g_ref)
        g = g_ref[...]
        w = w_ref[...].astype(F32)
        nm_ref[...], nv_ref[...], st_ref[...] = adam(w, g, m_ref[...], v_ref[...], WEIGHT_DECAY)
        dots_ref[...] = jnp.sum(w * g, axis=1, keepdims=True)

    return pl.pallas_call(
        body,
        grid=(r // rows_at_once,),
        in_specs=[smem()] + [pl.BlockSpec(shape, at) for _, shape, at in grads] + [own] * 3
        + [pl.BlockSpec(memory_space=pl.ANY)] * len(deps),
        out_specs=[own] * 4 + [rows(rows_at_once, 1)],
        out_shape=[out] * 4 + [jax.ShapeDtypeStruct((r, 1), F32)],
        compiler_params=pltpu.CompilerParams(dimension_semantics=("arbitrary",), vmem_limit_bytes=ADAM_MB * 1024 * 1024),
        cost_estimate=cost(3),
        name="adam",
    )(info, *[g for g, _, _ in grads], weight, first, second, *deps)


CORES = [(0, 1), (1, 0), (2, 3), (3, 2)]
CHIPS = [(0, 2), (2, 0), (1, 3), (3, 1)]


def to_core(a):
    return lax.ppermute(a, "wshard", CORES)


def to_chip(a):
    return lax.ppermute(a, "wshard", CHIPS)


def copy_body(*refs):
    for a, b in zip(refs[: len(refs) // 2], refs[len(refs) // 2 :]):
        b[...] = a[...]


def copies(arrays):
    return pl.pallas_call(
        copy_body,
        grid=(1,),
        in_specs=[full(a.shape) for a in arrays],
        out_specs=[full(a.shape) for a in arrays],
        out_shape=[jax.ShapeDtypeStruct(a.shape, a.dtype) for a in arrays],
        compiler_params=pltpu.CompilerParams(vmem_limit_bytes=8 * 1024 * 1024),
        name="copies",
    )(*arrays)


def after(a, first):
    return together_at([a, first])[0]


class Chain:
    def __init__(self, keep, send):
        count = lax.axis_size("seq")
        whole = []
        shift = 2
        while 1 << shift < count:
            whole.append(("whole", shift))
            shift += 1
        self.plan = [("core", 0), ("one", 0), ("two", 0), ("half", 1)] + whole + [("back", 1), ("end", 0)]
        self.at = 0
        self.kept = [keep]
        self.sends = [send]
        self.rows, self.columns = keep.shape[1:]

    def done(self):
        return self.at == len(self.plan)

    def start(self):
        if self.done():
            return
        kind, shift = self.plan[self.at]

        def along_seq(a):
            count = lax.axis_size("seq")
            return lax.ppermute(a, "seq", [(i, i ^ (1 << shift)) for i in range(count)])

        if kind == "core":
            ways = [to_core]
        elif kind == "one":
            ways = [to_chip, along_seq]
        elif kind == "two":
            ways = [along_seq, to_chip]
        else:
            ways = [along_seq]
        self.flights = [way(a) for way, a in zip(ways, self.sends)]

    def landing(self):
        kind, _ = self.plan[self.at]
        q, c = self.rows // 4, self.columns
        shapes = {
            "core": [(2 * q, c), (2, q, c)] * 2, "one": [(q, c)] * 4, "two": [(q, c)] * 2,
            "half": [(q, c)], "whole": [(q, c)], "back": [(2 * q, c)], "end": [(4 * q, c)],
        }[kind]

        def body(info_ref, ins, outs):
            bx, by, bz = (info_ref[0] >> 1) & 1, info_ref[1] & 1, (info_ref[1] >> 1) & 1

            def at(i, base=0):
                return pl.ds(pl.multiple_of(base + i * q, 16), q)

            if kind == "core":
                keep, got = ins
                for out, i in ((outs[0], bx), (outs[2], 1 - bx)):
                    out[...] = sum_of(keep[i, : 2 * q, :], got[i, : 2 * q, :])
                for out, i in ((outs[1], by), (outs[3], 1 - by)):
                    out[...] = sum_of(keep[:, at(i, 2 * q), :], got[:, at(i, 2 * q), :])
            elif kind == "one":
                for out, i in ((outs[0], by), (outs[2], 1 - by)):
                    out[...] = sum_of(ins[0][at(i), :], ins[2][at(i), :])
                for out, i in ((outs[1], bx), (outs[3], 1 - bx)):
                    out[...] = sum_of(ins[1][i], ins[3][i])
            elif kind == "two":
                first = sum_of(ins[0][...], ins[2][...])
                second = sum_of(ins[1][...], ins[3][...])
                put_by(bz, outs, first, second, slice(0, c))
            elif kind == "back":
                outs[0][at(bz), :] = ins[0][...]
                outs[0][at(1 - bz), :] = ins[1][...]
            elif kind == "end":
                for half in range(2):
                    outs[0][at(by, 2 * q * half), :] = ins[0][half * q : (half + 1) * q, :]
                    outs[0][at(1 - by, 2 * q * half), :] = ins[1][half * q : (half + 1) * q, :]
            else:
                outs[0][...] = sum_of(ins[0][...], ins[1][...])

        return self.kept + self.flights, shapes, body

    def landed(self, outs):
        kind, _ = self.plan[self.at]
        self.at += 1
        pairs = {"core": 2, "one": 2, "two": 1}.get(kind)
        self.kept = outs[:pairs] if pairs else outs
        self.sends = outs[pairs:] if pairs else outs


def put_by(bit, outs, first, second, cols):
    @pl.when(bit == 0)
    def _():
        outs[0][:, cols] = first
        outs[1][:, cols] = second

    @pl.when(bit != 0)
    def _():
        outs[0][:, cols] = second
        outs[1][:, cols] = first


class Joined(Chain):
    def __init__(self, first, second):
        self.both = (first, second)
        self.plan, self.at, self.rows = second.plan, second.at, second.rows
        self.columns = first.columns + second.columns

    def landing(self):
        if self.both is None:
            return Chain.landing(self)
        plans = [c.landing() for c in self.both]
        q = self.rows // 4

        def body(info_ref, ins, outs):
            bz = (info_ref[1] >> 1) & 1
            start = 0
            for i, c in enumerate(self.widths):
                a = ins[4 * i : 4 * i + 4]
                first = sum_of(a[0][...], a[2][...])
                second = sum_of(a[1][...], a[3][...])
                put_by(bz, outs, first, second, slice(start, start + c))
                start += c

        self.widths = [c.columns for c in self.both]
        return plans[0][0] + plans[1][0], [(q, self.columns)] * 2, body

    def landed(self, outs):
        self.both = None
        Chain.landed(self, outs)


def sum_of(a, b):
    return (a.astype(F32) + b.astype(F32)).astype(BF)


def nothing(*refs):
    pass


def together_at(arrays, seen=()):
    hbm = pl.BlockSpec(memory_space=pl.ANY)
    return pl.pallas_call(
        nothing,
        in_specs=[hbm] * (len(arrays) + len(seen)),
        out_specs=[hbm] * len(arrays),
        out_shape=[jax.ShapeDtypeStruct(a.shape, a.dtype) for a in arrays],
        input_output_aliases={i: i for i in range(len(arrays))},
        compiler_params=pltpu.CompilerParams(vmem_limit_bytes=1024 * 1024),
        name="boundary",
    )(*arrays, *seen)


def boundary(info, token, landing=(), starting=(), also=()):
    landing = [c for c in landing if not c.done()]
    plans = [c.landing() for c in landing]
    args = [info] + [a for p in plans for a in p[0]]
    through = [c.sends[0] for c in starting] + list(also) + [token]
    shapes = [jax.ShapeDtypeStruct(t, BF) for p in plans for t in p[1]]
    count = len(args)

    def body(*refs):
        ins = list(refs[1:count])
        outs = list(refs[count + len(through) :])
        for operands, shapes_i, land in plans:
            land(refs[0], [ins.pop(0) for _ in operands], [outs.pop(0) for _ in shapes_i])

    hbm = pl.BlockSpec(memory_space=pl.ANY)
    outs = pl.pallas_call(
        body,
        grid=(1,),
        in_specs=[smem()] + [full(a.shape) for a in args[1:]] + [hbm] * len(through),
        out_specs=[full(t.shape) for t in shapes] + [hbm] * len(through),
        out_shape=shapes + [jax.ShapeDtypeStruct(a.shape, a.dtype) for a in through],
        input_output_aliases={count + i: len(shapes) + i for i in range(len(through))},
        compiler_params=pltpu.CompilerParams(vmem_limit_bytes=16 * 1024 * 1024),
        cost_estimate=cost(1),
        name="land",
    )(*args, *through)
    outs = list(outs)
    for c, p in zip(landing, plans):
        c.landed([outs.pop(0) for _ in p[1]])
    for c in starting:
        c.sends = [outs.pop(0)]
    waits = [outs[-1]]
    for c in landing + list(starting):
        waits.append(c.sends[0])
        c.start()
    return outs[:-1], tuple(waits)


def neighbours(count):
    up = [(i, i + 1) for i in range(count - 1)]
    return up, [(j, i) for i, j in up]


def shards(
    hidden_in, cotangent, block_seq, block_place, attn_in, attn_out, ffn_in, ffn_out, norm_attn, norm_ffn,
    m_attn_in, m_attn_out, m_ffn_in, m_ffn_out, m_norm_attn, m_norm_ffn,
    v_attn_in, v_attn_out, v_ffn_in, v_ffn_out, v_norm_attn, v_norm_ffn,
):
    x = hidden_in[0]
    cot = cotangent[0]
    n = x.shape[0]
    ext = n + 2 * HALF
    w = lax.axis_index("wshard")
    count = lax.axis_size("seq")
    at = lax.axis_index("seq")
    up, down = neighbours(count)

    far = to_chip(attn_in)
    mate = to_core(attn_in)
    gain_own = jnp.stack([norm_attn, norm_ffn])
    gain_far, gain_mate = to_chip(gain_own), to_core(gain_own)
    x_low, x_high = lax.ppermute(x[n - HALF :], "seq", up), lax.ppermute(x[:HALF], "seq", down)
    attn_out_own, down_a, down_b = copies([attn_out, ffn_out[: D // 4], ffn_out[D // 4 :]])
    info = jnp.concatenate([jnp.stack([w, at]).astype(jnp.int32), block_seq[0], block_place[0]])
    some, rest = D // 4, FF // 4 - D // 4

    def units(start, first, size):
        return [ffn_in[:, start + s * (FF // 4) + first :][:, :size] for s in range(4)]

    in_g = jnp.concatenate(units(0, 0, some), axis=1)
    in_u = jnp.concatenate(units(FF, 0, some), axis=1)
    in_b = jnp.concatenate(units(0, some, rest) + units(FF, some, rest), axis=1)
    out_mate, g_mate, u_mate, da_mate, db_mate, b_mate = (to_core(a) for a in (attn_out_own, in_g, in_u, down_a, down_b, in_b))

    g_half = lax.dynamic_slice_in_dim(in_g, (at & 1) * (D // 8), D // 8, 0)
    (token,) = together_at(
        [jnp.zeros((8, 128), F32)], [x_low, x_high, info, mate, out_mate, g_mate, u_mate, da_mate, db_mate, b_mate]
    )
    far, g_half, in_u, attn_out_own, token = together_at([far, g_half, in_u, attn_out_own, token], [gain_far, gain_mate])
    farmate = to_core(far)
    out_far = to_chip(attn_out_own)
    g_mine = to_chip(g_half)
    u_far = to_chip(in_u)
    attn_parts = attn_in, mate, far, farmate
    gains = gain_own, gain_mate, gain_far, to_core(gain_far)
    nt, q, k, v, cos, sin, gain, token = qkv_call(info, x, x_low, x_high, gains, attn_parts)
    out_far, g_mine, token = together_at([out_far, g_mine, token])
    out_farmate = to_core(out_far)
    out_farmate, down_a, token = together_at([out_farmate, down_a, token])
    da_far = to_chip(down_a)
    g_other = lax.ppermute(g_mine, "seq", [(i, i ^ 1) for i in range(count)])
    out_parts = attn_out, out_mate, out_far, out_farmate
    mixed, middle, n2, out_w, lse, token = attend_call(info, q, k, v, x, out_parts, gain, deps=(token,))
    g_other, u_far, da_far, in_b, down_b, token = together_at([g_other, u_far, da_far, in_b, down_b, token])
    b_far = to_chip(in_b)
    db_far = to_chip(down_b)
    gate_parts = in_g, g_mate, g_mine, g_other, to_core(g_mine), to_core(g_other)
    up_parts = in_u, u_mate, u_far, to_core(u_far)
    down_parts = down_a, da_mate, da_far, to_core(da_far)
    pout, pgn, keep, send, token = ffn_a_call(info, n2, cot, gate_parts, up_parts, down_parts, deps=(token,))
    chain_a = Chain(keep, send)
    (b_far, db_far), deps = boundary(info, token, (), (chain_a,), (b_far, db_far))
    b_parts = in_b, b_mate, b_far, to_core(b_far)
    db_parts = down_b, db_mate, db_far, to_core(db_far)
    _, deps = boundary(info, deps[0], (chain_a,))
    block_out, gmid, gmix, keep, send, token = ffn_b_call(
        info, n2, cot, b_parts, db_parts, pout, pgn, middle, mixed, out_w, gain, deps=deps
    )
    chain_b = Chain(keep, send)
    grads, pieces = (), ()

    def back(p, at, width, deps):
        nonlocal grads, pieces
        if at == 0:
            pieces = ()
        out = attend_back_call(p, at, width, info, q, k, v, gmix, mixed, lse, cos, sin, nt, grads, pieces, deps)
        grads, pieces = out[:3], out[3:5]
        return out[5]

    _, deps = boundary(info, token, (chain_a,), (chain_b,))
    token = back(0, 0, 2 * QUAD, deps)
    _, deps = boundary(info, token, (chain_a, chain_b))
    token = back(1, 1, 2 * QUAD, deps)
    chain_c = Chain(*pieces)
    _, deps = boundary(info, token, (chain_a, chain_b), (chain_c,))
    token = back(2, 0, QUAD, deps)
    chain_d = Chain(*pieces)
    _, deps = boundary(info, token, (chain_b, chain_c), (chain_d,))
    rims = [jnp.concatenate([a[r] for a in grads[1:]], axis=1) for r in (slice(0, HALF), slice(n + HALF, ext))]
    rims, deps = boundary(info, deps[0], (chain_a, chain_b, chain_c, chain_d), (), rims)
    rims = lax.ppermute(rims[1], "seq", up), lax.ppermute(rims[0], "seq", down)
    rims, deps = boundary(info, deps[0], (chain_a, chain_b, chain_d), (), rims)
    grad_in, token = last_call(info, x, grads, rims, gmid, attn_parts, gain, deps=deps)
    chain_c = Joined(chain_c, chain_d)
    chains = (chain_a, chain_b, chain_c)
    while chain_c.at < len(chain_c.plan) - 1:
        _, deps = boundary(info, token, chains)
        token = deps[0]
    sum_a, sum_b = chain_a.kept[0], chain_b.kept[0]

    r = D // 4
    third = FF // 12

    def block_rows(a, first, step, columns):
        return a, (step, columns), lambda i: (first // step + i, 0)

    def lay_out(i, info_ref, refs, out):
        for b, ref in enumerate(refs):
            out[:, b * WIDE : (b + 1) * WIDE] = ref[...].astype(F32)

    res_attn_out = adam_call(
        info, lay_out, [block_rows(sum_b, (2 + b) * r, r // 2, WIDE) for b in range(2)], attn_out, m_attn_out, v_attn_out, r // 2
    )

    def lay_down(i, info_ref, refs, out):
        for b in range(2):
            out[:, b * WIDE : (b + 1) * WIDE] = jnp.where(i < 2, refs[b][...], refs[2 + b][...]).astype(F32)

    res_ffn_out = adam_call(
        info, lay_down,
        [(sum_a, (third, WIDE), lambda i, b=b: ((4 + b) * (r // third) + jnp.minimum(i, 1), 0)) for b in range(2)]
        + [(sum_b, (third, WIDE), lambda i, b=b: (4 * (r // third) + b, 0)) for b in range(2)],
        ffn_out, m_ffn_out, v_ffn_out, third,
    )

    def lay_units(i, info_ref, refs, out):
        for half in range(2):
            of_a = jnp.concatenate([refs[2 * half][...], refs[2 * half + 1][...]], axis=1).astype(F32)
            of_b = refs[4 + half][...].astype(F32)
            for s in range(4):
                start = half * FF + s * (some + rest)
                out[:, start : start + some] = of_a[:, s * some : (s + 1) * some]
                out[:, start + some : start + some + rest] = of_b[:, s * rest : (s + 1) * rest]

    step = r // 4
    res_ffn_in = adam_call(
        info, lay_units,
        [block_rows(sum_a, b * r, step, WIDE) for b in range(4)] + [block_rows(sum_b, b * r, step, WIDE) for b in range(2)],
        ffn_in, m_ffn_in, v_ffn_in, step, deps=(token,),
    )

    def row_of(part, i):
        at = part * r + i * step
        return at // (2 * r * 3 // 4), (at % (2 * r * 3 // 4)) // (r * 3 // 4), at % (r * 3 // 4)

    def source(part):
        def at(i):
            half, _, row = row_of(part, i)
            return (half * (r * 3 // 4) + row) // step, 0

        return at

    def lay_parts(i, info_ref, refs, out):
        for part in range(3):
            mine = row_of(part, i)[1] == (info_ref[1] & 1)
            out[:, part * D : (part + 1) * D] = jnp.where(mine, refs[part][...], refs[3 + part][...]).astype(F32)

    res_attn_in = adam_call(
        info, lay_parts,
        [(a, (step, D), source(part)) for a in (chain_c.kept[0], chain_c.flights[0]) for part in range(3)],
        attn_in, m_attn_in, v_attn_in, step,
    )
    results = [res_attn_in, res_attn_out, res_ffn_in, res_ffn_out]
    for res, own_gain, m, v_ in ((res_attn_in, norm_attn, m_norm_attn, v_norm_attn), (res_ffn_in, norm_ffn, m_norm_ffn, v_norm_ffn)):
        wide = own_gain.astype(F32)
        g = res[4][:, 0] / wide
        results.append((g,) + adam(wide, g, m, v_, 0.0))
    return (block_out[None], grad_in[None]) + tuple(res[i] for i in range(4) for res in results)


def solution(mesh):
    big = P("wshard", "seq", None)
    mat = P("wshard", None)
    vec = P("wshard")
    group = (mat, mat, mat, mat, vec, vec)
    in_specs = (big, big, mat, mat) + group * 3
    out_specs = (big, big) + group * 4
    return jax.shard_map(shards, mesh=mesh, in_specs=in_specs, out_specs=out_specs, check_vma=False)
```

```python
import functools

import jax
import jax.numpy as jnp
import numpy as np
from jax import lax
from jax.experimental import pallas as pl
from jax.experimental.pallas import tpu as pltpu
from jax.sharding import PartitionSpec as P

D = 768
FF = 1152
HEADS = 12
HD = 64
HALF = 64
STEP = 10
PAIR = 2 * HD
QB = 128
TILE = 256
ATILE = 512
WIDE = 384
ADAM_MB = 60
QUAD = 4 * HD

NORM_EPS = 1e-05
BETA_ONE = 0.9
BETA_TWO = 0.98
LEARN_RATE = 0.05
WEIGHT_DECAY = 0.01
ADAM_EPS = 1e-06
NEG_FILL = -1e30
THETA = 10000.0
BF = jnp.bfloat16
F32 = jnp.float32


def dot(left, right):
    return lax.dot_general(left, right, (((1,), (0,)), ((), ())), preferred_element_type=F32)


def dot_bt(left, right):
    return lax.dot_general(left, right, (((1,), (1,)), ((), ())), preferred_element_type=F32)


def dot_at(left, right):
    return lax.dot_general(left, right, (((0,), (0,)), ((), ())), preferred_element_type=F32)


def call(body, args, in_specs, out_specs, out_shape, megabytes, deps=(), aliases=None, **kw):
    first = len(args)
    n_out = len(out_shape)

    def wrapped(*refs):
        refs = refs[:first] + refs[first + len(deps) :]
        token = refs[first + n_out]
        token[...] = jnp.zeros_like(token)
        body(*refs[: first + n_out], *refs[first + n_out + 1 :])

    return pl.pallas_call(
        wrapped,
        in_specs=list(in_specs) + [pl.BlockSpec(memory_space=pl.ANY)] * len(deps),
        out_specs=list(out_specs) + [full((8, 128))],
        out_shape=list(out_shape) + [jax.ShapeDtypeStruct((8, 128), F32)],
        input_output_aliases=aliases or {},
        compiler_params=pltpu.CompilerParams(
            dimension_semantics=("arbitrary",), vmem_limit_bytes=megabytes * 1024 * 1024
        ),
        **kw,
    )(*args, *deps)


def full(shape):
    return pl.BlockSpec(shape, lambda i: (0,) * len(shape))


def rows(tile, width):
    return pl.BlockSpec((tile, width), lambda i: (i, 0))


def cost(microseconds):
    return pl.CostEstimate(flops=int(microseconds * 1.1e9), bytes_accessed=0, transcendentals=0)


def normalize(x):
    mean = jnp.mean(x, axis=-1, keepdims=True)
    centered = x - mean
    var = jnp.mean(centered * centered, axis=-1, keepdims=True)
    r = lax.rsqrt(var + NORM_EPS)
    return centered * r, r


def signed(sin):
    first = lax.broadcasted_iota(jnp.int32, sin.shape, 1) % HD < HD // 2
    zero = jnp.zeros_like(sin)
    return jnp.where(first, -sin, zero), jnp.where(first, zero, sin)


def turn(u, cos, sin_left, sin_right):
    return u * cos + pltpu.roll(u, PAIR - HD // 2, 1) * sin_left + pltpu.roll(u, HD // 2, 1) * sin_right


def blocks_of(info_ref):
    return (info_ref.shape[0] - 2) // 2


def sides(info_ref):
    count = blocks_of(info_ref)
    at = info_ref[1]
    own = info_ref[2 + at]
    left = (at > 0) & (info_ref[2 + jnp.maximum(at - 1, 0)] == own)
    right = (at < count - 1) & (info_ref[2 + jnp.minimum(at + 1, count - 1)] == own)
    return left, right


def bias_of(b, last, left, right):
    shape = (QB + 2 * HALF, QB)
    key = lax.broadcasted_iota(jnp.int32, shape, 0)
    off = key - lax.broadcasted_iota(jnp.int32, shape, 1)
    low = jnp.where((b > 0) | left, 0, HALF)
    high = jnp.where((b < last) | right, QB + 2 * HALF, QB + HALF)
    ok = (off >= 0) & (off <= 2 * HALF) & (key >= low) & (key < high)
    return jnp.where(ok, 0.0, NEG_FILL)


def lay(w, parts, out_ref, bit=0):
    r = out_ref.shape[0] // 4
    for i, ref in enumerate(parts):
        start = (w ^ i) * r
        if isinstance(ref, tuple):
            half = r // 2
            for j, a in enumerate(ref):
                out_ref[pl.ds(pl.multiple_of(start + (bit ^ j) * half, 16), half), :] = a[...]
        else:
            out_ref[pl.ds(pl.multiple_of(start, 32), r), :] = ref[...]


def deal(w, acc, cols, keep_ref, send_ref, at):
    r = acc.shape[0] // 4
    c = w & 1
    for x in range(2):
        keep_ref[x, at : at + r, :] = acc[pl.ds(pl.multiple_of((2 * x + c) * r, 32), r), cols].astype(BF)
        send_ref[x, at : at + r, :] = acc[pl.ds(pl.multiple_of((2 * x + 1 - c) * r, 32), r), cols].astype(BF)


def smem():
    return pl.BlockSpec(memory_space=pltpu.SMEM)


def piece(n_rows):
    return jax.ShapeDtypeStruct((2, n_rows, WIDE), BF)


def qkv_body(info_ref, x_ref, low_ref, high_ref, gain_a, gain_b, gain_c, gain_d, wa, wb, wc, wd, far_ref, near_ref,
             nt_ref, q_ref, k_ref, v_ref, cos_ref, sin_ref, gain_ref, w_ref, x_ext):
    t = q_ref.shape[0]
    i = pl.program_id(0)

    @pl.when(i == 0)
    def _():
        lay(info_ref[0], (wa, wb, wc, wd), w_ref)
        end = x_ext.shape[0] - HALF
        x_ext[:HALF, :] = low_ref[...]
        x_ext[HALF:end, :] = x_ref[...]
        x_ext[end:, :] = high_ref[...]
        r = D // 4
        for p, ref in enumerate((gain_a, gain_b, gain_c, gain_d)):
            gains = ref[...].astype(F32)
            for owner in range(4):

                @pl.when((info_ref[0] ^ p) == owner)
                def _():
                    gain_ref[:2, owner * r : (owner + 1) * r] = gains


    place = info_ref[2 + blocks_of(info_ref) + info_ref[1]]
    c2, s2 = far_ref[0, pl.ds(place, 1), :], far_ref[1, pl.ds(place, 1), :]
    c1, s1 = near_ref[0], near_ref[1]
    cos = c1 * c2 - s1 * s2
    sin = s1 * c2 + c1 * s2
    cos_ref[...] = cos
    sin_ref[...] = sin
    sl, sr = signed(sin)
    n, _ = normalize(x_ext[pl.ds(pl.multiple_of(i * t, 128), t), :].astype(F32))
    normed = (n * gain_ref[0:1, :]).astype(BF)
    nt_ref[...] = normed.T
    for part, ref, scale in ((0, q_ref, HD**-0.5), (1, k_ref, 1.0)):
        u = dot(normed, w_ref[:, part * D : (part + 1) * D])
        for p in range(D // PAIR):
            r = turn(u[:, p * PAIR : (p + 1) * PAIR], cos, sl, sr)
            ref[:, p * PAIR : (p + 1) * PAIR] = (r * scale).astype(BF)
    v_ref[...] = dot(normed, w_ref[:, 2 * D :]).astype(BF)


def angle_tables(n, ext):
    freq = THETA ** (-2.0 * (np.arange(PAIR) % (HD // 2)) / HD)

    def table(positions):
        angle = positions[:, None] * freq[None, :]
        return jnp.asarray(np.stack([np.cos(angle), np.sin(angle)]).astype(np.float32))

    return table(np.arange(4.0) * n), table(np.arange(float(ext)) - HALF)


def qkv_call(info, x, low, high, gains, w_parts, deps=()):
    n = x.shape[0]
    ext = n + 2 * HALF
    t = ext // 3
    out = jax.ShapeDtypeStruct((ext, D), BF)
    table = jax.ShapeDtypeStruct((ext, PAIR), F32)
    far, near = angle_tables(n, ext)
    return call(
        qkv_body,
        [info, x, low, high, *gains, *w_parts, far, near],
        grid=(3,),
        in_specs=[smem(), full((n, D)), full((HALF, D)), full((HALF, D))] + [full((2, D // 4))] * 4 + [full((D // 4, 3 * D))] * 4
        + [full(far.shape), pl.BlockSpec((2, t, PAIR), lambda i: (0, i, 0))],
        out_specs=[pl.BlockSpec((D, t), lambda i: (0, i))] + [rows(t, D)] * 3 + [rows(t, PAIR)] * 2 + [full((8, D))],
        out_shape=[jax.ShapeDtypeStruct((D, ext), BF)] + [out] * 3 + [table] * 2 + [jax.ShapeDtypeStruct((8, D), F32)],
        scratch_shapes=[pltpu.VMEM((D, 3 * D), BF), pltpu.VMEM((ext, D), BF)],
        megabytes=20,
        deps=deps,
        cost_estimate=cost(9),
        name="qkv",
    )


def apart(u):
    head = lax.broadcasted_iota(jnp.int32, u.shape, 1) // HD
    zero = jnp.zeros_like(u)
    return jnp.concatenate([jnp.where(head == h, u, zero) for h in range(4)], axis=0)


def together(u):
    r = u.shape[0] // 4
    head = lax.broadcasted_iota(jnp.int32, (r, QUAD), 1) // HD
    out = u[:r]
    for h in range(1, 4):
        out = jnp.where(head == h, u[h * r : (h + 1) * r], out)
    return out


def repeat(u):
    return jnp.concatenate([u] * 4, axis=1)


def attend_body(info_ref, q_ref, k_ref, v_ref, x_ref, wa, wb, wc, wd, gain_ref,
                mixed_ref, middle_ref, n2_ref, w_ref, lse_ref):
    i = pl.program_id(0)
    last = pl.num_programs(0) * (ATILE // QB) - 1
    left, right = sides(info_ref)

    @pl.when(i == 0)
    def _():
        lay(info_ref[0], (wa, wb, wc, wd), w_ref)

    for s in range(ATILE // QB):
        b = i * (ATILE // QB) + s
        start = pl.multiple_of(b * QB, QB)
        bias = repeat(bias_of(b, last, left, right))
        for g in range(D // QUAD):
            cols = slice(g * QUAD, (g + 1) * QUAD)
            win = pl.ds(start, QB + 2 * HALF)
            q4 = apart(q_ref[pl.ds(start + HALF, QB), cols])
            scores = dot_bt(k_ref[win, cols], q4) + bias
            most = jnp.max(scores, axis=0, keepdims=True)
            e = jnp.exp(scores - most)
            total = jnp.sum(e, axis=0, keepdims=True)
            probs = (e * (1.0 / total)).astype(BF)
            o = together(dot_at(probs, v_ref[win, cols]))
            mixed_ref[s * QB : (s + 1) * QB, cols] = o.astype(BF)
            lse = most + jnp.log(total)
            for h in range(4):
                lse_ref[g, h : h + 1, s * QB : (s + 1) * QB] = lse[:, h * QB : (h + 1) * QB]
    middle = x_ref[...].astype(F32) + dot(mixed_ref[...], w_ref[...])
    middle_ref[...] = middle.astype(BF)
    n, _ = normalize(middle)
    n2_ref[...] = (n * gain_ref[1:2, :]).astype(BF)


def attend_call(info, q, k, v, x, w_parts, gain, deps=()):
    n = x.shape[0]
    ext = q.shape[0]
    groups = D // QUAD
    return call(
        attend_body,
        [info, q, k, v, x, *w_parts, gain],
        grid=(n // ATILE,),
        in_specs=[smem()] + [full((ext, D))] * 3 + [rows(ATILE, D)] + [full((D // 4, D))] * 4 + [full((8, D))],
        out_specs=[rows(ATILE, D)] * 3 + [full((D, D)), pl.BlockSpec((groups, 4, ATILE), lambda i: (0, 0, i))],
        out_shape=[
            jax.ShapeDtypeStruct((n, D), BF), jax.ShapeDtypeStruct((n, D), BF), jax.ShapeDtypeStruct((n, D), BF),
            jax.ShapeDtypeStruct((D, D), BF), jax.ShapeDtypeStruct((groups, 4, n), F32),
        ],
        megabytes=16,
        deps=deps,
        cost_estimate=cost(11),
        name="attend",
    )


def hidden(n2, cot, both, wd):
    gate_up = jnp.concatenate([dot(n2, w[...]) for w in both], axis=1)
    half = gate_up.shape[1] // 2
    gate, up = gate_up[:, :half], gate_up[:, half:]
    ga = dot_bt(cot, wd)
    phi = 0.5 + 0.5 * lax.erf(gate * (2.0**-0.5))
    gelu = gate * phi
    act = (gelu * up).astype(BF)
    slope = phi + gate * (jnp.exp(-0.5 * gate * gate) * 0.3989422804014327)
    grads = jnp.concatenate([(ga * up * slope).astype(BF), (ga * gelu).astype(BF)], axis=1)
    out = dot(act, wd)
    size = grads.shape[1] // len(both)
    gn = sum(dot_bt(grads[:, i * size : (i + 1) * size], w[...]) for i, w in enumerate(both))
    return act, grads, out, gn


def ffn_a_body(info_ref, n2_ref, cot_ref, ga, gb, gc, gd, ge, gf, ua, ub, uc, ud, oa, ob, oc, od,
               out_ref, gn_ref, keep_ref, send_ref, wg_ref, wu_ref, wd_ref, acc, ad):
    i = pl.program_id(0)

    @pl.when(i == 0)
    def _():
        lay(info_ref[0], (ga, gb, (gc, gd), (ge, gf)), wg_ref, info_ref[1] & 1)
        lay(info_ref[0], (ua, ub, uc, ud), wu_ref)
        lay(info_ref[0], (oa, ob, oc, od), wd_ref)
        acc[...] = jnp.zeros_like(acc)
        ad[...] = jnp.zeros_like(ad)

    n2 = n2_ref[...]
    cot = cot_ref[...]
    nt = n2.T
    act, grads, total_out, total_gn = hidden(n2, cot, (wg_ref, wu_ref), wd_ref[...])
    acc[...] += dot(nt, grads)
    ad[...] += dot_at(act, cot)
    out_ref[...] = total_out.astype(BF)
    gn_ref[...] = total_gn.astype(BF)

    @pl.when(i == pl.num_programs(0) - 1)
    def _():
        for b in range(4):
            deal(info_ref[0], acc, slice(b * WIDE, (b + 1) * WIDE), keep_ref, send_ref, b * D // 4)
        for b in range(2):
            deal(info_ref[0], ad, slice(b * WIDE, (b + 1) * WIDE), keep_ref, send_ref, (4 + b) * D // 4)


def ffn_a_call(info, n2, cot, gate_parts, up_parts, down_parts, deps=()):
    n = n2.shape[0]
    part = jax.ShapeDtypeStruct((n, D), BF)
    size = 6 * D // 4
    return call(
        ffn_a_body,
        [info, n2, cot, *gate_parts, *up_parts, *down_parts],
        grid=(n // TILE,),
        in_specs=[smem()] + [rows(TILE, D)] * 2 + [full((D // 4, D))] * 2 + [full((D // 8, D))] * 4
        + [full((D // 4, D))] * 8,
        out_specs=[rows(TILE, D)] * 2 + [full((2, size, WIDE))] * 2,
        out_shape=[part, part, piece(size), piece(size)],
        scratch_shapes=[pltpu.VMEM((D, D), BF)] * 3 + [pltpu.VMEM((D, 2 * D), F32), pltpu.VMEM((D, D), F32)],
        megabytes=24,
        deps=deps,
        cost_estimate=cost(18),
        name="ffn_a",
    )


def norm_back(grad, n, r, gain):
    e = grad * gain
    return r * (e - jnp.mean(e, axis=-1, keepdims=True) - n * jnp.mean(e * n, axis=-1, keepdims=True))


def ffn_b_body(info_ref, n2_ref, cot_ref, ia, ib, ic, id_, oa, ob, oc, od, pout_ref, pgn_ref, mid_ref, mixed_ref, wo_ref, gain_ref,
               out_ref, gmid_ref, gmix_ref, keep_ref, send_ref, w_ref, wd_ref, acc, ad, ao):
    i = pl.program_id(0)

    @pl.when(i == 0)
    def _():
        lay(info_ref[0], (ia, ib, ic, id_), w_ref)
        lay(info_ref[0], (oa, ob, oc, od), wd_ref)
        acc[...] = jnp.zeros_like(acc)
        ao[...] = jnp.zeros_like(ao)
        ad[...] = jnp.zeros_like(ad)

    n2 = n2_ref[...]
    cot = cot_ref[...]
    act, grads, out, gn = hidden(n2, cot, (w_ref,), wd_ref[...])
    acc[...] += dot(n2.T, grads)
    ad[...] += dot_at(act, cot)
    middle = mid_ref[...].astype(F32)
    out_ref[...] = (middle + pout_ref[...].astype(F32) + out).astype(BF)
    n, r = normalize(middle)
    branch = (cot.astype(F32) + norm_back(pgn_ref[...].astype(F32) + gn, n, r, gain_ref[1:2, :])).astype(BF)
    gmid_ref[...] = branch
    gmix_ref[...] = dot_bt(branch, wo_ref[...]).astype(BF)
    ao[...] += dot_at(mixed_ref[...], branch)

    @pl.when(i == pl.num_programs(0) - 1)
    def _():
        w = info_ref[0]
        r = D // 4
        for b in range(2):
            cols = slice(b * WIDE, (b + 1) * WIDE)
            deal(w, acc, cols, keep_ref, send_ref, b * r)
            deal(w, ao, cols, keep_ref, send_ref, (2 + b) * r)
            deal(w, ad, cols, keep_ref, send_ref, 4 * r + b * r // 2)


def ffn_b_call(info, n2, cot, in_parts, down_parts, pout, pgn, middle, mixed, wo, gain, deps=()):
    n = n2.shape[0]
    size = 5 * D // 4
    return call(
        ffn_b_body,
        [info, n2, cot, *in_parts, *down_parts, pout, pgn, middle, mixed, wo, gain],
        grid=(n // TILE,),
        in_specs=[smem()] + [rows(TILE, D)] * 2 + [full((D // 4, D))] * 4 + [full((WIDE // 4, D))] * 4
        + [rows(TILE, D)] * 4 + [full((D, D)), full((8, D))],
        out_specs=[rows(TILE, D)] * 3 + [full((2, size, WIDE))] * 2,
        out_shape=[jax.ShapeDtypeStruct((n, D), BF)] * 3 + [piece(size), piece(size)],
        scratch_shapes=[pltpu.VMEM((D, D), BF), pltpu.VMEM((WIDE, D), BF),
                        pltpu.VMEM((D, D), F32), pltpu.VMEM((WIDE, D), F32), pltpu.VMEM((D, D), F32)],
        megabytes=24,
        deps=deps,
        cost_estimate=cost(14),
        name="ffn_b",
    )


def attend_back_body(info_ref, q_ref, k_ref, v_ref, g_ref, mixed_ref, lse_ref, cos_ref, sin_ref, nt_ref, *rest):
    dq_ref, dk_ref, dv_ref, keep_ref, send_ref, ak, av, aw = rest[-8:]
    ext = ak.shape[0]
    blocks = (ext - 2 * HALF) // QB
    left, right = sides(info_ref)
    ak[...] = jnp.zeros_like(ak)
    av[...] = jnp.zeros_like(av)
    zero = jnp.zeros((HALF, QUAD), BF)
    dq_ref[:HALF, :] = zero
    dq_ref[ext - HALF :, :] = zero
    prod = mixed_ref[...].astype(F32) * g_ref[...].astype(F32)
    head = lax.broadcasted_iota(jnp.int32, (8, QUAD), 1) // HD
    pick = jnp.where(head == lax.broadcasted_iota(jnp.int32, (8, QUAD), 0), 1.0, 0.0).astype(BF)
    high = prod.astype(BF)
    delta = dot_bt(pick, high) + dot_bt(pick, (prod - high.astype(F32)).astype(BF))

    def of_heads(a, start):
        return jnp.concatenate([a[h : h + 1, start : start + QB] for h in range(4)], axis=1)

    def unturn(u, at):
        cos = cos_ref[at, :]
        sl, sr = signed(-sin_ref[at, :])
        return jnp.concatenate([turn(u[:, c : c + PAIR], cos, sl, sr) for c in (0, PAIR)], axis=1).astype(BF)

    for b in range(blocks):
        start = b * QB
        win = slice(start, start + QB + 2 * HALF)
        here = slice(start + HALF, start + HALF + QB)
        bias = repeat(bias_of(b, blocks - 1, left, right))
        q4 = apart(q_ref[here, :])
        g4 = apart(g_ref[start : start + QB, :])
        kw = k_ref[win, :]
        probs = jnp.exp(dot_bt(kw, q4) + bias - of_heads(lse_ref[0], start))
        ds = (probs * (dot_bt(v_ref[win, :], g4) - of_heads(delta, start))).astype(BF)
        ak[win, :] += dot(ds, q4)
        av[win, :] += dot(probs.astype(BF), g4)
        dq_ref[here, :] = unturn(together(dot_at(ds, kw)) * HD**-0.5, here)
    dk_ref[...] = unturn(ak[...], slice(0, ext))
    dv_ref[...] = av[...].astype(BF)
    for part, ref in enumerate((dq_ref, dk_ref, dv_ref)):
        aw[...] = dot(nt_ref[...], ref[...])
        deal(info_ref[0], aw, slice(0, QUAD), keep_ref, send_ref, part * D // 4)


def attend_back_call(p, at, width, info, q, k, v, g, mixed, lse, cos, sin, nt, sofar, pieces, deps=()):
    n = g.shape[0]
    ext = q.shape[0]
    cols = pl.BlockSpec((ext, QUAD), lambda i: (0, p))
    inner = pl.BlockSpec((n, QUAD), lambda i: (0, p))
    own = jax.ShapeDtypeStruct((ext, D), BF)
    out = jax.ShapeDtypeStruct((2, 3 * D // 4, width), BF)
    args = [info, q, k, v, g, mixed, lse, cos, sin, nt]
    extra = list(sofar) + list(pieces)
    aliases = {}
    for i in range(len(sofar)):
        aliases[len(args) + i] = i
    for i in range(len(pieces)):
        aliases[len(args) + len(sofar) + i] = 3 + i
    mine = pl.BlockSpec((2, 3 * D // 4, QUAD), lambda i: (0, 0, at))
    return call(
        attend_back_body,
        args + extra,
        grid=(1,),
        in_specs=[smem(), cols, cols, cols, inner, inner, pl.BlockSpec((1, 4, n), lambda i: (p, 0, 0))]
        + [full((ext, PAIR))] * 2 + [full((D, ext))] + [pl.BlockSpec(memory_space=pl.ANY)] * len(extra),
        out_specs=[cols] * 3 + [mine] * 2,
        out_shape=[own, own, own, out, out],
        scratch_shapes=[pltpu.VMEM((ext, QUAD), F32), pltpu.VMEM((ext, QUAD), F32), pltpu.VMEM((D, QUAD), F32)],
        aliases=aliases,
        megabytes=12,
        deps=deps,
        cost_estimate=cost(4),
        name="attend_back",
    )


def last_body(info_ref, x_ref, dq_ref, dk_ref, dv_ref, rim_low, rim_high, gmid_ref, wa, wb, wc, wd, gain_ref, gin_ref, w_ref, *both):
    i = pl.program_id(0)
    start = pl.multiple_of(i * TILE, TILE)
    here = pl.ds(start + HALF, TILE)
    ext = dk_ref.shape[0]

    @pl.when(i == 0)
    def _():
        lay(info_ref[0], (wa, wb, wc, wd), w_ref)
        for j, ref in enumerate((dk_ref, dv_ref)):
            cols = slice(j * D, (j + 1) * D)
            both[j][...] = ref[...]
            both[j][HALF : 2 * HALF, :] += rim_low[:, cols]
            both[j][ext - 2 * HALF : ext - HALF, :] += rim_high[:, cols]

    total = jnp.zeros((TILE, D), F32)
    for j, ref in enumerate((dq_ref, *both)):
        total += dot_bt(ref[here, :], w_ref[:, j * D : (j + 1) * D])
    n, r = normalize(x_ref[...].astype(F32))
    gin_ref[...] = (gmid_ref[...].astype(F32) + norm_back(total, n, r, gain_ref[0:1, :])).astype(BF)


def last_call(info, x, grads, rims, gmid, w_parts, gain, deps=()):
    n = gmid.shape[0]
    ext = grads[0].shape[0]
    return call(
        last_body,
        [info, x, *grads, *rims, gmid, *w_parts, gain],
        grid=(n // TILE,),
        in_specs=[smem(), rows(TILE, D)] + [full((ext, D))] * 3 + [full((HALF, 2 * D))] * 2 + [rows(TILE, D)]
        + [full((D // 4, 3 * D))] * 4 + [full((8, D))],
        out_specs=[rows(TILE, D)],
        out_shape=[jax.ShapeDtypeStruct((n, D), BF)],
        scratch_shapes=[pltpu.VMEM((D, 3 * D), BF)] + [pltpu.VMEM((ext, D), BF)] * 2,
        megabytes=16,
        deps=deps,
        cost_estimate=cost(7),
        name="last",
    )


def adam(weight, grad, first_old, second, decay_rate):
    new_first = BETA_ONE * first_old + (1.0 - BETA_ONE) * grad
    new_second = BETA_TWO * second + (1.0 - BETA_TWO) * grad * grad
    root = jnp.sqrt(new_second * (1.0 / (1.0 - BETA_TWO**STEP))) + ADAM_EPS
    change = (-LEARN_RATE / (1.0 - BETA_ONE**STEP)) * (new_first / root)
    if decay_rate:
        change = change - (LEARN_RATE * decay_rate) * weight
    return (new_first, new_second, change)


def adam_call(info, assemble, grads, weight, first, second, rows_at_once, deps=()):
    r, width = weight.shape
    own = rows(rows_at_once, width)
    out = jax.ShapeDtypeStruct((r, width), F32)
    count = len(grads)

    def body(info_ref, *refs):
        blocks = refs[:count]
        w_ref, m_ref, v_ref = refs[count : count + 3]
        g_ref, nm_ref, nv_ref, st_ref, dots_ref = refs[-5:]
        assemble(pl.program_id(0), info_ref, blocks, g_ref)
        g = g_ref[...]
        w = w_ref[...].astype(F32)
        nm_ref[...], nv_ref[...], st_ref[...] = adam(w, g, m_ref[...], v_ref[...], WEIGHT_DECAY)
        dots_ref[...] = jnp.sum(w * g, axis=1, keepdims=True)

    return pl.pallas_call(
        body,
        grid=(r // rows_at_once,),
        in_specs=[smem()] + [pl.BlockSpec(shape, at) for _, shape, at in grads] + [own] * 3
        + [pl.BlockSpec(memory_space=pl.ANY)] * len(deps),
        out_specs=[own] * 4 + [rows(rows_at_once, 1)],
        out_shape=[out] * 4 + [jax.ShapeDtypeStruct((r, 1), F32)],
        compiler_params=pltpu.CompilerParams(dimension_semantics=("arbitrary",), vmem_limit_bytes=ADAM_MB * 1024 * 1024),
        cost_estimate=cost(3),
        name="adam",
    )(info, *[g for g, _, _ in grads], weight, first, second, *deps)


CORES = [(0, 1), (1, 0), (2, 3), (3, 2)]
CHIPS = [(0, 2), (2, 0), (1, 3), (3, 1)]


def to_core(a):
    return lax.ppermute(a, "wshard", CORES)


def to_chip(a):
    return lax.ppermute(a, "wshard", CHIPS)


def copy_body(*refs):
    for a, b in zip(refs[: len(refs) // 2], refs[len(refs) // 2 :]):
        b[...] = a[...]


def copies(arrays):
    return pl.pallas_call(
        copy_body,
        grid=(1,),
        in_specs=[full(a.shape) for a in arrays],
        out_specs=[full(a.shape) for a in arrays],
        out_shape=[jax.ShapeDtypeStruct(a.shape, a.dtype) for a in arrays],
        compiler_params=pltpu.CompilerParams(vmem_limit_bytes=8 * 1024 * 1024),
        name="copies",
    )(*arrays)


def after(a, first):
    return together_at([a, first])[0]


class Chain:
    def __init__(self, keep, send):
        count = lax.axis_size("seq")
        whole = []
        shift = 2
        while 1 << shift < count:
            whole.append(("whole", shift))
            shift += 1
        self.plan = [("core", 0), ("one", 0), ("two", 0), ("half", 1)] + whole + [("back", 1), ("end", 0)]
        self.at = 0
        self.kept = [keep]
        self.sends = [send]
        self.rows, self.columns = keep.shape[1:]

    def done(self):
        return self.at == len(self.plan)

    def start(self):
        if self.done():
            return
        kind, shift = self.plan[self.at]

        def along_seq(a):
            count = lax.axis_size("seq")
            return lax.ppermute(a, "seq", [(i, i ^ (1 << shift)) for i in range(count)])

        if kind == "core":
            ways = [to_core]
        elif kind == "one":
            ways = [to_chip, along_seq]
        elif kind == "two":
            ways = [along_seq, to_chip]
        else:
            ways = [along_seq]
        self.flights = [way(a) for way, a in zip(ways, self.sends)]

    def landing(self):
        kind, _ = self.plan[self.at]
        q, c = self.rows // 4, self.columns
        shapes = {
            "core": [(2 * q, c), (2, q, c)] * 2, "one": [(q, c)] * 4, "two": [(q, c)] * 2,
            "half": [(q, c)], "whole": [(q, c)], "back": [(2 * q, c)], "end": [(4 * q, c)],
        }[kind]

        def body(info_ref, ins, outs):
            bx, by, bz = (info_ref[0] >> 1) & 1, info_ref[1] & 1, (info_ref[1] >> 1) & 1

            def at(i, base=0):
                return pl.ds(pl.multiple_of(base + i * q, 16), q)

            if kind == "core":
                keep, got = ins
                for out, i in ((outs[0], bx), (outs[2], 1 - bx)):
                    out[...] = sum_of(keep[i, : 2 * q, :], got[i, : 2 * q, :])
                for out, i in ((outs[1], by), (outs[3], 1 - by)):
                    out[...] = sum_of(keep[:, at(i, 2 * q), :], got[:, at(i, 2 * q), :])
            elif kind == "one":
                for out, i in ((outs[0], by), (outs[2], 1 - by)):
                    out[...] = sum_of(ins[0][at(i), :], ins[2][at(i), :])
                for out, i in ((outs[1], bx), (outs[3], 1 - bx)):
                    out[...] = sum_of(ins[1][i], ins[3][i])
            elif kind == "two":
                first = sum_of(ins[0][...], ins[2][...])
                second = sum_of(ins[1][...], ins[3][...])
                put_by(bz, outs, first, second, slice(0, c))
            elif kind == "back":
                outs[0][at(bz), :] = ins[0][...]
                outs[0][at(1 - bz), :] = ins[1][...]
            elif kind == "end":
                for half in range(2):
                    outs[0][at(by, 2 * q * half), :] = ins[0][half * q : (half + 1) * q, :]
                    outs[0][at(1 - by, 2 * q * half), :] = ins[1][half * q : (half + 1) * q, :]
            else:
                outs[0][...] = sum_of(ins[0][...], ins[1][...])

        return self.kept + self.flights, shapes, body

    def landed(self, outs):
        kind, _ = self.plan[self.at]
        self.at += 1
        pairs = {"core": 2, "one": 2, "two": 1}.get(kind)
        self.kept = outs[:pairs] if pairs else outs
        self.sends = outs[pairs:] if pairs else outs


def put_by(bit, outs, first, second, cols):
    @pl.when(bit == 0)
    def _():
        outs[0][:, cols] = first
        outs[1][:, cols] = second

    @pl.when(bit != 0)
    def _():
        outs[0][:, cols] = second
        outs[1][:, cols] = first


class Joined(Chain):
    def __init__(self, first, second):
        self.both = (first, second)
        self.plan, self.at, self.rows = second.plan, second.at, second.rows
        self.columns = first.columns + second.columns

    def landing(self):
        if self.both is None:
            return Chain.landing(self)
        plans = [c.landing() for c in self.both]
        q = self.rows // 4

        def body(info_ref, ins, outs):
            bz = (info_ref[1] >> 1) & 1
            start = 0
            for i, c in enumerate(self.widths):
                a = ins[4 * i : 4 * i + 4]
                first = sum_of(a[0][...], a[2][...])
                second = sum_of(a[1][...], a[3][...])
                put_by(bz, outs, first, second, slice(start, start + c))
                start += c

        self.widths = [c.columns for c in self.both]
        return plans[0][0] + plans[1][0], [(q, self.columns)] * 2, body

    def landed(self, outs):
        self.both = None
        Chain.landed(self, outs)


def sum_of(a, b):
    return (a.astype(F32) + b.astype(F32)).astype(BF)


def nothing(*refs):
    pass


def together_at(arrays, seen=()):
    hbm = pl.BlockSpec(memory_space=pl.ANY)
    return pl.pallas_call(
        nothing,
        in_specs=[hbm] * (len(arrays) + len(seen)),
        out_specs=[hbm] * len(arrays),
        out_shape=[jax.ShapeDtypeStruct(a.shape, a.dtype) for a in arrays],
        input_output_aliases={i: i for i in range(len(arrays))},
        compiler_params=pltpu.CompilerParams(vmem_limit_bytes=1024 * 1024),
        name="boundary",
    )(*arrays, *seen)


def boundary(info, token, landing=(), starting=(), also=()):
    landing = [c for c in landing if not c.done()]
    plans = [c.landing() for c in landing]
    args = [info] + [a for p in plans for a in p[0]]
    through = [c.sends[0] for c in starting] + list(also) + [token]
    shapes = [jax.ShapeDtypeStruct(t, BF) for p in plans for t in p[1]]
    count = len(args)

    def body(*refs):
        ins = list(refs[1:count])
        outs = list(refs[count + len(through) :])
        for operands, shapes_i, land in plans:
            land(refs[0], [ins.pop(0) for _ in operands], [outs.pop(0) for _ in shapes_i])

    hbm = pl.BlockSpec(memory_space=pl.ANY)
    outs = pl.pallas_call(
        body,
        grid=(1,),
        in_specs=[smem()] + [full(a.shape) for a in args[1:]] + [hbm] * len(through),
        out_specs=[full(t.shape) for t in shapes] + [hbm] * len(through),
        out_shape=shapes + [jax.ShapeDtypeStruct(a.shape, a.dtype) for a in through],
        input_output_aliases={count + i: len(shapes) + i for i in range(len(through))},
        compiler_params=pltpu.CompilerParams(vmem_limit_bytes=16 * 1024 * 1024),
        cost_estimate=cost(1),
        name="land",
    )(*args, *through)
    outs = list(outs)
    for c, p in zip(landing, plans):
        c.landed([outs.pop(0) for _ in p[1]])
    for c in starting:
        c.sends = [outs.pop(0)]
    waits = [outs[-1]]
    for c in landing + list(starting):
        waits.append(c.sends[0])
        c.start()
    return outs[:-1], tuple(waits)


def neighbours(count):
    up = [(i, i + 1) for i in range(count - 1)]
    return up, [(j, i) for i, j in up]


def shards(
    hidden_in, cotangent, block_seq, block_place, attn_in, attn_out, ffn_in, ffn_out, norm_attn, norm_ffn,
    m_attn_in, m_attn_out, m_ffn_in, m_ffn_out, m_norm_attn, m_norm_ffn,
    v_attn_in, v_attn_out, v_ffn_in, v_ffn_out, v_norm_attn, v_norm_ffn,
):
    x = hidden_in[0]
    cot = cotangent[0]
    n = x.shape[0]
    ext = n + 2 * HALF
    w = lax.axis_index("wshard")
    count = lax.axis_size("seq")
    at = lax.axis_index("seq")
    up, down = neighbours(count)

    far = to_chip(attn_in)
    mate = to_core(attn_in)
    gain_own = jnp.stack([norm_attn, norm_ffn])
    gain_far, gain_mate = to_chip(gain_own), to_core(gain_own)
    x_low, x_high = lax.ppermute(x[n - HALF :], "seq", up), lax.ppermute(x[:HALF], "seq", down)
    attn_out_own, down_a, down_b = copies([attn_out, ffn_out[: D // 4], ffn_out[D // 4 :]])
    info = jnp.concatenate([jnp.stack([w, at]).astype(jnp.int32), block_seq[0], block_place[0]])
    some, rest = D // 4, FF // 4 - D // 4

    def units(start, first, size):
        return [ffn_in[:, start + s * (FF // 4) + first :][:, :size] for s in range(4)]

    in_g = jnp.concatenate(units(0, 0, some), axis=1)
    in_u = jnp.concatenate(units(FF, 0, some), axis=1)
    in_b = jnp.concatenate(units(0, some, rest) + units(FF, some, rest), axis=1)
    out_mate, g_mate, u_mate, da_mate, db_mate, b_mate = (to_core(a) for a in (attn_out_own, in_g, in_u, down_a, down_b, in_b))

    g_half = lax.dynamic_slice_in_dim(in_g, (at & 1) * (D // 8), D // 8, 0)
    (token,) = together_at(
        [jnp.zeros((8, 128), F32)], [x_low, x_high, info, mate, out_mate, g_mate, u_mate, da_mate, db_mate, b_mate]
    )
    far, g_half, in_u, attn_out_own, token = together_at([far, g_half, in_u, attn_out_own, token], [gain_far, gain_mate])
    farmate = to_core(far)
    out_far = to_chip(attn_out_own)
    g_mine = to_chip(g_half)
    u_far = to_chip(in_u)
    attn_parts = attn_in, mate, far, farmate
    gains = gain_own, gain_mate, gain_far, to_core(gain_far)
    nt, q, k, v, cos, sin, gain, token = qkv_call(info, x, x_low, x_high, gains, attn_parts)
    out_far, g_mine, down_a, token = together_at([out_far, g_mine, down_a, token])
    da_far = to_chip(down_a)
    out_farmate = to_core(out_far)
    out_farmate, token = together_at([out_farmate, token])
    g_other = lax.ppermute(g_mine, "seq", [(i, i ^ 1) for i in range(count)])
    out_parts = attn_out, out_mate, out_far, out_farmate
    mixed, middle, n2, out_w, lse, token = attend_call(info, q, k, v, x, out_parts, gain, deps=(token,))
    g_other, u_far, da_far, in_b, down_b, token = together_at([g_other, u_far, da_far, in_b, down_b, token])
    b_far = to_chip(in_b)
    db_far = to_chip(down_b)
    gate_parts = in_g, g_mate, g_mine, g_other, to_core(g_mine), to_core(g_other)
    up_parts = in_u, u_mate, u_far, to_core(u_far)
    down_parts = down_a, da_mate, da_far, to_core(da_far)
    pout, pgn, keep, send, token = ffn_a_call(info, n2, cot, gate_parts, up_parts, down_parts, deps=(token,))
    chain_a = Chain(keep, send)
    (b_far, db_far), deps = boundary(info, token, (), (chain_a,), (b_far, db_far))
    b_parts = in_b, b_mate, b_far, to_core(b_far)
    db_parts = down_b, db_mate, db_far, to_core(db_far)
    _, deps = boundary(info, deps[0], (chain_a,))
    block_out, gmid, gmix, keep, send, token = ffn_b_call(
        info, n2, cot, b_parts, db_parts, pout, pgn, middle, mixed, out_w, gain, deps=deps
    )
    chain_b = Chain(keep, send)
    grads, pieces = (), ()

    def back(p, at, width, deps):
        nonlocal grads, pieces
        if at == 0:
            pieces = ()
        out = attend_back_call(p, at, width, info, q, k, v, gmix, mixed, lse, cos, sin, nt, grads, pieces, deps)
        grads, pieces = out[:3], out[3:5]
        return out[5]

    _, deps = boundary(info, token, (chain_a,), (chain_b,))
    token = back(0, 0, 2 * QUAD, deps)
    _, deps = boundary(info, token, (chain_a, chain_b))
    token = back(1, 1, 2 * QUAD, deps)
    chain_c = Chain(*pieces)
    _, deps = boundary(info, token, (chain_a, chain_b), (chain_c,))
    token = back(2, 0, QUAD, deps)
    chain_d = Chain(*pieces)
    _, deps = boundary(info, token, (chain_b, chain_c), (chain_d,))
    rims = [jnp.concatenate([a[r] for a in grads[1:]], axis=1) for r in (slice(0, HALF), slice(n + HALF, ext))]
    rims, deps = boundary(info, deps[0], (chain_a, chain_b, chain_c, chain_d), (), rims)
    rims = lax.ppermute(rims[1], "seq", up), lax.ppermute(rims[0], "seq", down)
    rims, deps = boundary(info, deps[0], (chain_a, chain_b, chain_d), (), rims)
    grad_in, token = last_call(info, x, grads, rims, gmid, attn_parts, gain, deps=deps)
    chain_c = Joined(chain_c, chain_d)
    chains = (chain_a, chain_b, chain_c)
    while chain_c.at < len(chain_c.plan) - 1:
        _, deps = boundary(info, token, chains)
        token = deps[0]
    sum_a, sum_b = chain_a.kept[0], chain_b.kept[0]

    r = D // 4
    third = FF // 12

    def block_rows(a, first, step, columns):
        return a, (step, columns), lambda i: (first // step + i, 0)

    def lay_out(i, info_ref, refs, out):
        for b, ref in enumerate(refs):
            out[:, b * WIDE : (b + 1) * WIDE] = ref[...].astype(F32)

    res_attn_out = adam_call(
        info, lay_out, [block_rows(sum_b, (2 + b) * r, r // 2, WIDE) for b in range(2)], attn_out, m_attn_out, v_attn_out, r // 2
    )

    def lay_down(i, info_ref, refs, out):
        for b in range(2):
            out[:, b * WIDE : (b + 1) * WIDE] = jnp.where(i < 2, refs[b][...], refs[2 + b][...]).astype(F32)

    res_ffn_out = adam_call(
        info, lay_down,
        [(sum_a, (third, WIDE), lambda i, b=b: ((4 + b) * (r // third) + jnp.minimum(i, 1), 0)) for b in range(2)]
        + [(sum_b, (third, WIDE), lambda i, b=b: (4 * (r // third) + b, 0)) for b in range(2)],
        ffn_out, m_ffn_out, v_ffn_out, third,
    )

    def lay_units(i, info_ref, refs, out):
        for half in range(2):
            of_a = jnp.concatenate([refs[2 * half][...], refs[2 * half + 1][...]], axis=1).astype(F32)
            of_b = refs[4 + half][...].astype(F32)
            for s in range(4):
                start = half * FF + s * (some + rest)
                out[:, start : start + some] = of_a[:, s * some : (s + 1) * some]
                out[:, start + some : start + some + rest] = of_b[:, s * rest : (s + 1) * rest]

    step = r // 4
    res_ffn_in = adam_call(
        info, lay_units,
        [block_rows(sum_a, b * r, step, WIDE) for b in range(4)] + [block_rows(sum_b, b * r, step, WIDE) for b in range(2)],
        ffn_in, m_ffn_in, v_ffn_in, step, deps=(token,),
    )

    def row_of(part, i):
        at = part * r + i * step
        return at // (2 * r * 3 // 4), (at % (2 * r * 3 // 4)) // (r * 3 // 4), at % (r * 3 // 4)

    def source(part):
        def at(i):
            half, _, row = row_of(part, i)
            return (half * (r * 3 // 4) + row) // step, 0

        return at

    def lay_parts(i, info_ref, refs, out):
        for part in range(3):
            mine = row_of(part, i)[1] == (info_ref[1] & 1)
            out[:, part * D : (part + 1) * D] = jnp.where(mine, refs[part][...], refs[3 + part][...]).astype(F32)

    res_attn_in = adam_call(
        info, lay_parts,
        [(a, (step, D), source(part)) for a in (chain_c.kept[0], chain_c.flights[0]) for part in range(3)],
        attn_in, m_attn_in, v_attn_in, step,
    )
    results = [res_attn_in, res_attn_out, res_ffn_in, res_ffn_out]
    for res, own_gain, m, v_ in ((res_attn_in, norm_attn, m_norm_attn, v_norm_attn), (res_ffn_in, norm_ffn, m_norm_ffn, v_norm_ffn)):
        wide = own_gain.astype(F32)
        g = res[4][:, 0] / wide
        results.append((g,) + adam(wide, g, m, v_, 0.0))
    return (block_out[None], grad_in[None]) + tuple(res[i] for i in range(4) for res in results)


def solution(mesh):
    big = P("wshard", "seq", None)
    mat = P("wshard", None)
    vec = P("wshard")
    group = (mat, mat, mat, mat, vec, vec)
    in_specs = (big, big, mat, mat) + group * 3
    out_specs = (big, big) + group * 4
    return jax.shard_map(shards, mesh=mesh, in_specs=in_specs, out_specs=out_specs, check_vma=False)
```
